128 devices in a mesh: ta: 16 (over x, y_lo, core), sa: 8 (over z, y_hi).
Axes of the slice: x: 4, y: 4 (y_hi: 2, y_lo: 2; y = y_hi * 2 + y_lo), z: 4, core: 2. Of those that a mesh axis runs over, the one named last changes fastest.
Arguments:
- null_vectors: bfloat16 [2, 24, 4, 3, 64, 32, 128], P(None, None, None, None, 'ta', 'sa'), may hold values from -0.15234375 to 0.15234375
- gauge_links: bfloat16 [2, 4, 3, 3, 64, 32, 128], P(None, None, None, None, 'ta', 'sa'), may hold values from -3.59375 to 3.59375
- coarse_in: float32 [16, 8, 8, 96], P('ta', 'sa'), may hold values from -6 to 6
Outputs:
- coarse_links: float32 [16, 8, 8, 5, 4608], P('ta', 'sa')
- coarse_out: float32 [16, 8, 8, 96], P('ta', 'sa')
The draws below stay inside these ranges and needn't reach their ends.
All inputs are finite; a program needn't handle non-finite values.
Results may differ from the reference program's by a relative error of at most 0.0018.
Values may be sent and summed in bfloat16 or wider, within the bound.
No kernel may reach another device: no remote copies, remote signals or barrier semaphores. Data moves between devices by JAX's collectives and lax.ppermute only.
A program may use at most 256 MiB of HBM per device.

```python
import jax
import jax.numpy as jnp
from jax import lax

LAT_Y = 4
LAT_X = 32
NVEC = 24
LAT_T = 64
LAT_Z = 32
PLANE = 128
AGG_T = 16
AGG_Z = 8
AGG_Y = 1
AGG_X = 8
APLANE = 8
NCOL = 48
BLOCK = 4608


def levels(key, extent, pieces, smallest, top_value):
    gain = 1.0
    for position, shards_of in pieces:
        heights = jax.random.uniform(jax.random.fold_in(jax.random.fold_in(key, 6), position), (shards_of,), jnp.float32, smallest / len(pieces), top_value / len(pieces))
        gain = gain * jnp.repeat(jnp.exp(heights), extent[position] // shards_of).reshape((-1,) + (1,) * (len(extent) - 1 - position))
    return gain


def bell_draw(own_key, shape, scale, bound, cuts=(), kind=jnp.bfloat16):
    array = jax.random.normal(own_key, shape, jnp.float32) * scale
    if len(cuts) > 0:
        array = levels(own_key, shape, cuts, -0.22, 0.18) * array
    return jnp.clip(array, min=-bound, max=bound).astype(kind)


def setup_inputs(seed: int = 0) -> dict:
    splits = jax.random.split(jax.random.key(seed), 4)
    return {
        "null_vectors": bell_draw(splits[0], (2, NVEC, 4, 3, LAT_T, LAT_Z, PLANE), 0.0255, 0.15234375, ((4, 16), (5, 8))),
        "gauge_links": bell_draw(splits[1], (2, 4, 3, 3, LAT_T, LAT_Z, PLANE), 0.6, 3.59375, ((4, 16), (5, 8))),
        "coarse_in": bell_draw(splits[2], (AGG_T, AGG_Z, APLANE, 2 * NCOL), 1.0, 6.0, ((0, 16), (1, 8)), jnp.float32),
    }


gamma_rows = (
    ((2, 1.0, 0.0), (3, 1.0, 0.0), (0, 1.0, 0.0), (1, 1.0, 0.0)),
    ((2, 0.0, -1.0), (3, 0.0, 1.0), (0, 0.0, 1.0), (1, 0.0, -1.0)),
    ((3, -1.0, 0.0), (2, 1.0, 0.0), (1, 1.0, 0.0), (0, -1.0, 0.0)),
    ((3, 0.0, -1.0), (2, 0.0, -1.0), (1, 0.0, 1.0), (0, 0.0, 1.0)),
)
diag_shift = 1.0


def color_product(link_field, vectors):
    real_part = 0.0
    imag_part = 0.0
    for colour in range(3):
        link_r = link_field[0, :, colour][None, None].astype(jnp.float32)
        link_i = link_field[1, :, colour][None, None].astype(jnp.float32)
        vector_r = vectors[0, :, :, colour][:, :, None].astype(jnp.float32)
        vector_i = vectors[1, :, :, colour][:, :, None].astype(jnp.float32)
        real_part = real_part + link_r * vector_r - link_i * vector_i
        imag_part = imag_part + link_r * vector_i + link_i * vector_r
    return real_part, imag_part


def hop_terms(real_part, imag_part, direction):
    same_hop = jnp.stack([-0.5 * real_part, -0.5 * imag_part]).astype(jnp.bfloat16)
    rows_real = []
    rows_imag = []
    for spin in range(4):
        source, phase_r, phase_i = gamma_rows[direction][spin]
        rows_real.append(phase_r * real_part[:, source] - phase_i * imag_part[:, source])
        rows_imag.append(phase_r * imag_part[:, source] + phase_i * real_part[:, source])
    cross_hop = (0.5 * jnp.stack([jnp.stack(rows_real, 1), jnp.stack(rows_imag, 1)])).astype(jnp.bfloat16)
    return same_hop, cross_hop


def blocked(field):
    field_shape = field.shape
    return field.reshape(field_shape[:4] + (field_shape[4] // 4, 4, field_shape[5] // 4, 4, LAT_Y // 4, 4, LAT_X // 4, 4))


def pair_product(left_side, right_side):
    return jnp.einsum('rvscTaZbYdXe,qwscTaZbYdXe->TZYXrvqw', left_side.astype(jnp.float32),
                      right_side.astype(jnp.float32), precision=lax.Precision.HIGHEST)


def contract(vectors, same_hop, cross_hop):
    vector_count = vectors.shape[1]
    hops = jnp.concatenate([same_hop, cross_hop], axis=1)
    row_blocks = []
    for chirality in range(2):
        spin_range = slice(2 * chirality, 2 * chirality + 2)
        product = pair_product(vectors[:, :, spin_range], hops[:, :, spin_range])
        real_part = product[..., 0, :, 0, :] + product[..., 1, :, 1, :]
        imag_part = product[..., 0, :, 1, :] - product[..., 1, :, 0, :]
        components = []
        for component in (real_part, imag_part):
            same_cols = component[..., :vector_count]
            cross_cols = component[..., vector_count:]
            if chirality == 0:
                components.append(jnp.concatenate([same_cols, cross_cols], axis=-1))
            else:
                components.append(jnp.concatenate([cross_cols, same_cols], axis=-1))
        row_blocks.append(jnp.stack(components, axis=-3))
    return jnp.concatenate(row_blocks, axis=-2)


def gram(vectors):
    row_blocks = []
    for chirality in range(2):
        spin_range = slice(2 * chirality, 2 * chirality + 2)
        product = pair_product(vectors[:, :, spin_range], vectors[:, :, spin_range])
        real_part = product[..., 0, :, 0, :] + product[..., 1, :, 1, :]
        imag_part = product[..., 0, :, 1, :] - product[..., 1, :, 0, :]
        components = []
        for component in (real_part, imag_part):
            zero_block = jnp.zeros_like(component)
            if chirality == 0:
                components.append(jnp.concatenate([component, zero_block], axis=-1))
            else:
                components.append(jnp.concatenate([zero_block, component], axis=-1))
        row_blocks.append(jnp.stack(components, axis=-3))
    return jnp.concatenate(row_blocks, axis=-2)


def adjoint(blocks):
    vector_count = blocks.shape[-1] // 2
    chirality_sign = jnp.concatenate([jnp.ones(vector_count, jnp.float32), -jnp.ones(vector_count, jnp.float32)])
    outer_sign = chirality_sign[:, None] * chirality_sign[None, :]
    real_part = outer_sign * jnp.swapaxes(blocks[..., 0, :, :], -1, -2)
    imag_part = -outer_sign * jnp.swapaxes(blocks[..., 1, :, :], -1, -2)
    return jnp.stack([real_part, imag_part], axis=-3)


def neighbour(field, direction):
    if direction == 1:
        return jnp.roll(field, -1, axis=5)
    plane_field = field.reshape(field.shape[:6] + (LAT_Y, LAT_X))
    plane_field = jnp.roll(plane_field, -1, axis=6 if direction == 2 else 7)
    return plane_field.reshape(field.shape)


def slab_links(vectors, next_slice, gauge_slab):
    blocked_vectors = blocked(vectors)
    diagonal = diag_shift * gram(blocked_vectors)
    forward_links = []
    for direction in range(4):
        if direction == 0:
            shifted = jnp.concatenate([vectors[:, :, :, :, 1:], next_slice], axis=4)
        else:
            shifted = neighbour(vectors, direction)
        real_part, imag_part = color_product(gauge_slab[:, direction], shifted)
        same_hop, cross_hop = hop_terms(real_part, imag_part, direction)
        same_view = blocked(same_hop)
        cross_view = blocked(cross_hop)
        local_axis = 5 + 2 * direction
        inner_part = contract(lax.slice_in_dim(blocked_vectors, 0, 3, axis=local_axis),
                              lax.slice_in_dim(same_view, 0, 3, axis=local_axis),
                              lax.slice_in_dim(cross_view, 0, 3, axis=local_axis))
        outer_part = contract(lax.slice_in_dim(blocked_vectors, 3, 4, axis=local_axis),
                              lax.slice_in_dim(same_view, 3, 4, axis=local_axis),
                              lax.slice_in_dim(cross_view, 3, 4, axis=local_axis))
        diagonal = diagonal + inner_part + adjoint(inner_part)
        forward_links.append(outer_part)
    return jnp.stack([diagonal] + forward_links, axis=-4)


def matvec(blocks, coarse_vector):
    def times_vector(matrix, column):
        return jnp.einsum('...ij,...j->...i', matrix, column, precision=lax.Precision.HIGHEST)
    real_part = times_vector(blocks[..., 0, :, :], coarse_vector[..., 0, :]) - times_vector(blocks[..., 1, :, :], coarse_vector[..., 1, :])
    imag_part = times_vector(blocks[..., 0, :, :], coarse_vector[..., 1, :]) + times_vector(blocks[..., 1, :, :], coarse_vector[..., 0, :])
    return jnp.stack([real_part, imag_part], axis=-2)


def coarse_apply(coarse_blocks, coarse_vector):
    result = matvec(coarse_blocks[..., 0, :, :, :], coarse_vector)
    for direction in range(4):
        link_block = coarse_blocks[..., 1 + direction, :, :, :]
        result = result + matvec(link_block, jnp.roll(coarse_vector, -1, axis=direction))
        result = result + jnp.roll(matvec(adjoint(link_block), coarse_vector), 1, axis=direction)
    return result


def reference(null_vectors, gauge_links, coarse_in):
    def one_slab(slab_index):
        first_slice = (slab_index * 4).astype(jnp.int32)
        vectors = lax.dynamic_slice_in_dim(null_vectors, first_slice, 4, axis=4)
        following = ((first_slice + 4) % LAT_T).astype(jnp.int32)
        next_slice = lax.dynamic_slice_in_dim(null_vectors, following, 1, axis=4)
        gauge_slab = lax.dynamic_slice_in_dim(gauge_links, first_slice, 4, axis=4)
        return slab_links(vectors, next_slice, gauge_slab)[0]

    coarse_blocks = lax.map(one_slab, jnp.arange(AGG_T, dtype=jnp.int32))
    coarse_vector = coarse_in.reshape(AGG_T, AGG_Z, AGG_Y, AGG_X, 2, NCOL)
    once_applied = coarse_apply(coarse_blocks, coarse_vector)
    twice_applied = coarse_apply(coarse_blocks, once_applied)
    return (coarse_blocks.reshape(AGG_T, AGG_Z, APLANE, 5, BLOCK),
            twice_applied.reshape(AGG_T, AGG_Z, APLANE, 2 * NCOL))
```

```python
import jax
import jax.numpy as jnp
from jax import lax
from jax.experimental import pallas as pl
from jax.experimental.pallas import tpu as pltpu
from jax.sharding import PartitionSpec as P

NV = 24
ROWS = 48
F32 = jnp.float32
BF16 = jnp.bfloat16


def lane_ids(rows):
    return lax.broadcasted_iota(jnp.int32, (rows, 128), 1)


def roll(value, shift):
    return pltpu.roll(value, shift % 128, 1)


def exchange(planes):
    rows = planes[0].shape[0]
    lanes = lane_ids(rows)
    for bit in range(3):
        step = 4 << bit
        chosen = (lanes & step) != 0
        out = [None] * 8
        for low in range(8):
            if low >> bit & 1:
                continue
            high = low | 1 << bit
            out[low] = jnp.where(chosen, roll(planes[high], step), planes[low])
            out[high] = jnp.where(chosen, planes[high], roll(planes[low], -step))
        planes = out
    return planes


def colour(link, vector):
    out = []
    for c in range(3):
        real = imag = None
        for d in range(3):
            lr, li = link[(c * 3 + d) * 2], link[(c * 3 + d) * 2 + 1]
            vr, vi = vector[d * 2], vector[d * 2 + 1]
            re, im = lr * vr - li * vi, lr * vi + li * vr
            real = re if real is None else real + re
            imag = im if imag is None else imag + im
        out.append((real, imag))
    return out


def nt(a, b):
    return lax.dot_general(a, b, (((1,), (1,)), ((), ())), preferred_element_type=F32)


def variants(plain):
    second = (lane_ids(plain.shape[0]) & 16) != 0
    swapped = jnp.where(second, roll(plain, 16), roll(plain, -16))
    return (
        plain,
        jnp.where(second, -plain, plain),
        swapped,
        jnp.where(second, swapped, -swapped),
    )


def inner_kernel(
    v_ref, u_ref, out_ref, lt_ref, lz_ref, ut_ref, uz_ref, vf, vm, uf, cm, flat
):
    flat[...] = jnp.zeros_like(flat)

    @pl.loop(0, 4)
    def _(mu):
        for c in range(3):
            for d in range(3):
                for ri in range(2):
                    row = ((c * 3 + d) * 2 + ri) * 16
                    flat[0, pl.ds(row, 16), :] = 0.5 * u_ref[ri, mu, c, d].astype(F32)

        lanes = lane_ids(24)
        drop = ((lanes & 12) == 12) & (mu == 1)
        for t in range(4):
            z_planes = [flat[0, pl.ds(t * 4 + z, 24, stride=16), :] for z in range(4)]
            for a, value in enumerate(exchange(z_planes + z_planes)):
                uf[a, mu, t] = jnp.where(drop, 0.0, value)

        @pl.when(mu == 1)
        def _():
            t_planes = [flat[0, pl.ds(t * 4 + 3, 24, stride=16), :] for t in range(4)]
            for a, value in enumerate(exchange(t_planes + t_planes)):
                uz_ref[a] = value

    for a in range(8):
        ut_ref[a] = uf[a, 0, 3]

    @pl.loop(0, 6)
    def _(step):
        chi, c = step // 3, step % 3
        for sb in range(2):
            for ri in range(2):
                block = v_ref[ri, :, 2 * chi + sb, c].astype(F32)
                flat[sb, pl.ds(ri * 384, 384), :] = block.reshape(384, 128)
        for t in range(4):
            planes = [
                flat[sb, pl.ds(t * 4 + z, ROWS, stride=16), :] for sb in range(2) for z in range(4)
            ]
            column = pl.multiple_of((t * 3 + c) * 128, 128)
            for a, value in enumerate(exchange(planes)):
                vf[a, chi, t, c] = value
                for kind, operand in enumerate(variants(value)):
                    vm[kind, a, chi, :, pl.ds(column, 128)] = operand.astype(BF16)
        planes = [
            flat[sb, pl.ds(t * 4 + 3, ROWS, stride=16), :] for sb in range(2) for t in range(4)
        ]
        column = pl.multiple_of(c * 128, 128)
        for a, value in enumerate(exchange(planes)):
            both = variants(value)
            lz_ref[0, a, chi, :, pl.ds(column, 128)] = both[0].astype(BF16)
            lz_ref[1, a, chi, :, pl.ds(column, 128)] = both[1].astype(BF16)

    for a in range(8):
        for chi in range(2):
            lt_ref[a, chi] = vm[0, a, chi, :, 9 * 128 :]

    cm[...] = jnp.zeros_like(cm)

    @pl.loop(0, 8)
    def _(a):
        ahead = (a + 1) % 8
        lanes = lane_ids(24)
        x_last = (lanes & 3) == 3
        y_last = lanes >= 96
        blocks = []
        for chi in range(2):
            for t in range(4):
                for mu in range(4):
                    if mu == 0 and t == 3:
                        continue
                    link = [uf[a, mu, t, pl.ds(k, 1), :] for k in range(18)]
                    vector = []
                    for d in range(3):
                        for ri in range(2):
                            rows = pl.ds(ri * 24, 24)
                            if mu == 0:
                                value = vf[a, chi, t + 1, d, rows, :]
                            else:
                                value = vf[a, chi, t, d, rows, :]
                            if mu == 1:
                                value = roll(value, -4)
                            elif mu == 2:
                                value = roll(value, -32)
                            elif mu == 3:
                                other = vf[ahead, chi, t, d, rows, :]
                                value = jnp.where(x_last, roll(other, 3), roll(value, -1))
                            vector.append(value)
                    for c, parts in enumerate(colour(link, vector)):
                        column = slice((t * 3 + c) * 128, (t * 3 + c + 1) * 128)
                        for ri in range(2):
                            if mu < 2:
                                row = ri * 64 + mu * 32
                                cm[0, row : row + 24, column] = parts[ri].astype(BF16)
                            else:
                                last = y_last if mu == 2 else x_last
                                full = parts[ri]
                                outer = jnp.where(last, -full, 0.0)
                                row = ri * 64
                                cm[mu - 1, row : row + 24, column] = full.astype(BF16)
                                cm[mu - 1, row + 32 : row + 56, column] = outer.astype(BF16)
            near, far = vm[0, a, chi], vm[0, a, 1 - chi]
            tz = nt(jnp.concatenate([near, far, vm[1, a, 1 - chi]], 0), cm[0])
            y = nt(jnp.concatenate([near, vm[3, a, 1 - chi]], 0), cm[1])
            x = nt(jnp.concatenate([near, vm[2, a, 1 - chi]], 0), cm[2])
            gram = nt(near, near)
            blocks.append((tz, y, x, gram))
        combine_inner(blocks, a, out_ref)


def complex_of(product, sign):
    return product[:24] + sign * roll(product[24:], 64)


def times_i(value, sign):
    return -sign * roll(value, 64)


def combine_inner(blocks, a, out_ref):
    sign = sides()
    second = (lane_ids(NV) & 32) != 0
    upper = {}
    for chi, (tz, y, x, gram) in enumerate(blocks):
        phase = 1.0 if chi == 0 else -1.0
        z_tz = complex_of(tz[:48], sign)
        z_y = complex_of(y[:48], sign)
        z_x = complex_of(x[:48], sign)
        cross_t = complex_of(tz[48:96], sign)
        cross_z = phase * times_i(complex_of(tz[96:144], sign), sign)
        cross_y = phase * complex_of(y[48:96], sign)
        cross_x = phase * times_i(complex_of(x[48:96], sign), sign)
        same = -(z_tz + z_y + z_x)
        cross = jnp.where(second, cross_z, cross_t) + cross_y + cross_x
        same = same + roll(same, -32)
        cross = cross + roll(cross, -32)
        gram = jnp.concatenate([gram, jnp.zeros((ROWS, 128 - ROWS), F32)], 1)
        gram_r = gram[:24] + roll(gram[24:], -24)
        gram_i = roll(gram[:24], -24) - gram[24:]
        y_same, y_cross = roll(z_y, -32), -roll(cross_y, -32)
        x_same, x_cross = roll(z_x, -32), -roll(cross_x, -32)
        upper[chi, chi] = (same, y_same, x_same, gram_r, gram_i)
        upper[1 - chi, chi] = (cross, y_cross, x_cross, None, None)

    def whole(item, ri):
        return placed([[upper[row, col][item] for col in range(2)] for row in range(2)], ri)

    first_rows = lax.broadcasted_iota(jnp.int32, (ROWS, 128), 0) < NV
    cols = lane_ids(ROWS)
    flip = jnp.where(first_rows == (cols < NV), 1.0, -1.0).astype(F32)
    zero = jnp.zeros((NV, 128), F32)
    for ri in range(2):
        out_ref[a, 1, ri] = whole(1, ri)
        out_ref[a, 2, ri] = whole(2, ri)
        inner = whole(0, ri)
        turned = jnp.concatenate([inner, jnp.zeros((80, 128), F32)], 0).T[:ROWS]
        turned = flip * turned if ri == 0 else -flip * turned
        gram = [[upper[0, 0][3 + ri], zero], [zero, upper[1, 1][3 + ri]]]
        out_ref[a, 0, ri] = placed(gram, 0) + inner + turned


def placed(parts, ri):
    lanes = lane_ids(NV)
    left, right = lanes < NV, (lanes >= NV) & (lanes < 2 * NV)
    rows = []
    for row in range(2):
        second = jnp.where(right, roll(parts[row][1], NV - 64 * ri), 0.0)
        rows.append(jnp.where(left, roll(parts[row][0], -64 * ri), second))
    return jnp.concatenate(rows, 0)


def sides():
    return jnp.where(lane_ids(NV) < 64, 1.0, -1.0).astype(F32)


def inner_call(vectors, links):
    shape = jax.ShapeDtypeStruct
    vmem = pl.BlockSpec(memory_space=pltpu.VMEM)
    return pl.pallas_call(
        inner_kernel,
        out_shape=(
            shape((8, 3, 2, ROWS, 128), F32),
            shape((8, 2, ROWS, 384), BF16),
            shape((2, 8, 2, ROWS, 384), BF16),
            shape((8, 24, 128), F32),
            shape((8, 24, 128), F32),
        ),
        in_specs=[vmem] * 2,
        out_specs=(vmem,) * 5,
        scratch_shapes=[
            pltpu.VMEM((8, 2, 4, 3, ROWS, 128), F32),
            pltpu.VMEM((4, 8, 2, ROWS, 1536), BF16),
            pltpu.VMEM((8, 4, 4, 24, 128), F32),
            pltpu.VMEM((3, 128, 1536), BF16),
            pltpu.VMEM((2, 768, 128), F32),
        ],
        compiler_params=pltpu.CompilerParams(vmem_limit_bytes=56 * 1024 * 1024),
        cost_estimate=pl.CostEstimate(
            flops=40_000_000_000, bytes_accessed=6_000_000, transcendentals=0
        ),
        name="inner",
    )(vectors, links)


def face_kernel(v_ref, t_ref, z_ref, flat):
    @pl.loop(0, 6)
    def _(step):
        chi, c = step // 3, step % 3
        for sb in range(2):
            for ri in range(2):
                block = v_ref[ri, :, 2 * chi + sb, c].astype(F32)
                flat[sb, pl.ds(ri * 384, 384), :] = block.reshape(384, 128)
        column = pl.multiple_of(c * 128, 128)
        for out, stride in ((t_ref, 1), (z_ref, 4)):
            planes = [
                flat[sb, pl.ds(q * stride, ROWS, stride=16), :] for sb in range(2) for q in range(4)
            ]
            for a, value in enumerate(exchange(planes)):
                out[a, chi, :, pl.ds(column, 128)] = value.astype(BF16)


def face_call(vectors):
    face = jax.ShapeDtypeStruct((8, 2, ROWS, 384), BF16)
    vmem = pl.BlockSpec(memory_space=pltpu.VMEM)
    return pl.pallas_call(
        face_kernel,
        out_shape=(face, face),
        in_specs=[vmem],
        out_specs=(vmem, vmem),
        scratch_shapes=[pltpu.VMEM((2, 768, 128), F32)],
        compiler_params=pltpu.CompilerParams(vmem_limit_bytes=24 * 1024 * 1024),
        name="faces",
    )(vectors)


def outer_kernel(ft_ref, fz_ref, lt_ref, lz_ref, ut_ref, uz_ref, out_ref, cm):
    cm[...] = jnp.zeros_like(cm)

    @pl.loop(0, 8)
    def _(a):
        sign = sides()
        parts = ([[None, None], [None, None]], [[None, None], [None, None]])
        for chi in range(2):
            phase = 1.0 if chi == 0 else -1.0
            for mu, (face, links) in enumerate(((ft_ref, ut_ref), (fz_ref, uz_ref))):
                link = [links[a, pl.ds(k, 1), :] for k in range(18)]
                vector = []
                for d in range(3):
                    value = face[a, chi, :, d * 128 : (d + 1) * 128].astype(F32)
                    vector += [value[:NV], value[NV:]]
                for c, both in enumerate(colour(link, vector)):
                    column = slice(c * 128, (c + 1) * 128)
                    cm[mu, 0:24, column] = both[0].astype(BF16)
                    cm[mu, 64:88, column] = both[1].astype(BF16)
                if mu == 0:
                    left = jnp.concatenate([lt_ref[a, chi], lt_ref[a, 1 - chi]], 0)
                else:
                    left = jnp.concatenate([lz_ref[0, a, chi], lz_ref[1, a, 1 - chi]], 0)
                product = nt(left, cm[mu])
                cross = complex_of(product[ROWS:], sign)
                if mu == 1:
                    cross = phase * times_i(cross, sign)
                parts[mu][chi][chi] = -complex_of(product[:ROWS], sign)
                parts[mu][1 - chi][chi] = cross
        for mu in range(2):
            for ri in range(2):
                out_ref[a, mu, ri] = placed(parts[mu], ri)


def outer_call(face_t, face_z, left_t, left_z, link_t, link_z):
    vmem = pl.BlockSpec(memory_space=pltpu.VMEM)
    return pl.pallas_call(
        outer_kernel,
        out_shape=jax.ShapeDtypeStruct((8, 2, 2, ROWS, 128), F32),
        in_specs=[vmem] * 6,
        out_specs=vmem,
        scratch_shapes=[pltpu.VMEM((2, 128, 384), BF16)],
        compiler_params=pltpu.CompilerParams(vmem_limit_bytes=24 * 1024 * 1024),
        name="outer",
    )(face_t, face_z, left_t, left_z, link_t, link_z)


def signs():
    rows = lax.broadcasted_iota(jnp.int32, (ROWS, 128), 0)
    return jnp.where(rows < NV, 1.0, -1.0).astype(F32), jnp.where(lane_ids(1) < NV, 1.0, -1.0).astype(F32)


def split(row):
    keep = lane_ids(1) < ROWS
    return jnp.where(keep, row, 0.0), jnp.where(keep, roll(row, -ROWS), 0.0)


def joined(real, imag):
    lanes = lane_ids(1)
    low, high = lanes < ROWS, (lanes >= ROWS) & (lanes < 2 * ROWS)
    return jnp.where(low, real, jnp.where(high, roll(imag, ROWS), 0.0))


def forward(block, row):
    pr, pi = split(row)
    br, bi = block
    return br * pr - bi * pi, br * pi + bi * pr


def column_of(row, eye):
    return jnp.sum(jnp.where(eye, row, 0.0), axis=1, keepdims=True)


def row_of(column, eye):
    return jnp.sum(jnp.where(eye, column, 0.0), axis=0, keepdims=True)


def backward(block, column_r, column_i, col_sign):
    br, bi = block
    real = jnp.sum(br * column_r + bi * column_i, axis=0, keepdims=True)
    imag = jnp.sum(br * column_i - bi * column_r, axis=0, keepdims=True)
    return joined(col_sign * real, col_sign * imag)


def eye_mask():
    rows = lax.broadcasted_iota(jnp.int32, (ROWS, 128), 0)
    return rows == lane_ids(ROWS)


def local_apply(inner, outer, vec, part_ref, bt_ref, bz_ref):
    eye = eye_mask()
    row_sign, col_sign = signs()
    part_ref[...] = jnp.zeros_like(part_ref)

    @pl.loop(0, 8)
    def _(a):
        own = vec[pl.ds(a, 1), :]
        ahead = (a + 1) % 8
        nxt = vec[pl.ds(ahead, 1), :]
        block = lambda ref, slot: (ref[a, slot, 0], ref[a, slot, 1])
        f0 = forward(block(inner, 0), own)
        f1 = forward(block(inner, 1), own)
        f2 = forward(block(inner, 2), nxt)
        real = jnp.sum(f0[0] + f1[0] + f2[0], axis=1, keepdims=True)
        imag = jnp.sum(f0[1] + f1[1] + f2[1], axis=1, keepdims=True)
        pr, pi = split(own)
        column_r = row_sign * column_of(pr, eye)
        column_i = row_sign * column_of(pi, eye)
        back_y = backward(block(inner, 1), column_r, column_i, col_sign)
        back_x = backward(block(inner, 2), column_r, column_i, col_sign)
        bt_ref[pl.ds(a, 1), :] = backward(block(outer, 0), column_r, column_i, col_sign)
        bz_ref[pl.ds(a, 1), :] = backward(block(outer, 1), column_r, column_i, col_sign)
        part_ref[pl.ds(a, 1), :] += joined(row_of(real, eye), row_of(imag, eye)) + back_y
        part_ref[pl.ds(ahead, 1), :] += back_x


def ahead_apply(outer, vt, vz, part_ref):
    eye = eye_mask()

    @pl.loop(0, 8)
    def _(a):
        ft = forward((outer[a, 0, 0], outer[a, 0, 1]), vt[pl.ds(a, 1), :])
        fz = forward((outer[a, 1, 0], outer[a, 1, 1]), vz[pl.ds(a, 1), :])
        real = jnp.sum(ft[0] + fz[0], axis=1, keepdims=True)
        imag = jnp.sum(ft[1] + fz[1], axis=1, keepdims=True)
        part_ref[pl.ds(a, 1), :] += joined(row_of(real, eye), row_of(imag, eye))


def first_kernel(inner, outer, vec, vt, vz, part_ref, bt_ref, bz_ref):
    local_apply(inner, outer, vec, part_ref, bt_ref, bz_ref)
    ahead_apply(outer, vt, vz, part_ref)


def second_kernel(inner, outer, part, rt, rz, vec_ref, part_ref, bt_ref, bz_ref):
    vec_ref[...] = part[...] + rt[...] + rz[...]
    local_apply(inner, outer, vec_ref, part_ref, bt_ref, bz_ref)


def last_kernel(outer, part, rt, rz, vt, vz, out_ref):
    out_ref[...] = part[...] + rt[...] + rz[...]
    ahead_apply(outer, vt, vz, out_ref)


def small_call(kernel, count, name, *args):
    vmem = pl.BlockSpec(memory_space=pltpu.VMEM)
    row = jax.ShapeDtypeStruct((8, 128), F32)
    return pl.pallas_call(
        kernel,
        out_shape=(row,) * count,
        in_specs=[vmem] * len(args),
        out_specs=(vmem,) * count,
        compiler_params=pltpu.CompilerParams(vmem_limit_bytes=24 * 1024 * 1024),
        name=name,
    )(*args)


def shifted(value, axis, steps):
    count = lax.axis_size(axis)
    return lax.ppermute(value, axis, [(k, (k + steps) % count) for k in range(count)])


def per_device(null_vectors, gauge_links, coarse_in):
    vectors = null_vectors.reshape(2, NV, 4, 3, 16, 128)
    links = gauge_links.reshape(2, 4, 3, 3, 16, 128)
    vec = jnp.pad(coarse_in.reshape(8, 2 * ROWS), ((0, 0), (0, 32)))
    face_t, face_z = face_call(vectors)
    face_z = shifted(face_z, "sa", -1)
    face_t = shifted(face_t, "ta", -1)
    vec_t, vec_z = shifted(vec, "ta", -1), shifted(vec, "sa", -1)
    inner, left_t, left_z, link_t, link_z = inner_call(vectors, links)
    outer = outer_call(face_t, face_z, left_t, left_z, link_t, link_z)
    part, bt, bz = small_call(first_kernel, 3, "first", inner, outer, vec, vec_t, vec_z)
    rt, rz = shifted(bt, "ta", 1), shifted(bz, "sa", 1)
    once, part, bt, bz = small_call(second_kernel, 4, "second", inner, outer, part, rt, rz)
    rt, rz = shifted(bt, "ta", 1), shifted(bz, "sa", 1)
    vec_t, vec_z = shifted(once, "ta", -1), shifted(once, "sa", -1)
    (twice,) = small_call(last_kernel, 1, "last", outer, part, rt, rz, vec_t, vec_z)
    blocks = jnp.concatenate([inner[:, :1], outer, inner[:, 1:]], 1)[..., :ROWS]
    return blocks.reshape(1, 1, 8, 5, 2 * ROWS * ROWS), twice[:, : 2 * ROWS].reshape(1, 1, 8, 2 * ROWS)


def solution(mesh):
    placed_sites = P(None, None, None, None, "ta", "sa", None)
    return jax.shard_map(
        per_device,
        mesh=mesh,
        in_specs=(placed_sites, placed_sites, P("ta", "sa", None, None)),
        out_specs=(P("ta", "sa", None, None, None), P("ta", "sa", None, None)),
        check_vma=False,
    )
```

```python
import jax
import jax.numpy as jnp
from jax import lax
from jax.experimental import pallas as pl
from jax.experimental.pallas import tpu as pltpu
from jax.sharding import PartitionSpec as P

NV = 24
ROWS = 48
F32 = jnp.float32
BF16 = jnp.bfloat16


def lane_ids(rows):
    return lax.broadcasted_iota(jnp.int32, (rows, 128), 1)


def roll(value, shift):
    return pltpu.roll(value, shift % 128, 1)


def exchange_bit(low, high, bit):
    step = 4 << bit
    chosen = (lane_ids(low.shape[0]) & step) != 0
    return jnp.where(chosen, roll(high, step), low), jnp.where(chosen, high, roll(low, -step))


def exchange(sets):
    for bit in range(3):
        for planes in sets:
            for low in range(8):
                if not low >> bit & 1:
                    high = low | 1 << bit
                    planes[low], planes[high] = exchange_bit(planes[low], planes[high], bit)
    return sets


def colour(link, vector):
    out = []
    for c in range(3):
        real = imag = None
        for d in range(3):
            lr, li = link[(c * 3 + d) * 2], link[(c * 3 + d) * 2 + 1]
            vr, vi = vector[d * 2], vector[d * 2 + 1]
            re, im = lr * vr - li * vi, lr * vi + li * vr
            real = re if real is None else real + re
            imag = im if imag is None else imag + im
        out.append((real, imag))
    return out


def nt(a, b):
    return lax.dot_general(a, b, (((1,), (1,)), ((), ())), preferred_element_type=F32)


def inner_kernel(
    v_ref, u_ref, out_ref, lt_ref, lz_ref, ut_ref, uz_ref, vm, uf, cm, flat, kept
):
    flat[...] = jnp.zeros_like(flat)

    @pl.loop(0, 4)
    def _(mu):
        for c in range(3):
            for d in range(3):
                for ri in range(2):
                    row = ((c * 3 + d) * 2 + ri) * 16
                    flat[0, pl.ds(row, 16), :] = 0.5 * u_ref[ri, mu, c, d].astype(F32)

        drop = ((lane_ids(24) & 12) == 12) & (mu == 1)

        def load(t, plane):
            first = plane % 4 * 4 + 3 if t == 4 else t * 4 + plane % 4
            return flat[0, pl.ds(first, 24, stride=16), :]

        for group in ((0, 1), (2, 3), (4,)):
            done = exchange([[load(t, plane) for plane in range(8)] for t in group])
            for t, values in zip(group, done):
                for a, value in enumerate(values):
                    uf[a, mu, t] = value if t == 4 else jnp.where(drop, 0.0, value)

    for a in range(8):
        uz_ref[a] = uf[a, 1, 4]

    for a in range(8):
        ut_ref[a] = uf[a, 0, 3]

    @pl.loop(0, 6)
    def _(step):
        chi, c = step // 3, step % 3
        for sb in range(2):
            for ri in range(2):
                block = v_ref[ri, :, 2 * chi + sb, c].astype(F32)
                flat[sb, pl.ds(ri * 384, 384), :] = block.reshape(384, 128)

        def load(t, plane):
            sb, q = plane // 4, plane % 4
            first = q * 4 + 3 if t == 4 else t * 4 + q
            return flat[sb, pl.ds(first, ROWS, stride=16), :].astype(BF16)

        second = (lane_ids(ROWS) & 16) != 0
        for group in ((0, 1), (2, 3), (4,)):
            done = exchange([[load(t, plane) for plane in range(8)] for t in group])
            turned = [[jnp.where(second, -value, value) for value in values] for values in done]
            if group != (4,):
                swapped = [
                    [jnp.where(second, roll(value, 16), roll(value, -16)) for value in values]
                    for values in done
                ]
            for k, t in enumerate(group):
                for a in range(8):
                    if t == 4:
                        column = pl.multiple_of(c * 128, 128)
                        lz_ref[0, a, chi, :, pl.ds(column, 128)] = done[k][a]
                        lz_ref[1, a, chi, :, pl.ds(column, 128)] = turned[k][a]
                        continue
                    column = pl.multiple_of((t * 3 + c) * 128, 128)
                    vm[0, a, chi, :, pl.ds(column, 128)] = done[k][a]
                    vm[1, a, chi, :, pl.ds(column, 128)] = turned[k][a]
                    value = swapped[k][a]
                    vm[2, a, chi, :, pl.ds(column, 128)] = value
                    vm[3, a, chi, :, pl.ds(column, 128)] = jnp.where(second, value, -value)

    for a in range(8):
        for chi in range(2):
            lt_ref[a, chi] = vm[0, a, chi, :, 9 * 128 :]

    cm[...] = jnp.zeros_like(cm)

    def fill(a, chi):
        ahead = lax.rem(a + 1, 8)
        x_last = (lane_ids(NV) & 3) == 3
        x_last_pair = (lane_ids(ROWS) & 3) == 3
        y_last = lane_ids(NV) >= 96
        for t in range(4):
            for mu in range(4):
                if mu == 0 and t == 3:
                    continue
                link = [uf[a, mu, t, pl.ds(k, 1), :] for k in range(18)]
                vector = []
                for d in range(3):
                    first = (((t + 1) if mu == 0 else t) * 3 + d) * 128
                    value = vm[0, a, chi, :, first : first + 128]
                    if mu == 1:
                        value = roll(value, -4)
                    elif mu == 2:
                        value = roll(value, -32)
                    elif mu == 3:
                        other = vm[0, ahead, chi, :, first : first + 128]
                        value = jnp.where(x_last_pair, roll(other, 3), roll(value, -1))
                    value = value.astype(F32)
                    vector += [value[:NV], value[NV:]]
                for c, parts in enumerate(colour(link, vector)):
                    column = slice((t * 3 + c) * 128, (t * 3 + c + 1) * 128)
                    for ri in range(2):
                        if mu < 2:
                            row = ri * 64 + mu * 32
                            cm[chi, 0, row : row + 24, column] = parts[ri].astype(BF16)
                        else:
                            last = y_last if mu == 2 else x_last
                            outer = jnp.where(last, -parts[ri], 0.0)
                            row = ri * 64
                            cm[chi, mu - 1, row : row + 24, column] = parts[ri].astype(BF16)
                            cm[chi, mu - 1, row + 32 : row + 56, column] = outer.astype(BF16)

    def multiply(a, chi):
        near, far = vm[0, a, chi], vm[0, a, 1 - chi]
        return (
            nt(jnp.concatenate([near, far, vm[1, a, 1 - chi]], 0), cm[chi, 0]),
            nt(jnp.concatenate([near, vm[3, a, 1 - chi]], 0), cm[chi, 1]),
            nt(jnp.concatenate([near, vm[2, a, 1 - chi]], 0), cm[chi, 2]),
            nt(near, near),
        )

    def keep(blocks):
        for value, (start, rows) in zip(blocks, ((0, 144), (144, 96), (240, 96), (336, 48))):
            kept[start : start + rows, : value.shape[1]] = value

    def finish(a):
        first = (kept[0:144, :], kept[144:240, :], kept[240:336, :], kept[336:384, :ROWS])
        combine_inner([first, multiply(a, 1)], a, out_ref)

    fill(0, 0)
    keep(multiply(0, 0))
    fill(0, 1)

    @pl.loop(1, 8)
    def _(a):
        finish(a - 1)
        fill(a, 0)
        keep(multiply(a, 0))
        fill(a, 1)

    finish(7)


def complex_of(product, sign):
    return product[:24] + sign * roll(product[24:], 64)


def times_i(value, sign):
    return -sign * roll(value, 64)


def combine_inner(blocks, a, out_ref):
    sign = sides()
    second = (lane_ids(NV) & 32) != 0
    upper = {}
    for chi, (tz, y, x, gram) in enumerate(blocks):
        phase = 1.0 if chi == 0 else -1.0
        z_tz = complex_of(tz[:48], sign)
        z_y = complex_of(y[:48], sign)
        z_x = complex_of(x[:48], sign)
        cross_t = complex_of(tz[48:96], sign)
        cross_z = phase * times_i(complex_of(tz[96:144], sign), sign)
        cross_y = phase * complex_of(y[48:96], sign)
        cross_x = phase * times_i(complex_of(x[48:96], sign), sign)
        same = -(z_tz + z_y + z_x)
        cross = jnp.where(second, cross_z, cross_t) + cross_y + cross_x
        same = same + roll(same, -32)
        cross = cross + roll(cross, -32)
        gram = jnp.concatenate([gram, jnp.zeros((ROWS, 128 - ROWS), F32)], 1)
        gram_r = gram[:24] + roll(gram[24:], -24)
        gram_i = roll(gram[:24], -24) - gram[24:]
        y_same, y_cross = roll(z_y, -32), -roll(cross_y, -32)
        x_same, x_cross = roll(z_x, -32), -roll(cross_x, -32)
        upper[chi, chi] = (same, y_same, x_same, gram_r, gram_i)
        upper[1 - chi, chi] = (cross, y_cross, x_cross, None, None)

    def whole(item, ri):
        return placed([[upper[row, col][item] for col in range(2)] for row in range(2)], ri)

    first_rows = lax.broadcasted_iota(jnp.int32, (ROWS, 128), 0) < NV
    cols = lane_ids(ROWS)
    flip = jnp.where(first_rows == (cols < NV), 1.0, -1.0).astype(F32)
    zero = jnp.zeros((NV, 128), F32)
    for ri in range(2):
        out_ref[a, 1, ri] = whole(1, ri)
        out_ref[a, 2, ri] = whole(2, ri)
        inner = whole(0, ri)
        turned = jnp.concatenate([inner, jnp.zeros((80, 128), F32)], 0).T[:ROWS]
        turned = flip * turned if ri == 0 else -flip * turned
        gram = [[upper[0, 0][3 + ri], zero], [zero, upper[1, 1][3 + ri]]]
        out_ref[a, 0, ri] = placed(gram, 0) + inner + turned


def placed(parts, ri):
    lanes = lane_ids(NV)
    left, right = lanes < NV, (lanes >= NV) & (lanes < 2 * NV)
    rows = []
    for row in range(2):
        second = jnp.where(right, roll(parts[row][1], NV - 64 * ri), 0.0)
        rows.append(jnp.where(left, roll(parts[row][0], -64 * ri), second))
    return jnp.concatenate(rows, 0)


def sides():
    return jnp.where(lane_ids(NV) < 64, 1.0, -1.0).astype(F32)


def inner_call(vectors, links):
    shape = jax.ShapeDtypeStruct
    vmem = pl.BlockSpec(memory_space=pltpu.VMEM)
    return pl.pallas_call(
        inner_kernel,
        out_shape=(
            shape((8, 3, 2, ROWS, 128), F32),
            shape((8, 2, ROWS, 384), BF16),
            shape((2, 8, 2, ROWS, 384), BF16),
            shape((8, 24, 128), F32),
            shape((8, 24, 128), F32),
        ),
        in_specs=[vmem] * 2,
        out_specs=(vmem,) * 5,
        scratch_shapes=[
            pltpu.VMEM((4, 8, 2, ROWS, 1536), BF16),
            pltpu.VMEM((8, 4, 5, 24, 128), F32),
            pltpu.VMEM((2, 3, 128, 1536), BF16),
            pltpu.VMEM((2, 768, 128), F32),
            pltpu.VMEM((384, 128), F32),
        ],
        compiler_params=pltpu.CompilerParams(vmem_limit_bytes=24 * 1024 * 1024),
        cost_estimate=pl.CostEstimate(
            flops=40_000_000_000, bytes_accessed=6_000_000, transcendentals=0
        ),
        name="inner",
    )(vectors, links)


def face_kernel(v_ref, t_ref, z_ref, flat):
    @pl.loop(0, 6)
    def _(step):
        chi, c = step // 3, step % 3
        for sb in range(2):
            for ri in range(2):
                block = v_ref[ri, :, 2 * chi + sb, c].astype(F32)
                flat[sb, pl.ds(ri * 384, 384), :] = block.reshape(384, 128)
        column = pl.multiple_of(c * 128, 128)

        def load(k, plane):
            return flat[plane // 4, pl.ds(plane % 4 * (1, 4)[k], ROWS, stride=16), :].astype(BF16)

        done = exchange([[load(k, plane) for plane in range(8)] for k in range(2)])
        for out, values in zip((t_ref, z_ref), done):
            for a, value in enumerate(values):
                out[a, chi, :, pl.ds(column, 128)] = value


def face_call(vectors):
    face = jax.ShapeDtypeStruct((8, 2, ROWS, 384), BF16)
    vmem = pl.BlockSpec(memory_space=pltpu.VMEM)
    return pl.pallas_call(
        face_kernel,
        out_shape=(face, face),
        in_specs=[vmem],
        out_specs=(vmem, vmem),
        scratch_shapes=[pltpu.VMEM((2, 768, 128), F32)],
        compiler_params=pltpu.CompilerParams(vmem_limit_bytes=12 * 1024 * 1024),
        name="faces",
    )(vectors)


def outer_kernel(ft_ref, fz_ref, lt_ref, lz_ref, ut_ref, uz_ref, out_ref, cm):
    cm[...] = jnp.zeros_like(cm)

    @pl.loop(0, 8)
    def _(a):
        sign = sides()
        parts = ([[None, None], [None, None]], [[None, None], [None, None]])
        for chi in range(2):
            phase = 1.0 if chi == 0 else -1.0
            for mu, (face, links) in enumerate(((ft_ref, ut_ref), (fz_ref, uz_ref))):
                link = [links[a, pl.ds(k, 1), :] for k in range(18)]
                vector = []
                for d in range(3):
                    value = face[a, chi, :, d * 128 : (d + 1) * 128].astype(F32)
                    vector += [value[:NV], value[NV:]]
                for c, both in enumerate(colour(link, vector)):
                    column = slice(c * 128, (c + 1) * 128)
                    cm[mu, 0:24, column] = both[0].astype(BF16)
                    cm[mu, 64:88, column] = both[1].astype(BF16)
                if mu == 0:
                    left = jnp.concatenate([lt_ref[a, chi], lt_ref[a, 1 - chi]], 0)
                else:
                    left = jnp.concatenate([lz_ref[0, a, chi], lz_ref[1, a, 1 - chi]], 0)
                product = nt(left, cm[mu])
                cross = complex_of(product[ROWS:], sign)
                if mu == 1:
                    cross = phase * times_i(cross, sign)
                parts[mu][chi][chi] = -complex_of(product[:ROWS], sign)
                parts[mu][1 - chi][chi] = cross
        for mu in range(2):
            for ri in range(2):
                out_ref[a, mu, ri] = placed(parts[mu], ri)


def outer_call(face_t, face_z, left_t, left_z, link_t, link_z):
    vmem = pl.BlockSpec(memory_space=pltpu.VMEM)
    return pl.pallas_call(
        outer_kernel,
        out_shape=jax.ShapeDtypeStruct((8, 2, 2, ROWS, 128), F32),
        in_specs=[vmem] * 6,
        out_specs=vmem,
        scratch_shapes=[pltpu.VMEM((2, 128, 384), BF16)],
        compiler_params=pltpu.CompilerParams(vmem_limit_bytes=12 * 1024 * 1024),
        name="outer",
    )(face_t, face_z, left_t, left_z, link_t, link_z)


def signs():
    rows = lax.broadcasted_iota(jnp.int32, (ROWS, 128), 0)
    return jnp.where(rows < NV, 1.0, -1.0).astype(F32), jnp.where(lane_ids(1) < NV, 1.0, -1.0).astype(F32)


def split(row):
    keep = lane_ids(1) < ROWS
    return jnp.where(keep, row, 0.0), jnp.where(keep, roll(row, -ROWS), 0.0)


def joined(real, imag):
    lanes = lane_ids(1)
    low, high = lanes < ROWS, (lanes >= ROWS) & (lanes < 2 * ROWS)
    return jnp.where(low, real, jnp.where(high, roll(imag, ROWS), 0.0))


def forward(block, row):
    pr, pi = split(row)
    br, bi = block
    return br * pr - bi * pi, br * pi + bi * pr


def column_of(row, eye):
    return jnp.sum(jnp.where(eye, row, 0.0), axis=1, keepdims=True)


def row_of(column, eye):
    return jnp.sum(jnp.where(eye, column, 0.0), axis=0, keepdims=True)


def backward(block, column_r, column_i, col_sign):
    br, bi = block
    real = jnp.sum(br * column_r + bi * column_i, axis=0, keepdims=True)
    imag = jnp.sum(br * column_i - bi * column_r, axis=0, keepdims=True)
    return joined(col_sign * real, col_sign * imag)


def eye_mask():
    rows = lax.broadcasted_iota(jnp.int32, (ROWS, 128), 0)
    return rows == lane_ids(ROWS)


def local_apply(inner, outer, vec, part_ref, bt_ref, bz_ref):
    eye = eye_mask()
    row_sign, col_sign = signs()
    part_ref[...] = jnp.zeros_like(part_ref)

    @pl.loop(0, 8)
    def _(a):
        own = vec[pl.ds(a, 1), :]
        ahead = (a + 1) % 8
        nxt = vec[pl.ds(ahead, 1), :]
        block = lambda ref, slot: (ref[a, slot, 0], ref[a, slot, 1])
        f0 = forward(block(inner, 0), own)
        f1 = forward(block(inner, 1), own)
        f2 = forward(block(inner, 2), nxt)
        real = jnp.sum(f0[0] + f1[0] + f2[0], axis=1, keepdims=True)
        imag = jnp.sum(f0[1] + f1[1] + f2[1], axis=1, keepdims=True)
        pr, pi = split(own)
        column_r = row_sign * column_of(pr, eye)
        column_i = row_sign * column_of(pi, eye)
        back_y = backward(block(inner, 1), column_r, column_i, col_sign)
        back_x = backward(block(inner, 2), column_r, column_i, col_sign)
        bt_ref[pl.ds(a, 1), :] = backward(block(outer, 0), column_r, column_i, col_sign)
        bz_ref[pl.ds(a, 1), :] = backward(block(outer, 1), column_r, column_i, col_sign)
        part_ref[pl.ds(a, 1), :] += joined(row_of(real, eye), row_of(imag, eye)) + back_y
        part_ref[pl.ds(ahead, 1), :] += back_x


def ahead_apply(outer, vt, vz, part_ref):
    eye = eye_mask()

    @pl.loop(0, 8)
    def _(a):
        ft = forward((outer[a, 0, 0], outer[a, 0, 1]), vt[pl.ds(a, 1), :])
        fz = forward((outer[a, 1, 0], outer[a, 1, 1]), vz[pl.ds(a, 1), :])
        real = jnp.sum(ft[0] + fz[0], axis=1, keepdims=True)
        imag = jnp.sum(ft[1] + fz[1], axis=1, keepdims=True)
        part_ref[pl.ds(a, 1), :] += joined(row_of(real, eye), row_of(imag, eye))


def first_kernel(inner, outer, vec, vt, vz, part_ref, bt_ref, bz_ref):
    local_apply(inner, outer, vec, part_ref, bt_ref, bz_ref)
    ahead_apply(outer, vt, vz, part_ref)


def second_kernel(inner, outer, part, rt, rz, vec_ref, part_ref, bt_ref, bz_ref):
    vec_ref[...] = part[...] + rt[...] + rz[...]
    local_apply(inner, outer, vec_ref, part_ref, bt_ref, bz_ref)


def last_kernel(outer, part, rt, rz, vt, vz, out_ref):
    out_ref[...] = part[...] + rt[...] + rz[...]
    ahead_apply(outer, vt, vz, out_ref)


def small_call(kernel, count, name, *args):
    vmem = pl.BlockSpec(memory_space=pltpu.VMEM)
    row = jax.ShapeDtypeStruct((8, 128), F32)
    return pl.pallas_call(
        kernel,
        out_shape=(row,) * count,
        in_specs=[vmem] * len(args),
        out_specs=(vmem,) * count,
        compiler_params=pltpu.CompilerParams(vmem_limit_bytes=12 * 1024 * 1024),
        name=name,
    )(*args)


def shifted(value, axis, steps):
    count = lax.axis_size(axis)
    return lax.ppermute(value, axis, [(k, (k + steps) % count) for k in range(count)])


def per_device(null_vectors, gauge_links, coarse_in):
    vectors = null_vectors.reshape(2, NV, 4, 3, 16, 128)
    links = gauge_links.reshape(2, 4, 3, 3, 16, 128)
    vec = jnp.pad(coarse_in.reshape(8, 2 * ROWS), ((0, 0), (0, 32)))
    face_t, face_z = face_call(vectors)
    face_z = shifted(face_z, "sa", -1)
    face_t = shifted(face_t, "ta", -1)
    vec_t, vec_z = shifted(vec, "ta", -1), shifted(vec, "sa", -1)
    inner, left_t, left_z, link_t, link_z = inner_call(vectors, links)
    outer = outer_call(face_t, face_z, left_t, left_z, link_t, link_z)
    part, bt, bz = small_call(first_kernel, 3, "first", inner, outer, vec, vec_t, vec_z)
    rt, rz = shifted(bt, "ta", 1), shifted(bz, "sa", 1)
    once, part, bt, bz = small_call(second_kernel, 4, "second", inner, outer, part, rt, rz)
    rt, rz = shifted(bt, "ta", 1), shifted(bz, "sa", 1)
    vec_t, vec_z = shifted(once, "ta", -1), shifted(once, "sa", -1)
    (twice,) = small_call(last_kernel, 1, "last", outer, part, rt, rz, vec_t, vec_z)
    blocks = jnp.concatenate([inner[:, :1], outer, inner[:, 1:]], 1)[..., :ROWS]
    return blocks.reshape(1, 1, 8, 5, 2 * ROWS * ROWS), twice[:, : 2 * ROWS].reshape(1, 1, 8, 2 * ROWS)


def solution(mesh):
    placed_sites = P(None, None, None, None, "ta", "sa", None)
    return jax.shard_map(
        per_device,
        mesh=mesh,
        in_specs=(placed_sites, placed_sites, P("ta", "sa", None, None)),
        out_specs=(P("ta", "sa", None, None, None), P("ta", "sa", None, None)),
        check_vma=False,
    )
```

```python
import jax
import jax.numpy as jnp
from jax import lax
from jax.experimental import pallas as pl
from jax.experimental.pallas import tpu as pltpu
from jax.sharding import PartitionSpec as P

NV = 24
ROWS = 48
F32 = jnp.float32
BF16 = jnp.bfloat16


def lane_ids(rows):
    return lax.broadcasted_iota(jnp.int32, (rows, 128), 1)


def roll(value, shift):
    return pltpu.roll(value, shift % 128, 1)


def exchange_bit(low, high, bit):
    step = 4 << bit
    chosen = (lane_ids(low.shape[0]) & step) != 0
    return jnp.where(chosen, roll(high, step), low), jnp.where(chosen, high, roll(low, -step))


def exchange(sets):
    for bit in range(3):
        for planes in sets:
            for low in range(8):
                if not low >> bit & 1:
                    high = low | 1 << bit
                    planes[low], planes[high] = exchange_bit(planes[low], planes[high], bit)
    return sets


def colour(link, vector):
    out = []
    for c in range(3):
        real = imag = None
        for d in range(3):
            lr, li = link[(c * 3 + d) * 2], link[(c * 3 + d) * 2 + 1]
            vr, vi = vector[d * 2], vector[d * 2 + 1]
            re, im = lr * vr - li * vi, lr * vi + li * vr
            real = re if real is None else real + re
            imag = im if imag is None else imag + im
        out.append((real, imag))
    return out


def nt(a, b):
    return lax.dot_general(a, b, (((1,), (1,)), ((), ())), preferred_element_type=F32)


def inner_kernel(
    v_ref, u_ref, out_ref, lt_ref, lz_ref, ut_ref, uz_ref, vm, uf, cm, flat, kept
):
    flat[...] = jnp.zeros_like(flat)

    @pl.loop(0, 4)
    def _(mu):
        for c in range(3):
            for d in range(3):
                for ri in range(2):
                    row = ((c * 3 + d) * 2 + ri) * 16
                    flat[0, pl.ds(row, 16), :] = 0.5 * u_ref[ri, mu, c, d].astype(F32)

        drop = ((lane_ids(24) & 12) == 12) & (mu == 1)

        def load(t, plane):
            first = plane % 4 * 4 + 3 if t == 4 else t * 4 + plane % 4
            return flat[0, pl.ds(first, 24, stride=16), :]

        for group in ((0, 1), (2, 3), (4,)):
            done = exchange([[load(t, plane) for plane in range(8)] for t in group])
            for t, values in zip(group, done):
                for a, value in enumerate(values):
                    uf[a, mu, t] = value if t == 4 else jnp.where(drop, 0.0, value)

    for a in range(8):
        uz_ref[a] = uf[a, 1, 4]

    for a in range(8):
        ut_ref[a] = uf[a, 0, 3]

    @pl.loop(0, 6)
    def _(step):
        chi, c = step // 3, step % 3
        for sb in range(2):
            for ri in range(2):
                block = v_ref[ri, :, 2 * chi + sb, c].astype(F32)
                flat[sb, pl.ds(ri * 384, 384), :] = block.reshape(384, 128)

        def load(t, plane):
            sb, q = plane // 4, plane % 4
            first = q * 4 + 3 if t == 4 else t * 4 + q
            return flat[sb, pl.ds(first, ROWS, stride=16), :].astype(BF16)

        second = (lane_ids(ROWS) & 16) != 0
        for group in ((0, 1), (2, 3), (4,)):
            done = exchange([[load(t, plane) for plane in range(8)] for t in group])
            turned = [[jnp.where(second, -value, value) for value in values] for values in done]
            if group != (4,):
                swapped = [
                    [jnp.where(second, roll(value, 16), roll(value, -16)) for value in values]
                    for values in done
                ]
            for k, t in enumerate(group):
                for a in range(8):
                    if t == 4:
                        column = pl.multiple_of(c * 128, 128)
                        lz_ref[0, a, chi, :, pl.ds(column, 128)] = done[k][a]
                        lz_ref[1, a, chi, :, pl.ds(column, 128)] = turned[k][a]
                        continue
                    column = pl.multiple_of((t * 3 + c) * 128, 128)
                    vm[0, a, chi, :, pl.ds(column, 128)] = done[k][a]
                    vm[1, a, chi, :, pl.ds(column, 128)] = turned[k][a]
                    value = swapped[k][a]
                    vm[2, a, chi, :, pl.ds(column, 128)] = value
                    vm[3, a, chi, :, pl.ds(column, 128)] = jnp.where(second, value, -value)

    for a in range(8):
        for chi in range(2):
            lt_ref[a, chi] = vm[0, a, chi, :, 9 * 128 :]

    cm[...] = jnp.zeros_like(cm)

    def fill(a, chi):
        ahead = lax.rem(a + 1, 8)
        x_last = (lane_ids(NV) & 3) == 3
        x_last_pair = (lane_ids(ROWS) & 3) == 3
        y_last = lane_ids(NV) >= 96
        for t in range(4):
            for mu in range(4):
                if mu == 0 and t == 3:
                    continue
                link = [uf[a, mu, t, pl.ds(k, 1), :] for k in range(18)]
                vector = []
                for d in range(3):
                    first = (((t + 1) if mu == 0 else t) * 3 + d) * 128
                    value = vm[0, a, chi, :, first : first + 128]
                    if mu == 1:
                        value = roll(value, -4)
                    elif mu == 2:
                        value = roll(value, -32)
                    elif mu == 3:
                        other = vm[0, ahead, chi, :, first : first + 128]
                        value = jnp.where(x_last_pair, roll(other, 3), roll(value, -1))
                    value = value.astype(F32)
                    vector += [value[:NV], value[NV:]]
                for c, parts in enumerate(colour(link, vector)):
                    column = slice((t * 3 + c) * 128, (t * 3 + c + 1) * 128)
                    for ri in range(2):
                        if mu < 2:
                            row = ri * 64 + mu * 32
                            cm[chi, 0, row : row + 24, column] = parts[ri].astype(BF16)
                        else:
                            last = y_last if mu == 2 else x_last
                            outer = jnp.where(last, -parts[ri], 0.0)
                            row = ri * 64
                            cm[chi, mu - 1, row : row + 24, column] = parts[ri].astype(BF16)
                            cm[chi, mu - 1, row + 32 : row + 56, column] = outer.astype(BF16)

    def multiply(a, chi):
        near, far = vm[0, a, chi], vm[0, a, 1 - chi]
        return (
            nt(jnp.concatenate([near, far, vm[1, a, 1 - chi]], 0), cm[chi, 0]),
            nt(jnp.concatenate([near, vm[3, a, 1 - chi]], 0), cm[chi, 1]),
            nt(jnp.concatenate([near, vm[2, a, 1 - chi]], 0), cm[chi, 2]),
            nt(near, near),
        )

    def keep(blocks):
        for value, (start, rows) in zip(blocks, ((0, 144), (144, 96), (240, 96), (336, 48))):
            kept[start : start + rows, : value.shape[1]] = value

    def finish(a):
        first = (kept[0:144, :], kept[144:240, :], kept[240:336, :], kept[336:384, :ROWS])
        combine_inner([first, multiply(a, 1)], a, out_ref)

    fill(0, 0)
    keep(multiply(0, 0))
    fill(0, 1)

    @pl.loop(1, 8)
    def _(a):
        finish(a - 1)
        fill(a, 0)
        keep(multiply(a, 0))
        fill(a, 1)

    finish(7)


def complex_of(product, sign):
    return product[:24] + sign * roll(product[24:], 64)


def times_i(value, sign):
    return -sign * roll(value, 64)


def combine_inner(blocks, a, out_ref):
    sign = sides()
    second = (lane_ids(NV) & 32) != 0
    upper = {}
    for chi, (tz, y, x, gram) in enumerate(blocks):
        phase = 1.0 if chi == 0 else -1.0
        z_tz = complex_of(tz[:48], sign)
        z_y = complex_of(y[:48], sign)
        z_x = complex_of(x[:48], sign)
        cross_t = complex_of(tz[48:96], sign)
        cross_z = phase * times_i(complex_of(tz[96:144], sign), sign)
        cross_y = phase * complex_of(y[48:96], sign)
        cross_x = phase * times_i(complex_of(x[48:96], sign), sign)
        same = -(z_tz + z_y + z_x)
        cross = jnp.where(second, cross_z, cross_t) + cross_y + cross_x
        same = same + roll(same, -32)
        cross = cross + roll(cross, -32)
        gram = jnp.concatenate([gram, jnp.zeros((ROWS, 128 - ROWS), F32)], 1)
        gram_r = gram[:24] + roll(gram[24:], -24)
        gram_i = roll(gram[:24], -24) - gram[24:]
        y_same, y_cross = roll(z_y, -32), -roll(cross_y, -32)
        x_same, x_cross = roll(z_x, -32), -roll(cross_x, -32)
        upper[chi, chi] = (same, y_same, x_same, gram_r, gram_i)
        upper[1 - chi, chi] = (cross, y_cross, x_cross, None, None)

    def whole(item, ri):
        return placed([[upper[row, col][item] for col in range(2)] for row in range(2)], ri)

    first_rows = lax.broadcasted_iota(jnp.int32, (ROWS, 128), 0) < NV
    cols = lane_ids(ROWS)
    flip = jnp.where(first_rows == (cols < NV), 1.0, -1.0).astype(F32)
    zero = jnp.zeros((NV, 128), F32)
    for ri in range(2):
        out_ref[a, 1, ri] = whole(1, ri)
        out_ref[a, 2, ri] = whole(2, ri)
        inner = whole(0, ri)
        turned = jnp.concatenate([inner, jnp.zeros((80, 128), F32)], 0).T[:ROWS]
        turned = flip * turned if ri == 0 else -flip * turned
        gram = [[upper[0, 0][3 + ri], zero], [zero, upper[1, 1][3 + ri]]]
        out_ref[a, 0, ri] = placed(gram, 0) + inner + turned


def placed(parts, ri):
    lanes = lane_ids(NV)
    left, right = lanes < NV, (lanes >= NV) & (lanes < 2 * NV)
    rows = []
    for row in range(2):
        second = jnp.where(right, roll(parts[row][1], NV - 64 * ri), 0.0)
        rows.append(jnp.where(left, roll(parts[row][0], -64 * ri), second))
    return jnp.concatenate(rows, 0)


def sides():
    return jnp.where(lane_ids(NV) < 64, 1.0, -1.0).astype(F32)


def inner_call(vectors, links):
    shape = jax.ShapeDtypeStruct
    vmem = pl.BlockSpec(memory_space=pltpu.VMEM)
    return pl.pallas_call(
        inner_kernel,
        out_shape=(
            shape((8, 3, 2, ROWS, 128), F32),
            shape((8, 2, ROWS, 384), BF16),
            shape((2, 8, 2, ROWS, 384), BF16),
            shape((8, 24, 128), F32),
            shape((8, 24, 128), F32),
        ),
        in_specs=[vmem] * 2,
        out_specs=(vmem,) * 5,
        scratch_shapes=[
            pltpu.VMEM((4, 8, 2, ROWS, 1536), BF16),
            pltpu.VMEM((8, 4, 5, 24, 128), F32),
            pltpu.VMEM((2, 3, 128, 1536), BF16),
            pltpu.VMEM((2, 768, 128), F32),
            pltpu.VMEM((384, 128), F32),
        ],
        compiler_params=pltpu.CompilerParams(vmem_limit_bytes=24 * 1024 * 1024),
        cost_estimate=pl.CostEstimate(
            flops=40_000_000_000, bytes_accessed=6_000_000, transcendentals=0
        ),
        name="inner",
    )(vectors, links)


def face_kernel(v_ref, t_ref, z_ref, flat):
    @pl.loop(0, 6)
    def _(step):
        chi, c = step // 3, step % 3
        for sb in range(2):
            for ri in range(2):
                block = v_ref[ri, :, 2 * chi + sb, c].astype(F32)
                flat[sb, pl.ds(ri * 384, 384), :] = block.reshape(384, 128)
        column = pl.multiple_of(c * 128, 128)

        def load(k, plane):
            return flat[plane // 4, pl.ds(plane % 4 * (1, 4)[k], ROWS, stride=16), :].astype(BF16)

        done = exchange([[load(k, plane) for plane in range(8)] for k in range(2)])
        for out, values in zip((t_ref, z_ref), done):
            for a, value in enumerate(values):
                out[a, chi, :, pl.ds(column, 128)] = value


def face_call(vectors):
    face = jax.ShapeDtypeStruct((8, 2, ROWS, 384), BF16)
    vmem = pl.BlockSpec(memory_space=pltpu.VMEM)
    return pl.pallas_call(
        face_kernel,
        out_shape=(face, face),
        in_specs=[vmem],
        out_specs=(vmem, vmem),
        scratch_shapes=[pltpu.VMEM((2, 768, 128), F32)],
        compiler_params=pltpu.CompilerParams(vmem_limit_bytes=12 * 1024 * 1024),
        name="faces",
    )(vectors)


def outer_kernel(ft_ref, fz_ref, lt_ref, lz_ref, ut_ref, uz_ref, vec_ref, out_ref, bt_ref, bz_ref, cm):
    cm[...] = jnp.zeros_like(cm)

    @pl.loop(0, 8)
    def _(a):
        for chi in range(2):
            for mu, (face, links) in enumerate(((ft_ref, ut_ref), (fz_ref, uz_ref))):
                link = [links[a, pl.ds(k, 1), :] for k in range(18)]
                vector = []
                for d in range(3):
                    value = face[a, chi, :, d * 128 : (d + 1) * 128].astype(F32)
                    vector += [value[:NV], value[NV:]]
                for c, both in enumerate(colour(link, vector)):
                    column = slice(c * 128, (c + 1) * 128)
                    cm[a, chi, mu, 0:24, column] = both[0].astype(BF16)
                    cm[a, chi, mu, 64:88, column] = both[1].astype(BF16)

    sign = sides()
    eye = eye_mask()
    row_sign, col_sign = signs()
    for a in range(8):
        parts = ([[None, None], [None, None]], [[None, None], [None, None]])
        for chi in range(2):
            phase = 1.0 if chi == 0 else -1.0
            for mu in range(2):
                if mu == 0:
                    left = jnp.concatenate([lt_ref[a, chi], lt_ref[a, 1 - chi]], 0)
                else:
                    left = jnp.concatenate([lz_ref[0, a, chi], lz_ref[1, a, 1 - chi]], 0)
                product = nt(left, cm[a, chi, mu])
                cross = complex_of(product[ROWS:], sign)
                if mu == 1:
                    cross = phase * times_i(cross, sign)
                parts[mu][chi][chi] = -complex_of(product[:ROWS], sign)
                parts[mu][1 - chi][chi] = cross
        pr, pi = split(vec_ref[pl.ds(a, 1), :])
        column_r = row_sign * column_of(pr, eye)
        column_i = row_sign * column_of(pi, eye)
        for mu, back in enumerate((bt_ref, bz_ref)):
            block = placed(parts[mu], 0), placed(parts[mu], 1)
            out_ref[a, mu, 0] = block[0]
            out_ref[a, mu, 1] = block[1]
            back[pl.ds(a, 1), :] = backward(block, column_r, column_i, col_sign)


def outer_call(face_t, face_z, left_t, left_z, link_t, link_z, vec):
    vmem = pl.BlockSpec(memory_space=pltpu.VMEM)
    row = jax.ShapeDtypeStruct((8, 128), F32)
    return pl.pallas_call(
        outer_kernel,
        out_shape=(jax.ShapeDtypeStruct((8, 2, 2, ROWS, 128), F32), row, row),
        in_specs=[vmem] * 7,
        out_specs=(vmem,) * 3,
        scratch_shapes=[pltpu.VMEM((8, 2, 2, 128, 384), BF16)],
        compiler_params=pltpu.CompilerParams(vmem_limit_bytes=12 * 1024 * 1024),
        name="outer",
    )(face_t, face_z, left_t, left_z, link_t, link_z, vec)


def signs():
    rows = lax.broadcasted_iota(jnp.int32, (ROWS, 128), 0)
    return jnp.where(rows < NV, 1.0, -1.0).astype(F32), jnp.where(lane_ids(1) < NV, 1.0, -1.0).astype(F32)


def split(row):
    keep = lane_ids(1) < ROWS
    return jnp.where(keep, row, 0.0), jnp.where(keep, roll(row, -ROWS), 0.0)


def joined(real, imag):
    lanes = lane_ids(1)
    low, high = lanes < ROWS, (lanes >= ROWS) & (lanes < 2 * ROWS)
    return jnp.where(low, real, jnp.where(high, roll(imag, ROWS), 0.0))


def forward(block, row):
    pr, pi = split(row)
    br, bi = block
    return br * pr - bi * pi, br * pi + bi * pr


def column_of(row, eye):
    return jnp.sum(jnp.where(eye, row, 0.0), axis=1, keepdims=True)


def row_of(column, eye):
    return jnp.sum(jnp.where(eye, column, 0.0), axis=0, keepdims=True)


def backward(block, column_r, column_i, col_sign):
    br, bi = block
    real = jnp.sum(br * column_r + bi * column_i, axis=0, keepdims=True)
    imag = jnp.sum(br * column_i - bi * column_r, axis=0, keepdims=True)
    return joined(col_sign * real, col_sign * imag)


def eye_mask():
    rows = lax.broadcasted_iota(jnp.int32, (ROWS, 128), 0)
    return rows == lane_ids(ROWS)


def local_apply(inner, vec, part_ref):
    eye = eye_mask()
    row_sign, col_sign = signs()
    own, kept = [], []
    for a in range(8):
        here, ahead = vec[pl.ds(a, 1), :], vec[pl.ds((a + 1) % 8, 1), :]
        diag, y, x = ((inner[a, k, 0], inner[a, k, 1]) for k in range(3))
        f0, f1, f2 = forward(diag, here), forward(y, here), forward(x, ahead)
        real = jnp.sum(f0[0] + f1[0] + f2[0], axis=1, keepdims=True)
        imag = jnp.sum(f0[1] + f1[1] + f2[1], axis=1, keepdims=True)
        pr, pi = split(here)
        column_r = row_sign * column_of(pr, eye)
        column_i = row_sign * column_of(pi, eye)
        back_y = backward(y, column_r, column_i, col_sign)
        own.append(joined(row_of(real, eye), row_of(imag, eye)) + back_y)
        kept.append(backward(x, column_r, column_i, col_sign))
    for a in range(8):
        part_ref[pl.ds(a, 1), :] = own[a] + kept[(a + 7) % 8]


def ahead_apply(outer, vt, vz, part_ref):
    eye = eye_mask()
    for a in range(8):
        ft = forward((outer[a, 0, 0], outer[a, 0, 1]), vt[pl.ds(a, 1), :])
        fz = forward((outer[a, 1, 0], outer[a, 1, 1]), vz[pl.ds(a, 1), :])
        real = jnp.sum(ft[0] + fz[0], axis=1, keepdims=True)
        imag = jnp.sum(ft[1] + fz[1], axis=1, keepdims=True)
        part_ref[pl.ds(a, 1), :] += joined(row_of(real, eye), row_of(imag, eye))


def first_kernel(inner, outer, vec, vt, vz, part_ref):
    local_apply(inner, vec, part_ref)
    ahead_apply(outer, vt, vz, part_ref)


def back_kernel(outer, part, rt, rz, vec_ref, bt_ref, bz_ref):
    vec_ref[...] = part[...] + rt[...] + rz[...]
    eye = eye_mask()
    row_sign, col_sign = signs()
    for a in range(8):
        pr, pi = split(vec_ref[pl.ds(a, 1), :])
        column_r = row_sign * column_of(pr, eye)
        column_i = row_sign * column_of(pi, eye)
        for mu, back in enumerate((bt_ref, bz_ref)):
            block = outer[a, mu, 0], outer[a, mu, 1]
            back[pl.ds(a, 1), :] = backward(block, column_r, column_i, col_sign)


def last_kernel(outer, part, rt, rz, vt, vz, out_ref):
    out_ref[...] = part[...] + rt[...] + rz[...]
    ahead_apply(outer, vt, vz, out_ref)


def blocks_kernel(inner, outer, out_ref):
    sources = ((inner, 0), (outer, 0), (outer, 1), (inner, 1), (inner, 2))
    for slot, (ref, k) in enumerate(sources):
        for ri in range(2):
            for group in range(ROWS // 8):
                pieces = []
                for row in range(group * 8, group * 8 + 8):
                    pieces.append(jnp.concatenate([ref[a, k, ri, row : row + 1, :] for a in range(8)], 0))
                wide = lane_rows(pieces)
                first = ri * ROWS * ROWS + group * 8 * ROWS
                out_ref[slot, :, first : first + 8 * ROWS] = wide


def lane_rows(pieces):
    tiles = []
    for tile in range(3):
        total = None
        for k, piece in enumerate(pieces):
            shift = k * ROWS - tile * 128
            if -ROWS < shift < 128:
                moved = piece if shift == 0 else roll(piece, shift)
                if shift < 0:
                    moved = jnp.where(lane_ids(8) < ROWS + shift, moved, 0.0)
                elif shift + ROWS > 128:
                    moved = jnp.where(lane_ids(8) >= shift, moved, 0.0)
                total = moved if total is None else total + moved
        tiles.append(total)
    return jnp.concatenate(tiles, 1)


def small_call(kernel, count, name, *args):
    vmem = pl.BlockSpec(memory_space=pltpu.VMEM)
    row = jax.ShapeDtypeStruct((8, 128), F32)
    return pl.pallas_call(
        kernel,
        out_shape=(row,) * count,
        in_specs=[vmem] * len(args),
        out_specs=(vmem,) * count,
        compiler_params=pltpu.CompilerParams(vmem_limit_bytes=12 * 1024 * 1024),
        name=name,
    )(*args)


def blocks_call(inner, outer):
    vmem = pl.BlockSpec(memory_space=pltpu.VMEM)
    return pl.pallas_call(
        blocks_kernel,
        out_shape=jax.ShapeDtypeStruct((5, 8, 2 * ROWS * ROWS), F32),
        in_specs=[vmem] * 2,
        out_specs=vmem,
        compiler_params=pltpu.CompilerParams(vmem_limit_bytes=12 * 1024 * 1024),
        cost_estimate=pl.CostEstimate(flops=0, bytes_accessed=6_000_000, transcendentals=0),
        name="blocks",
    )(inner, outer)


def shifted(value, axis, steps):
    count = lax.axis_size(axis)
    return lax.ppermute(value, axis, [(k, (k + steps) % count) for k in range(count)])


def per_device(null_vectors, gauge_links, coarse_in):
    vectors = null_vectors.reshape(2, NV, 4, 3, 16, 128)
    links = gauge_links.reshape(2, 4, 3, 3, 16, 128)
    vec = jnp.pad(coarse_in.reshape(8, 2 * ROWS), ((0, 0), (0, 32)))
    face_t, face_z = face_call(vectors)
    face_z = shifted(face_z, "sa", -1)
    face_t = shifted(face_t, "ta", -1)
    vec_t, vec_z = shifted(vec, "ta", -1), shifted(vec, "sa", -1)
    inner, left_t, left_z, link_t, link_z = inner_call(vectors, links)
    outer, bt, bz = outer_call(face_t, face_z, left_t, left_z, link_t, link_z, vec)
    rz, rt = shifted(bz, "sa", 1), shifted(bt, "ta", 1)
    (part,) = small_call(first_kernel, 1, "first", inner, outer, vec, vec_t, vec_z)
    once, bt, bz = small_call(back_kernel, 3, "back", outer, part, rt, rz)
    vec_z, vec_t = shifted(once, "sa", -1), shifted(once, "ta", -1)
    rz, rt = shifted(bz, "sa", 1), shifted(bt, "ta", 1)
    (part,) = small_call(local_apply, 1, "local", inner, once)
    blocks = blocks_call(inner, outer)
    (twice,) = small_call(last_kernel, 1, "last", outer, part, rt, rz, vec_t, vec_z)
    blocks = jnp.swapaxes(blocks, 0, 1)
    return blocks.reshape(1, 1, 8, 5, 2 * ROWS * ROWS), twice[:, : 2 * ROWS].reshape(1, 1, 8, 2 * ROWS)


def solution(mesh):
    placed_sites = P(None, None, None, None, "ta", "sa", None)
    return jax.shard_map(
        per_device,
        mesh=mesh,
        in_specs=(placed_sites, placed_sites, P("ta", "sa", None, None)),
        out_specs=(P("ta", "sa", None, None, None), P("ta", "sa", None, None)),
        check_vma=False,
    )
```

```python
import jax
import jax.numpy as jnp
from jax import lax
from jax.experimental import pallas as pl
from jax.experimental.pallas import tpu as pltpu
from jax.sharding import PartitionSpec as P

NV = 24
ROWS = 48
F32 = jnp.float32
BF16 = jnp.bfloat16


def lane_ids(rows):
    return lax.broadcasted_iota(jnp.int32, (rows, 128), 1)


def roll(value, shift):
    return pltpu.roll(value, shift % 128, 1)


def exchange_bit(low, high, bit):
    step = 4 << bit
    chosen = (lane_ids(low.shape[0]) & step) != 0
    return jnp.where(chosen, roll(high, step), low), jnp.where(chosen, high, roll(low, -step))


def exchange(sets):
    for bit in range(3):
        for planes in sets:
            for low in range(8):
                if not low >> bit & 1:
                    high = low | 1 << bit
                    planes[low], planes[high] = exchange_bit(planes[low], planes[high], bit)
    return sets


def colour(link, vector):
    out = []
    for c in range(3):
        real = imag = None
        for d in range(3):
            lr, li = link[(c * 3 + d) * 2], link[(c * 3 + d) * 2 + 1]
            vr, vi = vector[d * 2], vector[d * 2 + 1]
            re, im = lr * vr - li * vi, lr * vi + li * vr
            real = re if real is None else real + re
            imag = im if imag is None else imag + im
        out.append((real, imag))
    return out


def nt(a, b):
    return lax.dot_general(a, b, (((1,), (1,)), ((), ())), preferred_element_type=F32)


def inner_kernel(
    v_ref, u_hbm, out_ref, lt_ref, lz_ref, ut_ref, uz_ref, vm, uf, cm, flat, kept, u_ref, sem
):
    fetch = pltpu.make_async_copy(u_hbm, u_ref, sem)
    fetch.start()

    @pl.loop(0, 6)
    def _(step):
        chi, c = step // 3, step % 3
        for sb in range(2):
            for ri in range(2):
                block = v_ref[ri, :, 2 * chi + sb, c].astype(F32)
                flat[sb, pl.ds(ri * 384, 384), :] = block.reshape(384, 128)

        def load(t, plane):
            sb, q = plane // 4, plane % 4
            first = q * 4 + 3 if t == 4 else t * 4 + q
            return flat[sb, pl.ds(first, ROWS, stride=16), :].astype(BF16)

        second = (lane_ids(ROWS) & 16) != 0
        for group in ((0, 1), (2, 3), (4,)):
            done = exchange([[load(t, plane) for plane in range(8)] for t in group])
            turned = [[jnp.where(second, -value, value) for value in values] for values in done]
            if group != (4,):
                swapped = [
                    [jnp.where(second, roll(value, 16), roll(value, -16)) for value in values]
                    for values in done
                ]
            for k, t in enumerate(group):
                for a in range(8):
                    if t == 4:
                        column = pl.multiple_of(c * 128, 128)
                        lz_ref[0, a, chi, :, pl.ds(column, 128)] = done[k][a]
                        lz_ref[1, a, chi, :, pl.ds(column, 128)] = turned[k][a]
                        continue
                    column = pl.multiple_of((t * 3 + c) * 128, 128)
                    vm[0, a, chi, :, pl.ds(column, 128)] = done[k][a]
                    vm[1, a, chi, :, pl.ds(column, 128)] = turned[k][a]
                    value = swapped[k][a]
                    vm[2, a, chi, :, pl.ds(column, 128)] = value
                    vm[3, a, chi, :, pl.ds(column, 128)] = jnp.where(second, value, -value)

    for a in range(8):
        for chi in range(2):
            lt_ref[a, chi] = vm[0, a, chi, :, 9 * 128 :]

    fetch.wait()

    flat[...] = jnp.zeros_like(flat)

    @pl.loop(0, 4)
    def _(mu):
        for c in range(3):
            for d in range(3):
                for ri in range(2):
                    row = ((c * 3 + d) * 2 + ri) * 16
                    flat[0, pl.ds(row, 16), :] = 0.5 * u_ref[ri, mu, c, d].astype(F32)

        drop = ((lane_ids(24) & 12) == 12) & (mu == 1)

        def load(t, plane):
            first = plane % 4 * 4 + 3 if t == 4 else t * 4 + plane % 4
            return flat[0, pl.ds(first, 24, stride=16), :]

        for group in ((0, 1), (2, 3), (4,)):
            done = exchange([[load(t, plane) for plane in range(8)] for t in group])
            for t, values in zip(group, done):
                for a, value in enumerate(values):
                    uf[a, mu, t] = value if t == 4 else jnp.where(drop, 0.0, value)

    for a in range(8):
        uz_ref[a] = uf[a, 1, 4]

    for a in range(8):
        ut_ref[a] = uf[a, 0, 3]

    cm[...] = jnp.zeros_like(cm)

    def fill(a, chi):
        ahead = lax.rem(a + 1, 8)
        x_last = (lane_ids(NV) & 3) == 3
        x_last_pair = (lane_ids(ROWS) & 3) == 3
        y_last = lane_ids(NV) >= 96
        for t in range(4):
            for mu in range(4):
                if mu == 0 and t == 3:
                    continue
                link = [uf[a, mu, t, pl.ds(k, 1), :] for k in range(18)]
                vector = []
                for d in range(3):
                    first = (((t + 1) if mu == 0 else t) * 3 + d) * 128
                    value = vm[0, a, chi, :, first : first + 128]
                    if mu == 1:
                        value = roll(value, -4)
                    elif mu == 2:
                        value = roll(value, -32)
                    elif mu == 3:
                        other = vm[0, ahead, chi, :, first : first + 128]
                        value = jnp.where(x_last_pair, roll(other, 3), roll(value, -1))
                    value = value.astype(F32)
                    vector += [value[:NV], value[NV:]]
                for c, parts in enumerate(colour(link, vector)):
                    column = slice((t * 3 + c) * 128, (t * 3 + c + 1) * 128)
                    for ri in range(2):
                        if mu < 2:
                            row = ri * 64 + mu * 32
                            cm[chi, 0, row : row + 24, column] = parts[ri].astype(BF16)
                        else:
                            last = y_last if mu == 2 else x_last
                            outer = jnp.where(last, -parts[ri], 0.0)
                            row = ri * 64
                            cm[chi, mu - 1, row : row + 24, column] = parts[ri].astype(BF16)
                            cm[chi, mu - 1, row + 32 : row + 56, column] = outer.astype(BF16)

    def multiply(a, chi):
        near, far = vm[0, a, chi], vm[0, a, 1 - chi]
        return (
            nt(jnp.concatenate([near, far, vm[1, a, 1 - chi]], 0), cm[chi, 0]),
            nt(jnp.concatenate([near, vm[3, a, 1 - chi]], 0), cm[chi, 1]),
            nt(jnp.concatenate([near, vm[2, a, 1 - chi]], 0), cm[chi, 2]),
            nt(near, near),
        )

    def keep(blocks):
        for value, (start, rows) in zip(blocks, ((0, 144), (144, 96), (240, 96), (336, 48))):
            kept[start : start + rows, : value.shape[1]] = value

    def finish(a):
        first = (kept[0:144, :], kept[144:240, :], kept[240:336, :], kept[336:384, :ROWS])
        combine_inner([first, multiply(a, 1)], a, out_ref)

    fill(0, 0)
    keep(multiply(0, 0))
    fill(0, 1)

    @pl.loop(1, 8)
    def _(a):
        finish(a - 1)
        fill(a, 0)
        keep(multiply(a, 0))
        fill(a, 1)

    finish(7)


def complex_of(product, sign):
    return product[:24] + sign * roll(product[24:], 64)


def times_i(value, sign):
    return -sign * roll(value, 64)


def combine_inner(blocks, a, out_ref):
    sign = sides()
    second = (lane_ids(NV) & 32) != 0
    upper = {}
    for chi, (tz, y, x, gram) in enumerate(blocks):
        phase = 1.0 if chi == 0 else -1.0
        z_tz = complex_of(tz[:48], sign)
        z_y = complex_of(y[:48], sign)
        z_x = complex_of(x[:48], sign)
        cross_t = complex_of(tz[48:96], sign)
        cross_z = phase * times_i(complex_of(tz[96:144], sign), sign)
        cross_y = phase * complex_of(y[48:96], sign)
        cross_x = phase * times_i(complex_of(x[48:96], sign), sign)
        same = -(z_tz + z_y + z_x)
        cross = jnp.where(second, cross_z, cross_t) + cross_y + cross_x
        same = same + roll(same, -32)
        cross = cross + roll(cross, -32)
        gram = jnp.concatenate([gram, jnp.zeros((ROWS, 128 - ROWS), F32)], 1)
        gram_r = gram[:24] + roll(gram[24:], -24)
        gram_i = roll(gram[:24], -24) - gram[24:]
        y_same, y_cross = roll(z_y, -32), -roll(cross_y, -32)
        x_same, x_cross = roll(z_x, -32), -roll(cross_x, -32)
        upper[chi, chi] = (same, y_same, x_same, gram_r, gram_i)
        upper[1 - chi, chi] = (cross, y_cross, x_cross, None, None)

    def whole(item, ri):
        return placed([[upper[row, col][item] for col in range(2)] for row in range(2)], ri)

    first_rows = lax.broadcasted_iota(jnp.int32, (ROWS, 128), 0) < NV
    cols = lane_ids(ROWS)
    flip = jnp.where(first_rows == (cols < NV), 1.0, -1.0).astype(F32)
    zero = jnp.zeros((NV, 128), F32)
    for ri in range(2):
        out_ref[a, 1, ri] = whole(1, ri)
        out_ref[a, 2, ri] = whole(2, ri)
        inner = whole(0, ri)
        turned = jnp.concatenate([inner, jnp.zeros((80, 128), F32)], 0).T[:ROWS]
        turned = flip * turned if ri == 0 else -flip * turned
        gram = [[upper[0, 0][3 + ri], zero], [zero, upper[1, 1][3 + ri]]]
        out_ref[a, 0, ri] = placed(gram, 0) + inner + turned


def placed(parts, ri):
    lanes = lane_ids(NV)
    left, right = lanes < NV, (lanes >= NV) & (lanes < 2 * NV)
    rows = []
    for row in range(2):
        second = jnp.where(right, roll(parts[row][1], NV - 64 * ri), 0.0)
        rows.append(jnp.where(left, roll(parts[row][0], -64 * ri), second))
    return jnp.concatenate(rows, 0)


def sides():
    return jnp.where(lane_ids(NV) < 64, 1.0, -1.0).astype(F32)


def inner_call(vectors, links):
    shape = jax.ShapeDtypeStruct
    vmem = pl.BlockSpec(memory_space=pltpu.VMEM)
    return pl.pallas_call(
        inner_kernel,
        out_shape=(
            shape((8, 3, 2, ROWS, 128), F32),
            shape((8, 2, ROWS, 384), BF16),
            shape((2, 8, 2, ROWS, 384), BF16),
            shape((8, 24, 128), F32),
            shape((8, 24, 128), F32),
        ),
        in_specs=[vmem, pl.BlockSpec(memory_space=pltpu.HBM)],
        out_specs=(vmem,) * 5,
        scratch_shapes=[
            pltpu.VMEM((4, 8, 2, ROWS, 1536), BF16),
            pltpu.VMEM((8, 4, 5, 24, 128), F32),
            pltpu.VMEM((2, 3, 128, 1536), BF16),
            pltpu.VMEM((2, 768, 128), F32),
            pltpu.VMEM((384, 128), F32),
            pltpu.VMEM((2, 4, 3, 3, 16, 128), BF16),
            pltpu.SemaphoreType.DMA,
        ],
        compiler_params=pltpu.CompilerParams(vmem_limit_bytes=24 * 1024 * 1024),
        cost_estimate=pl.CostEstimate(
            flops=40_000_000_000, bytes_accessed=6_000_000, transcendentals=0
        ),
        name="inner",
    )(vectors, pltpu.with_memory_space_constraint(links, pltpu.HBM))


def face_kernel(v_hbm, phi_hbm, t_ref, z_ref, vec_ref, flat, v_ref, phi_ref, sem):
    def fetch(chi, c, k):
        part = (slice(None), slice(None), pl.ds(2 * chi, 2), c)
        return pltpu.make_async_copy(v_hbm.at[part], v_ref.at[part], sem.at[k])

    for k in range(6):
        fetch(k // 3, k % 3, k).start()
    small = pltpu.make_async_copy(phi_hbm, phi_ref, sem.at[6])
    small.start()

    @pl.loop(0, 6)
    def _(step):
        chi, c = step // 3, step % 3
        fetch(chi, c, step).wait()
        for sb in range(2):
            for ri in range(2):
                block = v_ref[ri, :, 2 * chi + sb, c].astype(F32)
                flat[sb, pl.ds(ri * 384, 384), :] = block.reshape(384, 128)
        column = pl.multiple_of(c * 128, 128)

        def load(k, plane):
            return flat[plane // 4, pl.ds(plane % 4 * (1, 4)[k], ROWS, stride=16), :].astype(BF16)

        done = exchange([[load(k, plane) for plane in range(8)] for k in range(2)])
        for out, values in zip((t_ref, z_ref), done):
            for a, value in enumerate(values):
                out[a * 2 + chi, :, pl.ds(column, 128)] = value

    small.wait()
    vec = jnp.concatenate([phi_ref[...], jnp.zeros((8, 32), F32)], 1)
    vec_ref[...] = vec
    pieces = []
    for _ in range(3):
        piece = vec.astype(BF16)
        vec = vec - piece.astype(F32)
        pieces += [piece, jnp.zeros((8, 128), BF16)]
    rider = jnp.concatenate([p.astype(F32) for p in pieces], 0).astype(BF16)
    for ref in (t_ref, z_ref):
        ref[16, :, 0:128] = rider
        ref[16, :, 128:384] = jnp.zeros((ROWS, 256), BF16)


def ridden(face):
    return sum(face[16, 16 * k : 16 * k + 16, 0:128].astype(F32)[:8] for k in range(3))


def face_call(vectors, phi):
    face = jax.ShapeDtypeStruct((17, ROWS, 384), BF16)
    vmem = pl.BlockSpec(memory_space=pltpu.VMEM)
    return pl.pallas_call(
        face_kernel,
        out_shape=(face, face, jax.ShapeDtypeStruct((8, 128), F32)),
        in_specs=[pl.BlockSpec(memory_space=pltpu.HBM)] * 2,
        out_specs=(vmem,) * 3,
        scratch_shapes=[
            pltpu.VMEM((2, 768, 128), F32),
            pltpu.VMEM((2, NV, 4, 3, 16, 128), BF16),
            pltpu.VMEM((8, 2 * ROWS), F32),
            pltpu.SemaphoreType.DMA((7,)),
        ],
        compiler_params=pltpu.CompilerParams(vmem_limit_bytes=12 * 1024 * 1024),
        name="faces",
    )(*(pltpu.with_memory_space_constraint(x, pltpu.HBM) for x in (vectors, phi)))


def outer_kernel(ft_ref, fz_ref, lt_ref, lz_ref, ut_ref, uz_ref, vec_ref, out_ref, bt_ref, bz_ref, cm):
    cm[...] = jnp.zeros_like(cm)

    @pl.loop(0, 8)
    def _(a):
        for chi in range(2):
            for mu, (face, links) in enumerate(((ft_ref, ut_ref), (fz_ref, uz_ref))):
                link = [links[a, pl.ds(k, 1), :] for k in range(18)]
                vector = []
                for d in range(3):
                    value = face[a * 2 + chi, :, d * 128 : (d + 1) * 128].astype(F32)
                    vector += [value[:NV], value[NV:]]
                for c, both in enumerate(colour(link, vector)):
                    column = slice(c * 128, (c + 1) * 128)
                    cm[a, chi, mu, 0:24, column] = both[0].astype(BF16)
                    cm[a, chi, mu, 64:88, column] = both[1].astype(BF16)

    sign = sides()
    eye = eye_mask()
    row_sign, col_sign = signs()
    for a in range(8):
        parts = ([[None, None], [None, None]], [[None, None], [None, None]])
        for chi in range(2):
            phase = 1.0 if chi == 0 else -1.0
            for mu in range(2):
                if mu == 0:
                    left = jnp.concatenate([lt_ref[a, chi], lt_ref[a, 1 - chi]], 0)
                else:
                    left = jnp.concatenate([lz_ref[0, a, chi], lz_ref[1, a, 1 - chi]], 0)
                product = nt(left, cm[a, chi, mu])
                cross = complex_of(product[ROWS:], sign)
                if mu == 1:
                    cross = phase * times_i(cross, sign)
                parts[mu][chi][chi] = -complex_of(product[:ROWS], sign)
                parts[mu][1 - chi][chi] = cross
        pr, pi = split(vec_ref[pl.ds(a, 1), :])
        column_r = row_sign * column_of(pr, eye)
        column_i = row_sign * column_of(pi, eye)
        for mu, back in enumerate((bt_ref, bz_ref)):
            block = placed(parts[mu], 0), placed(parts[mu], 1)
            out_ref[a, mu, 0] = block[0]
            out_ref[a, mu, 1] = block[1]
            back[pl.ds(a, 1), :] = backward(block, column_r, column_i, col_sign)


def outer_call(face_t, face_z, left_t, left_z, link_t, link_z, vec):
    vmem = pl.BlockSpec(memory_space=pltpu.VMEM)
    row = jax.ShapeDtypeStruct((8, 128), F32)
    return pl.pallas_call(
        outer_kernel,
        out_shape=(jax.ShapeDtypeStruct((8, 2, 2, ROWS, 128), F32), row, row),
        in_specs=[vmem] * 7,
        out_specs=(vmem,) * 3,
        scratch_shapes=[pltpu.VMEM((8, 2, 2, 128, 384), BF16)],
        compiler_params=pltpu.CompilerParams(vmem_limit_bytes=12 * 1024 * 1024),
        name="outer",
    )(face_t, face_z, left_t, left_z, link_t, link_z, vec)


def signs():
    rows = lax.broadcasted_iota(jnp.int32, (ROWS, 128), 0)
    return jnp.where(rows < NV, 1.0, -1.0).astype(F32), jnp.where(lane_ids(1) < NV, 1.0, -1.0).astype(F32)


def split(row):
    keep = lane_ids(1) < ROWS
    return jnp.where(keep, row, 0.0), jnp.where(keep, roll(row, -ROWS), 0.0)


def joined(real, imag):
    lanes = lane_ids(1)
    low, high = lanes < ROWS, (lanes >= ROWS) & (lanes < 2 * ROWS)
    return jnp.where(low, real, jnp.where(high, roll(imag, ROWS), 0.0))


def forward(block, row):
    pr, pi = split(row)
    br, bi = block
    return br * pr - bi * pi, br * pi + bi * pr


def column_of(row, eye):
    return jnp.sum(jnp.where(eye, row, 0.0), axis=1, keepdims=True)


def row_of(column, eye):
    return jnp.sum(jnp.where(eye, column, 0.0), axis=0, keepdims=True)


def backward(block, column_r, column_i, col_sign):
    br, bi = block
    real = jnp.sum(br * column_r + bi * column_i, axis=0, keepdims=True)
    imag = jnp.sum(br * column_i - bi * column_r, axis=0, keepdims=True)
    return joined(col_sign * real, col_sign * imag)


def eye_mask():
    rows = lax.broadcasted_iota(jnp.int32, (ROWS, 128), 0)
    return rows == lane_ids(ROWS)


def local_apply(inner, vec, part_ref):
    eye = eye_mask()
    row_sign, col_sign = signs()
    own, kept = [], []
    for a in range(8):
        here, ahead = vec[pl.ds(a, 1), :], vec[pl.ds((a + 1) % 8, 1), :]
        diag, y, x = ((inner[a, k, 0], inner[a, k, 1]) for k in range(3))
        f0, f1, f2 = forward(diag, here), forward(y, here), forward(x, ahead)
        real = jnp.sum(f0[0] + f1[0] + f2[0], axis=1, keepdims=True)
        imag = jnp.sum(f0[1] + f1[1] + f2[1], axis=1, keepdims=True)
        pr, pi = split(here)
        column_r = row_sign * column_of(pr, eye)
        column_i = row_sign * column_of(pi, eye)
        back_y = backward(y, column_r, column_i, col_sign)
        own.append(joined(row_of(real, eye), row_of(imag, eye)) + back_y)
        kept.append(backward(x, column_r, column_i, col_sign))
    for a in range(8):
        part_ref[pl.ds(a, 1), :] = own[a] + kept[(a + 7) % 8]


def ahead_apply(outer, vt, vz):
    eye = eye_mask()
    rows = []
    for a in range(8):
        ft = forward((outer[a, 0, 0], outer[a, 0, 1]), vt[a : a + 1])
        fz = forward((outer[a, 1, 0], outer[a, 1, 1]), vz[a : a + 1])
        real = jnp.sum(ft[0] + fz[0], axis=1, keepdims=True)
        imag = jnp.sum(ft[1] + fz[1], axis=1, keepdims=True)
        rows.append(joined(row_of(real, eye), row_of(imag, eye)))
    return jnp.concatenate(rows, 0)


def first_kernel(inner, outer, vec, ft, fz, part_ref):
    local_apply(inner, vec, part_ref)
    part_ref[...] += ahead_apply(outer, ridden(ft), ridden(fz))


def back_kernel(outer, part, rt, rz, vec_ref, bt_ref, bz_ref):
    vec_ref[...] = part[...] + rt[...] + rz[...]
    eye = eye_mask()
    row_sign, col_sign = signs()
    for a in range(8):
        pr, pi = split(vec_ref[pl.ds(a, 1), :])
        column_r = row_sign * column_of(pr, eye)
        column_i = row_sign * column_of(pi, eye)
        for mu, back in enumerate((bt_ref, bz_ref)):
            block = outer[a, mu, 0], outer[a, mu, 1]
            back[pl.ds(a, 1), :] = backward(block, column_r, column_i, col_sign)


def last_kernel(outer, part, rt, rz, vt, vz, out_ref):
    total = part[...] + rt[...] + rz[...] + ahead_apply(outer, vt[...], vz[...])
    out_ref[...] = total[:, : 2 * ROWS]


def blocks_kernel(inner, outer, out_ref):
    sources = ((inner, 0), (outer, 0), (outer, 1), (inner, 1), (inner, 2))
    for slot, (ref, k) in enumerate(sources):
        for ri in range(2):
            for group in range(ROWS // 8):
                pieces = []
                for row in range(group * 8, group * 8 + 8):
                    pieces.append(jnp.concatenate([ref[a, k, ri, row : row + 1, :] for a in range(8)], 0))
                wide = lane_rows(pieces)
                first = ri * ROWS * ROWS + group * 8 * ROWS
                out_ref[slot, :, first : first + 8 * ROWS] = wide


def lane_rows(pieces):
    tiles = []
    for tile in range(3):
        total = None
        for k, piece in enumerate(pieces):
            shift = k * ROWS - tile * 128
            if -ROWS < shift < 128:
                moved = piece if shift == 0 else roll(piece, shift)
                if shift < 0:
                    moved = jnp.where(lane_ids(8) < ROWS + shift, moved, 0.0)
                elif shift + ROWS > 128:
                    moved = jnp.where(lane_ids(8) >= shift, moved, 0.0)
                total = moved if total is None else total + moved
        tiles.append(total)
    return jnp.concatenate(tiles, 1)


def small_call(kernel, count, name, *args, width=128):
    vmem = pl.BlockSpec(memory_space=pltpu.VMEM)
    row = jax.ShapeDtypeStruct((8, width), F32)
    return pl.pallas_call(
        kernel,
        out_shape=(row,) * count,
        in_specs=[vmem] * len(args),
        out_specs=(vmem,) * count,
        compiler_params=pltpu.CompilerParams(vmem_limit_bytes=12 * 1024 * 1024),
        name=name,
    )(*args)


def blocks_call(inner, outer):
    vmem = pl.BlockSpec(memory_space=pltpu.VMEM)
    return pl.pallas_call(
        blocks_kernel,
        out_shape=jax.ShapeDtypeStruct((5, 8, 2 * ROWS * ROWS), F32),
        in_specs=[vmem] * 2,
        out_specs=vmem,
        compiler_params=pltpu.CompilerParams(vmem_limit_bytes=12 * 1024 * 1024),
        cost_estimate=pl.CostEstimate(flops=0, bytes_accessed=6_000_000, transcendentals=0),
        name="blocks",
    )(inner, outer)


def shifted(value, axis, steps):
    count = lax.axis_size(axis)
    return lax.ppermute(value, axis, [(k, (k + steps) % count) for k in range(count)])


def per_device(null_vectors, gauge_links, coarse_in):
    vectors = null_vectors.reshape(2, NV, 4, 3, 16, 128)
    links = gauge_links.reshape(2, 4, 3, 3, 16, 128)
    face_t, face_z, vec = face_call(vectors, coarse_in.reshape(8, 2 * ROWS))
    face_t, face_z = shifted(face_t, "ta", -1), shifted(face_z, "sa", -1)
    inner, left_t, left_z, link_t, link_z = inner_call(vectors, links)
    outer, bt, bz = outer_call(face_t, face_z, left_t, left_z, link_t, link_z, vec)
    rt, rz = shifted(bt, "ta", 1), shifted(bz, "sa", 1)
    (part,) = small_call(first_kernel, 1, "first", inner, outer, vec, face_t, face_z)
    once, bt, bz = small_call(back_kernel, 3, "back", outer, part, rt, rz)
    vec_t, rt = shifted(once, "ta", -1), shifted(bt, "ta", 1)
    vec_z, rz = shifted(once, "sa", -1), shifted(bz, "sa", 1)
    (part,) = small_call(local_apply, 1, "local", inner, once)
    blocks = blocks_call(inner, outer)
    (twice,) = small_call(last_kernel, 1, "last", outer, part, rt, rz, vec_t, vec_z, width=2 * ROWS)
    blocks = jnp.swapaxes(blocks, 0, 1)
    return blocks.reshape(1, 1, 8, 5, 2 * ROWS * ROWS), twice.reshape(1, 1, 8, 2 * ROWS)


def solution(mesh):
    placed_sites = P(None, None, None, None, "ta", "sa", None)
    return jax.shard_map(
        per_device,
        mesh=mesh,
        in_specs=(placed_sites, placed_sites, P("ta", "sa", None, None)),
        out_specs=(P("ta", "sa", None, None, None), P("ta", "sa", None, None)),
        check_vma=False,
    )
```

```python
import functools

import jax
import jax.numpy as jnp
from jax import lax
from jax.experimental import pallas as pl
from jax.experimental.pallas import tpu as pltpu
from jax.sharding import PartitionSpec as P

NV = 24
ROWS = 48
F32 = jnp.float32
BF16 = jnp.bfloat16


def lane_ids(rows):
    return lax.broadcasted_iota(jnp.int32, (rows, 128), 1)


def roll(value, shift):
    return pltpu.roll(value, shift % 128, 1) if shift % 128 else value


def exchange_bit(low, high, bit):
    step = 4 << bit
    chosen = (lane_ids(low.shape[0]) & step) != 0
    return jnp.where(chosen, roll(high, step), low), jnp.where(chosen, high, roll(low, -step))


def exchange(sets):
    for bit in range(3):
        for planes in sets:
            for low in range(8):
                if not low >> bit & 1:
                    high = low | 1 << bit
                    planes[low], planes[high] = exchange_bit(planes[low], planes[high], bit)
    return sets


def colour(link, vector):
    out = []
    for c in range(3):
        real = imag = None
        for d in range(3):
            lr, li = link[(c * 3 + d) * 2], link[(c * 3 + d) * 2 + 1]
            vr, vi = vector[d * 2], vector[d * 2 + 1]
            re, im = lr * vr - li * vi, lr * vi + li * vr
            real = re if real is None else real + re
            imag = im if imag is None else imag + im
        out.append((real, imag))
    return out


def nt(a, b):
    return lax.dot_general(a, b, (((1,), (1,)), ((), ())), preferred_element_type=F32)


def inner_kernel(
    v_ref, u_hbm, out_ref, lt_ref, lz_ref, ut_ref, uz_ref, vm, uf, cm, flat, kept, u_ref, sem
):
    fetch = pltpu.make_async_copy(u_hbm, u_ref, sem)
    fetch.start()

    @pl.loop(0, 6)
    def _(step):
        chi, c = step // 3, step % 3
        for sb in range(2):
            for ri in range(2):
                block = v_ref[ri, :, 2 * chi + sb, c].astype(F32)
                flat[sb, pl.ds(ri * 384, 384), :] = block.reshape(384, 128)

        def load(t, plane):
            sb, q = plane // 4, plane % 4
            first = q * 4 + 3 if t == 4 else t * 4 + q
            return flat[sb, pl.ds(first, ROWS, stride=16), :].astype(BF16)

        second = (lane_ids(ROWS) & 16) != 0
        for group in ((0, 1), (2, 3), (4,)):
            done = exchange([[load(t, plane) for plane in range(8)] for t in group])
            turned = [[jnp.where(second, -value, value) for value in values] for values in done]
            if group != (4,):
                swapped = [
                    [jnp.where(second, roll(value, 16), roll(value, -16)) for value in values]
                    for values in done
                ]
            for k, t in enumerate(group):
                for a in range(8):
                    if t == 4:
                        column = pl.multiple_of(c * 128, 128)
                        lz_ref[0, a, chi, :, pl.ds(column, 128)] = done[k][a]
                        lz_ref[1, a, chi, :, pl.ds(column, 128)] = turned[k][a]
                        continue
                    column = pl.multiple_of((t * 3 + c) * 128, 128)
                    vm[0, a, chi, :, pl.ds(column, 128)] = done[k][a]
                    vm[1, a, chi, :, pl.ds(column, 128)] = turned[k][a]
                    value = swapped[k][a]
                    vm[2, a, chi, :, pl.ds(column, 128)] = value
                    vm[3, a, chi, :, pl.ds(column, 128)] = jnp.where(second, value, -value)

    for a in range(8):
        for chi in range(2):
            lt_ref[a, chi] = vm[0, a, chi, :, 9 * 128 :]

    fetch.wait()

    flat[...] = jnp.zeros_like(flat)

    @pl.loop(0, 4)
    def _(mu):
        for c in range(3):
            for d in range(3):
                for ri in range(2):
                    row = ((c * 3 + d) * 2 + ri) * 16
                    flat[0, pl.ds(row, 16), :] = 0.5 * u_ref[ri, mu, c, d].astype(F32)

        drop = ((lane_ids(24) & 12) == 12) & (mu == 1)

        def load(t, plane):
            first = plane % 4 * 4 + 3 if t == 4 else t * 4 + plane % 4
            return flat[0, pl.ds(first, 24, stride=16), :]

        for group in ((0, 1), (2, 3), (4,)):
            done = exchange([[load(t, plane) for plane in range(8)] for t in group])
            for t, values in zip(group, done):
                for a, value in enumerate(values):
                    uf[a, mu, t] = value if t == 4 else jnp.where(drop, 0.0, value)

    for a in range(8):
        uz_ref[a] = uf[a, 1, 4]

    for a in range(8):
        ut_ref[a] = uf[a, 0, 3]

    def fill(a, chi):
        ahead = lax.rem(a + 1, 8)
        x_last = (lane_ids(NV) & 3) == 3
        x_last_pair = (lane_ids(ROWS) & 3) == 3
        y_last = lane_ids(NV) >= 96

        def hop(t, mu):
            link = [uf[a, mu, t, pl.ds(k, 1), :] for k in range(18)]
            vector = []
            for d in range(3):
                first = (((t + 1) if mu == 0 else t) * 3 + d) * 128
                value = vm[0, a, chi, :, first : first + 128]
                if mu == 1:
                    value = roll(value, -4)
                elif mu == 2:
                    value = roll(value, -32)
                elif mu == 3:
                    other = vm[0, ahead, chi, :, first : first + 128]
                    value = jnp.where(x_last_pair, roll(other, 3), roll(value, -1))
                value = value.astype(F32)
                vector += [value[:NV], value[NV:]]
            return colour(link, vector)

        nothing = [(jnp.zeros((NV, 128), F32),) * 2] * 3
        for t in range(4):
            for slot in range(3):
                if slot == 0:
                    one, two = hop(t, 0) if t < 3 else nothing, hop(t, 1)
                else:
                    last = y_last if slot == 1 else x_last
                    one = hop(t, slot + 1)
                    two = [[jnp.where(last, -part, 0.0) for part in pair] for pair in one]
                for c in range(3):
                    column = slice((t * 3 + c) * 128, (t * 3 + c + 1) * 128)
                    for ri in range(2):
                        both = jnp.concatenate([one[c][ri], two[c][ri]], 0).astype(BF16)
                        cm[chi, slot, ri * ROWS : ri * ROWS + ROWS, column] = both

    def multiply(a, chi):
        near, far = vm[0, a, chi], vm[0, a, 1 - chi]
        return (
            nt(jnp.concatenate([near, far, vm[1, a, 1 - chi]], 0), cm[chi, 0]),
            nt(jnp.concatenate([near, vm[3, a, 1 - chi]], 0), cm[chi, 1]),
            nt(jnp.concatenate([near, vm[2, a, 1 - chi]], 0), cm[chi, 2]),
            nt(near, near),
        )

    def keep(blocks):
        for value, (start, rows) in zip(blocks, ((0, 144), (144, 96), (240, 96), (336, 48))):
            kept[start : start + rows, : value.shape[1]] = value

    def finish(a):
        first = (kept[0:144, :96], kept[144:240, :96], kept[240:336, :96], kept[336:384, :ROWS])
        combine_inner([first, multiply(a, 1)], a, out_ref)

    fill(0, 0)
    keep(multiply(0, 0))
    fill(0, 1)

    @pl.loop(1, 8)
    def _(a):
        finish(a - 1)
        fill(a, 0)
        keep(multiply(a, 0))
        fill(a, 1)

    finish(7)


def widened(value):
    return jnp.concatenate([value, jnp.zeros((value.shape[0], 128 - value.shape[1]), F32)], 1)


def other_side(value, half):
    return jnp.where(lane_ids(value.shape[0]) < half, roll(value, -half), roll(value, half))


def sides(half):
    return jnp.where(lane_ids(NV) < half, 1.0, -1.0).astype(F32)


def complex_of(product, half):
    return product[:NV] + sides(half) * other_side(product[NV:], half)


def times_i(value, half):
    return -sides(half) * other_side(value, half)


def combine_inner(blocks, a, out_ref):
    lanes = lane_ids(NV)
    second = ((lanes >= 24) & (lanes < 48)) | (lanes >= 72)
    upper, grams = {}, [[None, None], [None, None]]
    zero = jnp.zeros((NV, 128), F32)
    for chi, products in enumerate(blocks):
        tz, y, x, gram = (widened(value) for value in products)
        phase = 1.0 if chi == 0 else -1.0
        z_tz, z_y, z_x = (complex_of(value[:ROWS], 48) for value in (tz, y, x))
        cross_t = complex_of(tz[48:96], 48)
        cross_z = phase * times_i(complex_of(tz[96:144], 48), 48)
        cross_y = phase * complex_of(y[48:96], 48)
        cross_x = phase * times_i(complex_of(x[48:96], 48), 48)
        same = -(z_tz + z_y + z_x)
        cross = jnp.where(second, cross_z, cross_t) + cross_y + cross_x
        same = same + roll(same, -NV)
        cross = cross + roll(cross, -NV)
        upper[chi, chi] = same, roll(z_y, -NV), roll(z_x, -NV)
        upper[1 - chi, chi] = cross, -roll(cross_y, -NV), -roll(cross_x, -NV)
        grams[chi][chi] = complex_of(gram, NV)
        grams[chi][1 - chi] = zero

    def whole(item, ri):
        return placed([[upper[row, col][item] for col in range(2)] for row in range(2)], 48 * ri)

    first_rows = lax.broadcasted_iota(jnp.int32, (ROWS, 128), 0) < NV
    cols = lane_ids(ROWS)
    flip = jnp.where(first_rows == (cols < NV), 1.0, -1.0).astype(F32)
    for ri in range(2):
        out_ref[a, 1, ri] = whole(1, ri)
        out_ref[a, 2, ri] = whole(2, ri)
        inner = whole(0, ri)
        turned = jnp.concatenate([inner, jnp.zeros((80, 128), F32)], 0).T[:ROWS]
        turned = flip * turned if ri == 0 else -flip * turned
        out_ref[a, 0, ri] = placed(grams, NV * ri) + inner + turned


def placed(parts, start):
    lanes = lane_ids(NV)
    left, right = lanes < NV, (lanes >= NV) & (lanes < 2 * NV)
    rows = []
    for row in range(2):
        second = jnp.where(right, roll(parts[row][1], NV - start), 0.0)
        rows.append(jnp.where(left, roll(parts[row][0], -start), second))
    return jnp.concatenate(rows, 0)


def inner_call(vectors, links):
    shape = jax.ShapeDtypeStruct
    vmem = pl.BlockSpec(memory_space=pltpu.VMEM)
    return pl.pallas_call(
        inner_kernel,
        out_shape=(
            shape((8, 3, 2, ROWS, 128), F32),
            shape((8, 2, ROWS, 384), BF16),
            shape((2, 8, 2, ROWS, 384), BF16),
            shape((8, 24, 128), F32),
            shape((8, 24, 128), F32),
        ),
        in_specs=[vmem, pl.BlockSpec(memory_space=pltpu.HBM)],
        out_specs=(vmem,) * 5,
        scratch_shapes=[
            pltpu.VMEM((4, 8, 2, ROWS, 1536), BF16),
            pltpu.VMEM((8, 4, 5, 24, 128), F32),
            pltpu.VMEM((2, 3, 96, 1536), BF16),
            pltpu.VMEM((2, 768, 128), F32),
            pltpu.VMEM((384, 128), F32),
            pltpu.VMEM((2, 4, 3, 3, 16, 128), BF16),
            pltpu.SemaphoreType.DMA,
        ],
        compiler_params=pltpu.CompilerParams(vmem_limit_bytes=24 * 1024 * 1024),
        cost_estimate=pl.CostEstimate(
            flops=40_000_000_000, bytes_accessed=6_000_000, transcendentals=0
        ),
        name="inner",
    )(vectors, pltpu.with_memory_space_constraint(links, pltpu.HBM))


def face_kernel(v_hbm, phi_hbm, t_ref, z_ref, vec_ref, flat, v_ref, phi_ref, sem):
    def fetch(chi, c, k):
        part = (slice(None), slice(None), pl.ds(2 * chi, 2), c)
        return pltpu.make_async_copy(v_hbm.at[part], v_ref.at[part], sem.at[k])

    for k in range(6):
        fetch(k // 3, k % 3, k).start()
    small = pltpu.make_async_copy(phi_hbm, phi_ref, sem.at[6])
    small.start()

    @pl.loop(0, 6)
    def _(step):
        chi, c = step // 3, step % 3
        fetch(chi, c, step).wait()
        for sb in range(2):
            for ri in range(2):
                block = v_ref[ri, :, 2 * chi + sb, c].astype(F32)
                flat[sb, pl.ds(ri * 384, 384), :] = block.reshape(384, 128)
        column = pl.multiple_of(c * 128, 128)

        def load(k, plane):
            return flat[plane // 4, pl.ds(plane % 4 * (1, 4)[k], ROWS, stride=16), :].astype(BF16)

        done = exchange([[load(k, plane) for plane in range(8)] for k in range(2)])
        for out, values in zip((t_ref, z_ref), done):
            for a, value in enumerate(values):
                rows = pl.ds(pl.multiple_of((a * 2 + chi) * ROWS, ROWS), ROWS)
                out[rows, pl.ds(column, 128)] = value

    small.wait()
    vec = jnp.concatenate([phi_ref[...], jnp.zeros((8, 32), F32)], 1)
    vec_ref[...] = vec
    pieces = []
    for _ in range(3):
        piece = vec.astype(BF16)
        vec = vec - piece.astype(F32)
        pieces.append(piece.astype(F32))
    rider = jnp.concatenate(pieces, 1)
    rider = jnp.concatenate([rider, jnp.zeros((8, 384), F32)], 0).astype(BF16)
    for ref in (t_ref, z_ref):
        ref[768:784, :] = rider


def ridden(face):
    return sum(face[768:784, 128 * k : 128 * k + 128].astype(F32)[:8] for k in range(3))


def face_call(vectors, phi):
    face = jax.ShapeDtypeStruct((784, 384), BF16)
    vmem = pl.BlockSpec(memory_space=pltpu.VMEM)
    return pl.pallas_call(
        face_kernel,
        out_shape=(face, face, jax.ShapeDtypeStruct((8, 128), F32)),
        in_specs=[pl.BlockSpec(memory_space=pltpu.HBM)] * 2,
        out_specs=(vmem,) * 3,
        scratch_shapes=[
            pltpu.VMEM((2, 768, 128), F32),
            pltpu.VMEM((2, NV, 4, 3, 16, 128), BF16),
            pltpu.VMEM((8, 2 * ROWS), F32),
            pltpu.SemaphoreType.DMA((7,)),
        ],
        compiler_params=pltpu.CompilerParams(vmem_limit_bytes=12 * 1024 * 1024),
        name="faces",
    )(*(pltpu.with_memory_space_constraint(x, pltpu.HBM) for x in (vectors, phi)))


def outer_kernel(mu, face, *refs):
    lefts, (links, vec_ref, out_ref, back_ref, cm) = refs[:-5], refs[-5:]

    @pl.loop(0, 8)
    def _(a):
        for chi in range(2):
            link = [links[a, pl.ds(k, 1), :] for k in range(18)]
            vector = []
            rows = pl.ds(pl.multiple_of((a * 2 + chi) * ROWS, ROWS), ROWS)
            for d in range(3):
                value = face[rows, d * 128 : (d + 1) * 128].astype(F32)
                vector += [value[:NV], value[NV:]]
            for c, both in enumerate(colour(link, vector)):
                cm[a, chi, :, c * 128 : (c + 1) * 128] = jnp.concatenate(both, 0).astype(BF16)

    eye = eye_mask()
    row_sign, col_sign = signs()
    for a in range(8):
        parts = [[None, None], [None, None]]
        for chi in range(2):
            if mu == 0:
                near, far = lefts[0][a, chi], lefts[0][a, 1 - chi]
            else:
                near, far = lefts[0][0, a, chi], lefts[0][1, a, 1 - chi]
            product = widened(nt(jnp.concatenate([near, far], 0), cm[a, chi]))
            cross = complex_of(product[ROWS:], NV)
            if mu == 1:
                cross = (1.0 if chi == 0 else -1.0) * times_i(cross, NV)
            parts[chi][chi] = -complex_of(product[:ROWS], NV)
            parts[1 - chi][chi] = cross
        pr, pi = split(vec_ref[pl.ds(a, 1), :])
        column_r = row_sign * column_of(pr, eye)
        column_i = row_sign * column_of(pi, eye)
        block = placed(parts, 0), placed(parts, NV)
        out_ref[a, 0] = block[0]
        out_ref[a, 1] = block[1]
        back_ref[pl.ds(a, 1), :] = backward(block, column_r, column_i, col_sign)


def outer_call(mu, name, *args):
    vmem = pl.BlockSpec(memory_space=pltpu.VMEM)
    shape = jax.ShapeDtypeStruct
    return pl.pallas_call(
        functools.partial(outer_kernel, mu),
        out_shape=(shape((8, 2, ROWS, 128), F32), shape((8, 128), F32)),
        in_specs=[vmem] * len(args),
        out_specs=(vmem,) * 2,
        scratch_shapes=[pltpu.VMEM((8, 2, ROWS, 384), BF16)],
        compiler_params=pltpu.CompilerParams(vmem_limit_bytes=12 * 1024 * 1024),
        name=name,
    )(*args)


def signs():
    rows = lax.broadcasted_iota(jnp.int32, (ROWS, 128), 0)
    return jnp.where(rows < NV, 1.0, -1.0).astype(F32), jnp.where(lane_ids(1) < NV, 1.0, -1.0).astype(F32)


def split(row):
    keep = lane_ids(1) < ROWS
    return jnp.where(keep, row, 0.0), jnp.where(keep, roll(row, -ROWS), 0.0)


def joined(real, imag):
    lanes = lane_ids(1)
    low, high = lanes < ROWS, (lanes >= ROWS) & (lanes < 2 * ROWS)
    return jnp.where(low, real, jnp.where(high, roll(imag, ROWS), 0.0))


def forward(block, row):
    pr, pi = split(row)
    br, bi = block
    return br * pr - bi * pi, br * pi + bi * pr


def column_of(row, eye):
    return jnp.sum(jnp.where(eye, row, 0.0), axis=1, keepdims=True)


def row_of(column, eye):
    return jnp.sum(jnp.where(eye, column, 0.0), axis=0, keepdims=True)


def backward(block, column_r, column_i, col_sign):
    br, bi = block
    real = jnp.sum(br * column_r + bi * column_i, axis=0, keepdims=True)
    imag = jnp.sum(br * column_i - bi * column_r, axis=0, keepdims=True)
    return joined(col_sign * real, col_sign * imag)


def eye_mask():
    rows = lax.broadcasted_iota(jnp.int32, (ROWS, 128), 0)
    return rows == lane_ids(ROWS)


def local_apply(inner, vec, part_ref):
    eye = eye_mask()
    row_sign, col_sign = signs()
    own, kept = [], []
    for a in range(8):
        here, ahead = vec[pl.ds(a, 1), :], vec[pl.ds((a + 1) % 8, 1), :]
        diag, y, x = ((inner[a, k, 0], inner[a, k, 1]) for k in range(3))
        f0, f1, f2 = forward(diag, here), forward(y, here), forward(x, ahead)
        real = jnp.sum(f0[0] + f1[0] + f2[0], axis=1, keepdims=True)
        imag = jnp.sum(f0[1] + f1[1] + f2[1], axis=1, keepdims=True)
        pr, pi = split(here)
        column_r = row_sign * column_of(pr, eye)
        column_i = row_sign * column_of(pi, eye)
        back_y = backward(y, column_r, column_i, col_sign)
        own.append(joined(row_of(real, eye), row_of(imag, eye)) + back_y)
        kept.append(backward(x, column_r, column_i, col_sign))
    for a in range(8):
        part_ref[pl.ds(a, 1), :] = own[a] + kept[(a + 7) % 8]


def ahead_apply(outer_t, outer_z, vt, vz):
    eye = eye_mask()
    rows = []
    for a in range(8):
        ft = forward((outer_t[a, 0], outer_t[a, 1]), vt[a : a + 1])
        fz = forward((outer_z[a, 0], outer_z[a, 1]), vz[a : a + 1])
        real = jnp.sum(ft[0] + fz[0], axis=1, keepdims=True)
        imag = jnp.sum(ft[1] + fz[1], axis=1, keepdims=True)
        rows.append(joined(row_of(real, eye), row_of(imag, eye)))
    return jnp.concatenate(rows, 0)


def first_kernel(inner, outer_t, outer_z, vec, ft, fz, part_ref):
    local_apply(inner, vec, part_ref)
    part_ref[...] += ahead_apply(outer_t, outer_z, ridden(ft), ridden(fz))


def back_kernel(outer_t, outer_z, part, rt, rz, vec_ref, bt_ref, bz_ref):
    vec_ref[...] = part[...] + rt[...] + rz[...]
    eye = eye_mask()
    row_sign, col_sign = signs()
    for a in range(8):
        pr, pi = split(vec_ref[pl.ds(a, 1), :])
        column_r = row_sign * column_of(pr, eye)
        column_i = row_sign * column_of(pi, eye)
        for outer, back in ((outer_t, bt_ref), (outer_z, bz_ref)):
            block = outer[a, 0], outer[a, 1]
            back[pl.ds(a, 1), :] = backward(block, column_r, column_i, col_sign)


def last_kernel(outer_t, outer_z, part, rt, rz, vt, vz, out_ref):
    total = part[...] + rt[...] + rz[...] + ahead_apply(outer_t, outer_z, vt[...], vz[...])
    out_ref[...] = total[:, : 2 * ROWS]


def blocks_kernel(inner, outer_t, outer_z, out_ref):
    sources = (inner.at[:, 0], outer_t, outer_z, inner.at[:, 1], inner.at[:, 2])
    for slot, ref in enumerate(sources):
        for ri in range(2):
            for group in range(ROWS // 8):
                pieces = []
                for row in range(group * 8, group * 8 + 8):
                    pieces.append(jnp.concatenate([ref[a, ri, row : row + 1, :] for a in range(8)], 0))
                wide = lane_rows(pieces)
                first = ri * ROWS * ROWS + group * 8 * ROWS
                out_ref[slot, :, first : first + 8 * ROWS] = wide


def lane_rows(pieces):
    tiles = []
    for tile in range(3):
        total = None
        for k, piece in enumerate(pieces):
            shift = k * ROWS - tile * 128
            if -ROWS < shift < 128:
                moved = piece if shift == 0 else roll(piece, shift)
                if shift < 0:
                    moved = jnp.where(lane_ids(8) < ROWS + shift, moved, 0.0)
                elif shift + ROWS > 128:
                    moved = jnp.where(lane_ids(8) >= shift, moved, 0.0)
                total = moved if total is None else total + moved
        tiles.append(total)
    return jnp.concatenate(tiles, 1)


def small_call(kernel, count, name, *args, width=128):
    vmem = pl.BlockSpec(memory_space=pltpu.VMEM)
    row = jax.ShapeDtypeStruct((8, width), F32)
    return pl.pallas_call(
        kernel,
        out_shape=(row,) * count,
        in_specs=[vmem] * len(args),
        out_specs=(vmem,) * count,
        compiler_params=pltpu.CompilerParams(vmem_limit_bytes=12 * 1024 * 1024),
        name=name,
    )(*args)


def blocks_call(inner, outer_t, outer_z):
    vmem = pl.BlockSpec(memory_space=pltpu.VMEM)
    return pl.pallas_call(
        blocks_kernel,
        out_shape=jax.ShapeDtypeStruct((5, 8, 2 * ROWS * ROWS), F32),
        in_specs=[vmem] * 3,
        out_specs=vmem,
        compiler_params=pltpu.CompilerParams(vmem_limit_bytes=12 * 1024 * 1024),
        cost_estimate=pl.CostEstimate(flops=0, bytes_accessed=6_000_000, transcendentals=0),
        name="blocks",
    )(inner, outer_t, outer_z)


def shifted(value, axis, steps):
    count = lax.axis_size(axis)
    return lax.ppermute(value, axis, [(k, (k + steps) % count) for k in range(count)])


def per_device(null_vectors, gauge_links, coarse_in):
    vectors = null_vectors.reshape(2, NV, 4, 3, 16, 128)
    links = gauge_links.reshape(2, 4, 3, 3, 16, 128)
    face_t, face_z, vec = face_call(vectors, coarse_in.reshape(8, 2 * ROWS))
    face_t, face_z = shifted(face_t, "ta", -1), shifted(face_z, "sa", -1)
    inner, left_t, left_z, link_t, link_z = inner_call(vectors, links)
    outer_t, bt = outer_call(0, "outer_t", face_t, left_t, link_t, vec)
    outer_z, bz = outer_call(1, "outer_z", face_z, left_z, link_z, vec)
    rt, rz = shifted(bt, "ta", 1), shifted(bz, "sa", 1)
    (part,) = small_call(first_kernel, 1, "first", inner, outer_t, outer_z, vec, face_t, face_z)
    once, bt, bz = small_call(back_kernel, 3, "back", outer_t, outer_z, part, rt, rz)
    vec_t, rt = shifted(once, "ta", -1), shifted(bt, "ta", 1)
    vec_z, rz = shifted(once, "sa", -1), shifted(bz, "sa", 1)
    (part,) = small_call(local_apply, 1, "local", inner, once)
    blocks = blocks_call(inner, outer_t, outer_z)
    (twice,) = small_call(last_kernel, 1, "last", outer_t, outer_z, part, rt, rz, vec_t, vec_z, width=2 * ROWS)
    blocks = jnp.swapaxes(blocks, 0, 1)
    return blocks.reshape(1, 1, 8, 5, 2 * ROWS * ROWS), twice.reshape(1, 1, 8, 2 * ROWS)


def solution(mesh):
    placed_sites = P(None, None, None, None, "ta", "sa", None)
    return jax.shard_map(
        per_device,
        mesh=mesh,
        in_specs=(placed_sites, placed_sites, P("ta", "sa", None, None)),
        out_specs=(P("ta", "sa", None, None, None), P("ta", "sa", None, None)),
        check_vma=False,
    )
```

```python
import functools

import jax
import jax.numpy as jnp
from jax import lax
from jax.experimental import pallas as pl
from jax.experimental.pallas import tpu as pltpu
from jax.sharding import PartitionSpec as P

NV = 24
ROWS = 48
F32 = jnp.float32
BF16 = jnp.bfloat16


def lane_ids(rows):
    return lax.broadcasted_iota(jnp.int32, (rows, 128), 1)


def roll(value, shift):
    return pltpu.roll(value, shift % 128, 1) if shift % 128 else value


def exchange_bit(low, high, bit):
    step = 4 << bit
    chosen = (lane_ids(low.shape[0]) & step) != 0
    return jnp.where(chosen, roll(high, step), low), jnp.where(chosen, high, roll(low, -step))


def exchange_twice(sets):
    for bit in range(2):
        for planes in sets:
            for low in range(4):
                if not low >> bit & 1:
                    high = low | 1 << bit
                    planes[low], planes[high] = exchange_bit(planes[low], planes[high], bit)
    out = []
    for planes in sets:
        pairs = [exchange_bit(plane, plane, 2) for plane in planes]
        out.append([pair[0] for pair in pairs] + [pair[1] for pair in pairs])
    return out


def exchange(sets):
    for bit in range(3):
        for planes in sets:
            for low in range(8):
                if not low >> bit & 1:
                    high = low | 1 << bit
                    planes[low], planes[high] = exchange_bit(planes[low], planes[high], bit)
    return sets


def colour(link, vector):
    out = []
    for c in range(3):
        real = imag = None
        for d in range(3):
            lr, li = link[(c * 3 + d) * 2], link[(c * 3 + d) * 2 + 1]
            vr, vi = vector[d * 2], vector[d * 2 + 1]
            re, im = lr * vr - li * vi, lr * vi + li * vr
            real = re if real is None else real + re
            imag = im if imag is None else imag + im
        out.append((real, imag))
    return out


def nt(a, b):
    return lax.dot_general(a, b, (((1,), (1,)), ((), ())), preferred_element_type=F32)


def inner_kernel(
    v_ref, u_hbm, own_ref, out_ref, lt_ref, lz_ref, ut_ref, uz_ref, vm, uf, cm, flat, kept, u_ref, sem
):
    fetch = pltpu.make_async_copy(u_hbm, u_ref, sem)
    fetch.start()

    @pl.loop(0, 6)
    def _(step):
        chi, c = step // 3, step % 3
        for sb in range(2):
            for ri in range(2):
                block = v_ref[ri, :, 2 * chi + sb, c].astype(F32)
                flat[sb, pl.ds(ri * 384, 384), :] = block.reshape(384, 128)

        def load(t, plane):
            sb, q = plane // 4, plane % 4
            first = q * 4 + 3 if t == 4 else t * 4 + q
            return flat[sb, pl.ds(first, ROWS, stride=16), :].astype(BF16)

        second = (lane_ids(ROWS) & 16) != 0
        for group in ((0,), (1, 2), (3, 4)):
            if group == (0,):
                rows = [pl.ds(pl.multiple_of((a * 2 + chi) * ROWS, ROWS), ROWS) for a in range(8)]
                column = pl.ds(pl.multiple_of(c * 128, 128), 128)
                done = [[own_ref[part, column] for part in rows]]
            else:
                done = exchange([[load(t, plane) for plane in range(8)] for t in group])
            turned = [[jnp.where(second, -value, value) for value in values] for values in done]
            swapped = [
                [jnp.where(second, roll(value, 16), roll(value, -16)) for value in values]
                for t, values in zip(group, done)
                if t < 4
            ]
            for k, t in enumerate(group):
                for a in range(8):
                    if t == 4:
                        column = pl.multiple_of(c * 128, 128)
                        lz_ref[0, a, chi, :, pl.ds(column, 128)] = done[k][a]
                        lz_ref[1, a, chi, :, pl.ds(column, 128)] = turned[k][a]
                        continue
                    column = pl.multiple_of((t * 3 + c) * 128, 128)
                    vm[0, a, chi, :, pl.ds(column, 128)] = done[k][a]
                    vm[1, a, chi, :, pl.ds(column, 128)] = turned[k][a]
                    value = swapped[k][a]
                    vm[2, a, chi, :, pl.ds(column, 128)] = value
                    vm[3, a, chi, :, pl.ds(column, 128)] = jnp.where(second, value, -value)

    for a in range(8):
        for chi in range(2):
            lt_ref[a, chi] = vm[0, a, chi, :, 9 * 128 :]

    fetch.wait()

    flat[...] = jnp.zeros_like(flat)

    @pl.loop(0, 4)
    def _(mu):
        for c in range(3):
            for d in range(3):
                for ri in range(2):
                    row = ((c * 3 + d) * 2 + ri) * 16
                    flat[0, pl.ds(row, 16), :] = 0.5 * u_ref[ri, mu, c, d].astype(F32)

        drop = ((lane_ids(24) & 12) == 12) & (mu == 1)
        sets = [[flat[0, pl.ds(t * 4 + z, 24, stride=16), :] for z in range(4)] for t in range(4)]
        for group in ((0, 1), (2, 3)):
            done = exchange_twice([sets[t] for t in group])
            for t, values in zip(group, done):
                for a, value in enumerate(values):
                    uf[a, mu, t] = jnp.where(drop, 0.0, value)

        @pl.when(mu == 1)
        def _():
            last = [flat[0, pl.ds(t * 4 + 3, 24, stride=16), :] for t in range(4)]
            for a, value in enumerate(exchange_twice([last])[0]):
                uz_ref[a] = value

    for a in range(8):
        ut_ref[a] = uf[a, 0, 3]

    def fill(a, chi):
        ahead = lax.rem(a + 1, 8)
        x_last = (lane_ids(NV) & 3) == 3
        x_last_pair = (lane_ids(ROWS) & 3) == 3
        y_last = lane_ids(NV) >= 96

        def hop(t, mu):
            link = [uf[a, mu, t, pl.ds(k, 1), :] for k in range(18)]
            vector = []
            for d in range(3):
                first = (((t + 1) if mu == 0 else t) * 3 + d) * 128
                value = vm[0, a, chi, :, first : first + 128]
                if mu == 1:
                    value = roll(value, -4)
                elif mu == 2:
                    value = roll(value, -32)
                elif mu == 3:
                    other = vm[0, ahead, chi, :, first : first + 128]
                    value = jnp.where(x_last_pair, roll(other, 3), roll(value, -1))
                value = value.astype(F32)
                vector += [value[:NV], value[NV:]]
            return colour(link, vector)

        nothing = [(jnp.zeros((NV, 128), F32),) * 2] * 3
        for t in range(4):
            for slot in range(3):
                if slot == 0:
                    one, two = hop(t, 0) if t < 3 else nothing, hop(t, 1)
                else:
                    last = y_last if slot == 1 else x_last
                    one = hop(t, slot + 1)
                    two = [[jnp.where(last, -part, 0.0) for part in pair] for pair in one]
                for c in range(3):
                    column = slice((t * 3 + c) * 128, (t * 3 + c + 1) * 128)
                    for ri in range(2):
                        both = jnp.concatenate([one[c][ri], two[c][ri]], 0).astype(BF16)
                        cm[chi, slot, ri * ROWS : ri * ROWS + ROWS, column] = both

    def multiply(a, chi):
        near, far = vm[0, a, chi], vm[0, a, 1 - chi]
        return (
            nt(jnp.concatenate([near, far, vm[1, a, 1 - chi]], 0), cm[chi, 0]),
            nt(jnp.concatenate([near, vm[3, a, 1 - chi]], 0), cm[chi, 1]),
            nt(jnp.concatenate([near, vm[2, a, 1 - chi]], 0), cm[chi, 2]),
            nt(near, near),
        )

    def keep(blocks):
        for value, (start, rows) in zip(blocks, ((0, 144), (144, 96), (240, 96), (336, 48))):
            kept[start : start + rows, : value.shape[1]] = value

    def finish(a):
        first = (kept[0:144, :96], kept[144:240, :96], kept[240:336, :96], kept[336:384, :ROWS])
        combine_inner([first, multiply(a, 1)], a, out_ref)

    fill(0, 0)
    keep(multiply(0, 0))
    fill(0, 1)

    @pl.loop(1, 8)
    def _(a):
        finish(a - 1)
        fill(a, 0)
        keep(multiply(a, 0))
        fill(a, 1)

    finish(7)


def widened(value):
    return jnp.concatenate([value, jnp.zeros((value.shape[0], 128 - value.shape[1]), F32)], 1)


def other_side(value, half):
    return jnp.where(lane_ids(value.shape[0]) < half, roll(value, -half), roll(value, half))


def sides(half):
    return jnp.where(lane_ids(NV) < half, 1.0, -1.0).astype(F32)


def complex_of(product, half):
    return product[:NV] + sides(half) * other_side(product[NV:], half)


def times_i(value, half):
    return -sides(half) * other_side(value, half)


def combine_inner(blocks, a, out_ref):
    lanes = lane_ids(NV)
    second = ((lanes >= 24) & (lanes < 48)) | (lanes >= 72)
    upper, grams = {}, [[None, None], [None, None]]
    zero = jnp.zeros((NV, 128), F32)
    for chi, products in enumerate(blocks):
        tz, y, x, gram = (widened(value) for value in products)
        phase = 1.0 if chi == 0 else -1.0
        z_tz, z_y, z_x = (complex_of(value[:ROWS], 48) for value in (tz, y, x))
        cross_t = complex_of(tz[48:96], 48)
        cross_z = phase * times_i(complex_of(tz[96:144], 48), 48)
        cross_y = phase * complex_of(y[48:96], 48)
        cross_x = phase * times_i(complex_of(x[48:96], 48), 48)
        same = -(z_tz + z_y + z_x)
        cross = jnp.where(second, cross_z, cross_t) + cross_y + cross_x
        same = same + roll(same, -NV)
        cross = cross + roll(cross, -NV)
        upper[chi, chi] = same, roll(z_y, -NV), roll(z_x, -NV)
        upper[1 - chi, chi] = cross, -roll(cross_y, -NV), -roll(cross_x, -NV)
        grams[chi][chi] = complex_of(gram, NV)
        grams[chi][1 - chi] = zero

    def whole(item, ri):
        return placed([[upper[row, col][item] for col in range(2)] for row in range(2)], 48 * ri)

    first_rows = lax.broadcasted_iota(jnp.int32, (ROWS, 128), 0) < NV
    cols = lane_ids(ROWS)
    flip = jnp.where(first_rows == (cols < NV), 1.0, -1.0).astype(F32)
    for ri in range(2):
        out_ref[a, 1, ri] = whole(1, ri)
        out_ref[a, 2, ri] = whole(2, ri)
        inner = whole(0, ri)
        turned = jnp.concatenate([inner, jnp.zeros((80, 128), F32)], 0).T[:ROWS]
        turned = flip * turned if ri == 0 else -flip * turned
        out_ref[a, 0, ri] = placed(grams, NV * ri) + inner + turned


def placed(parts, start):
    lanes = lane_ids(NV)
    left, right = lanes < NV, (lanes >= NV) & (lanes < 2 * NV)
    rows = []
    for row in range(2):
        second = jnp.where(right, roll(parts[row][1], NV - start), 0.0)
        rows.append(jnp.where(left, roll(parts[row][0], -start), second))
    return jnp.concatenate(rows, 0)


def inner_call(vectors, links, own):
    shape = jax.ShapeDtypeStruct
    vmem = pl.BlockSpec(memory_space=pltpu.VMEM)
    return pl.pallas_call(
        inner_kernel,
        out_shape=(
            shape((8, 3, 2, ROWS, 128), F32),
            shape((8, 2, ROWS, 384), BF16),
            shape((2, 8, 2, ROWS, 384), BF16),
            shape((8, 24, 128), F32),
            shape((8, 24, 128), F32),
        ),
        in_specs=[vmem, pl.BlockSpec(memory_space=pltpu.HBM), vmem],
        out_specs=(vmem,) * 5,
        scratch_shapes=[
            pltpu.VMEM((4, 8, 2, ROWS, 1536), BF16),
            pltpu.VMEM((8, 4, 4, 24, 128), F32),
            pltpu.VMEM((2, 3, 96, 1536), BF16),
            pltpu.VMEM((2, 768, 128), F32),
            pltpu.VMEM((384, 128), F32),
            pltpu.VMEM((2, 4, 3, 3, 16, 128), BF16),
            pltpu.SemaphoreType.DMA,
        ],
        compiler_params=pltpu.CompilerParams(vmem_limit_bytes=24 * 1024 * 1024),
        cost_estimate=pl.CostEstimate(
            flops=40_000_000_000, bytes_accessed=6_000_000, transcendentals=0
        ),
        name="inner",
    )(vectors, pltpu.with_memory_space_constraint(links, pltpu.HBM), own)


def face_kernel(v_hbm, phi_hbm, t_ref, z_ref, vec_ref, flat, v_ref, phi_ref, sem):
    def fetch(chi, c, k):
        part = (slice(None), slice(None), pl.ds(2 * chi, 2), c)
        return pltpu.make_async_copy(v_hbm.at[part], v_ref.at[part], sem.at[k])

    for k in range(6):
        fetch(k // 3, k % 3, k).start()
    small = pltpu.make_async_copy(phi_hbm, phi_ref, sem.at[6])
    small.start()

    @pl.loop(0, 6)
    def _(step):
        chi, c = step // 3, step % 3
        fetch(chi, c, step).wait()
        for sb in range(2):
            for ri in range(2):
                block = v_ref[ri, :, 2 * chi + sb, c].astype(F32)
                flat[sb, pl.ds(ri * 384, 384), :] = block.reshape(384, 128)
        column = pl.multiple_of(c * 128, 128)

        def load(k, plane):
            return flat[plane // 4, pl.ds(plane % 4 * (1, 4)[k], ROWS, stride=16), :].astype(BF16)

        done = exchange([[load(k, plane) for plane in range(8)] for k in range(2)])
        for out, values in zip((t_ref, z_ref), done):
            for a, value in enumerate(values):
                rows = pl.ds(pl.multiple_of((a * 2 + chi) * ROWS, ROWS), ROWS)
                out[rows, pl.ds(column, 128)] = value

    small.wait()
    vec = jnp.concatenate([phi_ref[...], jnp.zeros((8, 32), F32)], 1)
    vec_ref[...] = vec
    pieces = []
    for _ in range(3):
        piece = vec.astype(BF16)
        vec = vec - piece.astype(F32)
        pieces.append(piece.astype(F32))
    rider = jnp.concatenate(pieces, 1)
    rider = jnp.concatenate([rider, jnp.zeros((8, 384), F32)], 0).astype(BF16)
    for ref in (t_ref, z_ref):
        ref[768:784, :] = rider


def ridden(face):
    return sum(face[768:784, 128 * k : 128 * k + 128].astype(F32)[:8] for k in range(3))


def face_call(vectors, phi):
    face = jax.ShapeDtypeStruct((784, 384), BF16)
    vmem = pl.BlockSpec(memory_space=pltpu.VMEM)
    return pl.pallas_call(
        face_kernel,
        out_shape=(face, face, jax.ShapeDtypeStruct((8, 128), F32)),
        in_specs=[pl.BlockSpec(memory_space=pltpu.HBM)] * 2,
        out_specs=(vmem,) * 3,
        scratch_shapes=[
            pltpu.VMEM((2, 768, 128), F32),
            pltpu.VMEM((2, NV, 4, 3, 16, 128), BF16),
            pltpu.VMEM((8, 2 * ROWS), F32),
            pltpu.SemaphoreType.DMA((7,)),
        ],
        compiler_params=pltpu.CompilerParams(vmem_limit_bytes=12 * 1024 * 1024),
        name="faces",
    )(*(pltpu.with_memory_space_constraint(x, pltpu.HBM) for x in (vectors, phi)))


def outer_kernel(mu, face, *refs):
    lefts, (links, vec_ref, out_ref, back_ref, cm) = refs[:-5], refs[-5:]

    @pl.loop(0, 8)
    def _(a):
        for chi in range(2):
            link = [links[a, pl.ds(k, 1), :] for k in range(18)]
            vector = []
            rows = pl.ds(pl.multiple_of((a * 2 + chi) * ROWS, ROWS), ROWS)
            for d in range(3):
                value = face[rows, d * 128 : (d + 1) * 128].astype(F32)
                vector += [value[:NV], value[NV:]]
            for c, both in enumerate(colour(link, vector)):
                cm[a, chi, :, c * 128 : (c + 1) * 128] = jnp.concatenate(both, 0).astype(BF16)

    eye = eye_mask()
    row_sign, col_sign = signs()
    for a in range(8):
        parts = [[None, None], [None, None]]
        for chi in range(2):
            if mu == 0:
                near, far = lefts[0][a, chi], lefts[0][a, 1 - chi]
            else:
                near, far = lefts[0][0, a, chi], lefts[0][1, a, 1 - chi]
            product = widened(nt(jnp.concatenate([near, far], 0), cm[a, chi]))
            cross = complex_of(product[ROWS:], NV)
            if mu == 1:
                cross = (1.0 if chi == 0 else -1.0) * times_i(cross, NV)
            parts[chi][chi] = -complex_of(product[:ROWS], NV)
            parts[1 - chi][chi] = cross
        pr, pi = split(vec_ref[pl.ds(a, 1), :])
        column_r = row_sign * column_of(pr, eye)
        column_i = row_sign * column_of(pi, eye)
        block = placed(parts, 0), placed(parts, NV)
        out_ref[a, 0] = block[0]
        out_ref[a, 1] = block[1]
        back_ref[pl.ds(a, 1), :] = backward(block, column_r, column_i, col_sign)


def outer_call(mu, name, *args):
    vmem = pl.BlockSpec(memory_space=pltpu.VMEM)
    shape = jax.ShapeDtypeStruct
    return pl.pallas_call(
        functools.partial(outer_kernel, mu),
        out_shape=(shape((8, 2, ROWS, 128), F32), shape((8, 128), F32)),
        in_specs=[vmem] * len(args),
        out_specs=(vmem,) * 2,
        scratch_shapes=[pltpu.VMEM((8, 2, ROWS, 384), BF16)],
        compiler_params=pltpu.CompilerParams(vmem_limit_bytes=12 * 1024 * 1024),
        name=name,
    )(*args)


def signs():
    rows = lax.broadcasted_iota(jnp.int32, (ROWS, 128), 0)
    return jnp.where(rows < NV, 1.0, -1.0).astype(F32), jnp.where(lane_ids(1) < NV, 1.0, -1.0).astype(F32)


def split(row):
    keep = lane_ids(1) < ROWS
    return jnp.where(keep, row, 0.0), jnp.where(keep, roll(row, -ROWS), 0.0)


def joined(real, imag):
    lanes = lane_ids(1)
    low, high = lanes < ROWS, (lanes >= ROWS) & (lanes < 2 * ROWS)
    return jnp.where(low, real, jnp.where(high, roll(imag, ROWS), 0.0))


def forward(block, row):
    pr, pi = split(row)
    br, bi = block
    return br * pr - bi * pi, br * pi + bi * pr


def column_of(row, eye):
    return jnp.sum(jnp.where(eye, row, 0.0), axis=1, keepdims=True)


def row_of(column, eye):
    return jnp.sum(jnp.where(eye, column, 0.0), axis=0, keepdims=True)


def backward(block, column_r, column_i, col_sign):
    br, bi = block
    real = jnp.sum(br * column_r + bi * column_i, axis=0, keepdims=True)
    imag = jnp.sum(br * column_i - bi * column_r, axis=0, keepdims=True)
    return joined(col_sign * real, col_sign * imag)


def eye_mask():
    rows = lax.broadcasted_iota(jnp.int32, (ROWS, 128), 0)
    return rows == lane_ids(ROWS)


def local_apply(inner, vec, part_ref):
    eye = eye_mask()
    row_sign, col_sign = signs()
    own, kept = [], []
    for a in range(8):
        here, ahead = vec[pl.ds(a, 1), :], vec[pl.ds((a + 1) % 8, 1), :]
        diag, y, x = ((inner[a, k, 0], inner[a, k, 1]) for k in range(3))
        f0, f1, f2 = forward(diag, here), forward(y, here), forward(x, ahead)
        real = jnp.sum(f0[0] + f1[0] + f2[0], axis=1, keepdims=True)
        imag = jnp.sum(f0[1] + f1[1] + f2[1], axis=1, keepdims=True)
        pr, pi = split(here)
        column_r = row_sign * column_of(pr, eye)
        column_i = row_sign * column_of(pi, eye)
        back_y = backward(y, column_r, column_i, col_sign)
        own.append(joined(row_of(real, eye), row_of(imag, eye)) + back_y)
        kept.append(backward(x, column_r, column_i, col_sign))
    for a in range(8):
        part_ref[pl.ds(a, 1), :] = own[a] + kept[(a + 7) % 8]


def ahead_apply(outer_t, outer_z, vt, vz):
    eye = eye_mask()
    rows = []
    for a in range(8):
        ft = forward((outer_t[a, 0], outer_t[a, 1]), vt[a : a + 1])
        fz = forward((outer_z[a, 0], outer_z[a, 1]), vz[a : a + 1])
        real = jnp.sum(ft[0] + fz[0], axis=1, keepdims=True)
        imag = jnp.sum(ft[1] + fz[1], axis=1, keepdims=True)
        rows.append(joined(row_of(real, eye), row_of(imag, eye)))
    return jnp.concatenate(rows, 0)


def first_kernel(inner, outer_t, outer_z, vec, ft, fz, part_ref):
    local_apply(inner, vec, part_ref)
    part_ref[...] += ahead_apply(outer_t, outer_z, ridden(ft), ridden(fz))


def back_kernel(outer_t, outer_z, part, rt, rz, vec_ref, bt_ref, bz_ref):
    vec_ref[...] = part[...] + rt[...] + rz[...]
    eye = eye_mask()
    row_sign, col_sign = signs()
    for a in range(8):
        pr, pi = split(vec_ref[pl.ds(a, 1), :])
        column_r = row_sign * column_of(pr, eye)
        column_i = row_sign * column_of(pi, eye)
        for outer, back in ((outer_t, bt_ref), (outer_z, bz_ref)):
            block = outer[a, 0], outer[a, 1]
            back[pl.ds(a, 1), :] = backward(block, column_r, column_i, col_sign)


def last_kernel(outer_t, outer_z, part, rt, rz, vt, vz, out_ref):
    total = part[...] + rt[...] + rz[...] + ahead_apply(outer_t, outer_z, vt[...], vz[...])
    out_ref[...] = total[:, : 2 * ROWS]


def blocks_kernel(inner, outer_t, outer_z, out_ref):
    sources = (inner.at[:, 0], outer_t, outer_z, inner.at[:, 1], inner.at[:, 2])
    for slot, ref in enumerate(sources):
        for ri in range(2):
            for group in range(ROWS // 8):
                pieces = []
                for row in range(group * 8, group * 8 + 8):
                    pieces.append(jnp.concatenate([ref[a, ri, row : row + 1, :] for a in range(8)], 0))
                wide = lane_rows(pieces)
                first = ri * ROWS * ROWS + group * 8 * ROWS
                out_ref[slot, :, first : first + 8 * ROWS] = wide


def lane_rows(pieces):
    tiles = []
    for tile in range(3):
        total = None
        for k, piece in enumerate(pieces):
            shift = k * ROWS - tile * 128
            if -ROWS < shift < 128:
                moved = piece if shift == 0 else roll(piece, shift)
                if shift < 0:
                    moved = jnp.where(lane_ids(8) < ROWS + shift, moved, 0.0)
                elif shift + ROWS > 128:
                    moved = jnp.where(lane_ids(8) >= shift, moved, 0.0)
                total = moved if total is None else total + moved
        tiles.append(total)
    return jnp.concatenate(tiles, 1)


def small_call(kernel, count, name, *args, width=128):
    vmem = pl.BlockSpec(memory_space=pltpu.VMEM)
    row = jax.ShapeDtypeStruct((8, width), F32)
    return pl.pallas_call(
        kernel,
        out_shape=(row,) * count,
        in_specs=[vmem] * len(args),
        out_specs=(vmem,) * count,
        compiler_params=pltpu.CompilerParams(vmem_limit_bytes=12 * 1024 * 1024),
        name=name,
    )(*args)


def blocks_call(inner, outer_t, outer_z):
    vmem = pl.BlockSpec(memory_space=pltpu.VMEM)
    return pl.pallas_call(
        blocks_kernel,
        out_shape=jax.ShapeDtypeStruct((5, 8, 2 * ROWS * ROWS), F32),
        in_specs=[vmem] * 3,
        out_specs=vmem,
        compiler_params=pltpu.CompilerParams(vmem_limit_bytes=12 * 1024 * 1024),
        cost_estimate=pl.CostEstimate(flops=0, bytes_accessed=6_000_000, transcendentals=0),
        name="blocks",
    )(inner, outer_t, outer_z)


def shifted(value, axis, steps):
    count = lax.axis_size(axis)
    return lax.ppermute(value, axis, [(k, (k + steps) % count) for k in range(count)])


def per_device(null_vectors, gauge_links, coarse_in):
    vectors = null_vectors.reshape(2, NV, 4, 3, 16, 128)
    links = gauge_links.reshape(2, 4, 3, 3, 16, 128)
    face_t, face_z, vec = face_call(vectors, coarse_in.reshape(8, 2 * ROWS))
    own_t = face_t
    face_t, face_z = shifted(face_t, "ta", -1), shifted(face_z, "sa", -1)
    inner, left_t, left_z, link_t, link_z = inner_call(vectors, links, own_t)
    outer_t, bt = outer_call(0, "outer_t", face_t, left_t, link_t, vec)
    outer_z, bz = outer_call(1, "outer_z", face_z, left_z, link_z, vec)
    rt, rz = shifted(bt, "ta", 1), shifted(bz, "sa", 1)
    (part,) = small_call(first_kernel, 1, "first", inner, outer_t, outer_z, vec, face_t, face_z)
    once, bt, bz = small_call(back_kernel, 3, "back", outer_t, outer_z, part, rt, rz)
    vec_t, rt = shifted(once, "ta", -1), shifted(bt, "ta", 1)
    vec_z, rz = shifted(once, "sa", -1), shifted(bz, "sa", 1)
    (part,) = small_call(local_apply, 1, "local", inner, once)
    blocks = blocks_call(inner, outer_t, outer_z)
    (twice,) = small_call(last_kernel, 1, "last", outer_t, outer_z, part, rt, rz, vec_t, vec_z, width=2 * ROWS)
    blocks = jnp.swapaxes(blocks, 0, 1)
    return blocks.reshape(1, 1, 8, 5, 2 * ROWS * ROWS), twice.reshape(1, 1, 8, 2 * ROWS)


def solution(mesh):
    placed_sites = P(None, None, None, None, "ta", "sa", None)
    return jax.shard_map(
        per_device,
        mesh=mesh,
        in_specs=(placed_sites, placed_sites, P("ta", "sa", None, None)),
        out_specs=(P("ta", "sa", None, None, None), P("ta", "sa", None, None)),
        check_vma=False,
    )
```

```python
import functools

import jax
import jax.numpy as jnp
from jax import lax
from jax.experimental import pallas as pl
from jax.experimental.pallas import tpu as pltpu
from jax.sharding import PartitionSpec as P

NV = 24
ROWS = 48
F32 = jnp.float32
BF16 = jnp.bfloat16


def lane_ids(rows):
    return lax.broadcasted_iota(jnp.int32, (rows, 128), 1)


def roll(value, shift):
    return pltpu.roll(value, shift % 128, 1) if shift % 128 else value


def exchange_bit(low, high, bit):
    step = 4 << bit
    chosen = (lane_ids(low.shape[0]) & step) != 0
    return jnp.where(chosen, roll(high, step), low), jnp.where(chosen, high, roll(low, -step))


def exchange_twice(sets):
    for bit in range(2):
        for planes in sets:
            for low in range(4):
                if not low >> bit & 1:
                    high = low | 1 << bit
                    planes[low], planes[high] = exchange_bit(planes[low], planes[high], bit)
    out = []
    for planes in sets:
        pairs = [exchange_bit(plane, plane, 2) for plane in planes]
        out.append([pair[0] for pair in pairs] + [pair[1] for pair in pairs])
    return out


def exchange(sets):
    for bit in range(3):
        for planes in sets:
            for low in range(8):
                if not low >> bit & 1:
                    high = low | 1 << bit
                    planes[low], planes[high] = exchange_bit(planes[low], planes[high], bit)
    return sets


def colour(link, vector):
    out = []
    for c in range(3):
        real = imag = None
        for d in range(3):
            lr, li = link[(c * 3 + d) * 2], link[(c * 3 + d) * 2 + 1]
            vr, vi = vector[d * 2], vector[d * 2 + 1]
            re, im = lr * vr - li * vi, lr * vi + li * vr
            real = re if real is None else real + re
            imag = im if imag is None else imag + im
        out.append((real, imag))
    return out


def nt(a, b):
    return lax.dot_general(a, b, (((1,), (1,)), ((), ())), preferred_element_type=F32)


def inner_kernel(
    v_ref, u_hbm, own_ref, out_ref, lt_ref, lz_ref, ut_ref, uz_ref, vm, uf, cm, flat, sites, kept, u_ref, sem
):
    fetch = pltpu.make_async_copy(u_hbm, u_ref, sem)
    fetch.start()

    @pl.loop(0, 6)
    def _(step):
        chi, c = step // 3, step % 3
        for sb in range(2):
            parts = [v_ref[ri, :, 2 * chi + sb, c] for ri in range(2)]
            sites[sb] = jnp.swapaxes(jnp.concatenate(parts, 0), 0, 1)

        def load(t, plane):
            sb, q = plane // 4, plane % 4
            first = q * 4 + 3 if t == 4 else t * 4 + q
            return sites[sb, first]

        second = (lane_ids(ROWS) & 16) != 0
        for group in ((0,), (1, 2), (3, 4)):
            if group == (0,):
                rows = [pl.ds(pl.multiple_of((a * 2 + chi) * ROWS, ROWS), ROWS) for a in range(8)]
                column = pl.ds(pl.multiple_of(c * 128, 128), 128)
                done = [[own_ref[part, column] for part in rows]]
            else:
                done = exchange([[load(t, plane) for plane in range(8)] for t in group])
            turned = [[jnp.where(second, -value, value) for value in values] for values in done]
            swapped = [
                [jnp.where(second, roll(value, 16), roll(value, -16)) for value in values]
                for t, values in zip(group, done)
                if t < 4
            ]
            for k, t in enumerate(group):
                for a in range(8):
                    if t == 4:
                        column = pl.multiple_of(c * 128, 128)
                        lz_ref[0, a, chi, :, pl.ds(column, 128)] = done[k][a]
                        lz_ref[1, a, chi, :, pl.ds(column, 128)] = turned[k][a]
                        continue
                    column = pl.multiple_of((t * 3 + c) * 128, 128)
                    vm[0, a, chi, :, pl.ds(column, 128)] = done[k][a]
                    vm[1, a, chi, :, pl.ds(column, 128)] = turned[k][a]
                    value = swapped[k][a]
                    vm[2, a, chi, :, pl.ds(column, 128)] = value
                    vm[3, a, chi, :, pl.ds(column, 128)] = jnp.where(second, value, -value)

    for a in range(8):
        for chi in range(2):
            lt_ref[a, chi] = vm[0, a, chi, :, 9 * 128 :]

    fetch.wait()

    flat[...] = jnp.zeros_like(flat)

    @pl.loop(0, 4)
    def _(mu):
        for c in range(3):
            for d in range(3):
                for ri in range(2):
                    row = ((c * 3 + d) * 2 + ri) * 16
                    flat[pl.ds(row, 16), :] = 0.5 * u_ref[ri, mu, c, d].astype(F32)

        drop = ((lane_ids(24) & 12) == 12) & (mu == 1)
        sets = [[flat[pl.ds(t * 4 + z, 24, stride=16), :] for z in range(4)] for t in range(4)]
        for group in ((0, 1), (2, 3)):
            done = exchange_twice([sets[t] for t in group])
            for t, values in zip(group, done):
                for a, value in enumerate(values):
                    uf[a, mu, t] = jnp.where(drop, 0.0, value)

        @pl.when(mu == 1)
        def _():
            last = [flat[pl.ds(t * 4 + 3, 24, stride=16), :] for t in range(4)]
            for a, value in enumerate(exchange_twice([last])[0]):
                uz_ref[a] = value

    for a in range(8):
        ut_ref[a] = uf[a, 0, 3]

    def fill(a, chi):
        ahead = lax.rem(a + 1, 8)
        x_last = jnp.where((lane_ids(NV) & 3) == 3, -1.0, 0.0).astype(F32)
        x_last_pair = (lane_ids(ROWS) & 3) == 3
        y_last = jnp.where(lane_ids(NV) >= 96, -1.0, 0.0).astype(F32)

        def hop(t, mu):
            link = [uf[a, mu, t, pl.ds(k, 1), :] for k in range(18)]
            vector = []
            for d in range(3):
                first = (((t + 1) if mu == 0 else t) * 3 + d) * 128
                value = vm[0, a, chi, :, first : first + 128]
                if mu == 1:
                    value = roll(value, -4)
                elif mu == 2:
                    value = roll(value, -32)
                elif mu == 3:
                    other = vm[0, ahead, chi, :, first : first + 128]
                    value = jnp.where(x_last_pair, roll(other, 3), roll(value, -1))
                value = value.astype(F32)
                vector += [value[:NV], value[NV:]]
            return colour(link, vector)

        nothing = [(jnp.zeros((NV, 128), F32),) * 2] * 3
        for t in range(4):
            for slot in range(3):
                if slot == 0:
                    one, two = hop(t, 0) if t < 3 else nothing, hop(t, 1)
                else:
                    last = y_last if slot == 1 else x_last
                    one = hop(t, slot + 1)
                    two = [[part * last for part in pair] for pair in one]
                for c in range(3):
                    column = slice((t * 3 + c) * 128, (t * 3 + c + 1) * 128)
                    for ri in range(2):
                        both = jnp.concatenate([one[c][ri], two[c][ri]], 0).astype(BF16)
                        cm[chi, slot, ri * ROWS : ri * ROWS + ROWS, column] = both

    def multiply(a, chi):
        near, far = vm[0, a, chi], vm[0, a, 1 - chi]
        return (
            nt(jnp.concatenate([near, far, vm[1, a, 1 - chi]], 0), cm[chi, 0]),
            nt(jnp.concatenate([near, vm[3, a, 1 - chi]], 0), cm[chi, 1]),
            nt(jnp.concatenate([near, vm[2, a, 1 - chi]], 0), cm[chi, 2]),
            nt(near, near),
        )

    def keep(blocks):
        for value, (start, rows) in zip(blocks, ((0, 144), (144, 96), (240, 96), (336, 48))):
            kept[start : start + rows, : value.shape[1]] = value

    def finish(a):
        first = (kept[0:144, :96], kept[144:240, :96], kept[240:336, :96], kept[336:384, :ROWS])
        combine_inner([first, multiply(a, 1)], a, out_ref)

    fill(0, 0)
    keep(multiply(0, 0))
    fill(0, 1)

    @pl.loop(1, 8)
    def _(a):
        finish(a - 1)
        fill(a, 0)
        keep(multiply(a, 0))
        fill(a, 1)

    finish(7)


def widened(value):
    return jnp.concatenate([value, jnp.zeros((value.shape[0], 128 - value.shape[1]), F32)], 1)


def other_side(value, half):
    return jnp.where(lane_ids(value.shape[0]) < half, roll(value, -half), roll(value, half))


def sides(half):
    return jnp.where(lane_ids(NV) < half, 1.0, -1.0).astype(F32)


def complex_of(product, half):
    return product[:NV] + sides(half) * other_side(product[NV:], half)


def complex_i(product, half):
    return product[NV:] - sides(half) * other_side(product[:NV], half)


def combine_inner(blocks, a, out_ref):
    lanes = lane_ids(NV)
    second = ((lanes >= 24) & (lanes < 48)) | (lanes >= 72)
    upper, grams = {}, [[None, None], [None, None]]
    zero = jnp.zeros((NV, 128), F32)
    for chi, products in enumerate(blocks):
        tz, y, x, gram = (widened(value) for value in products)
        phase = 1.0 if chi == 0 else -1.0
        z_tz, z_y, z_x = (complex_of(value[:ROWS], 48) for value in (tz, y, x))
        cross_t = complex_of(tz[48:96], 48)
        cross_z = phase * complex_i(tz[96:144], 48)
        cross_y = phase * complex_of(y[48:96], 48)
        cross_x = phase * complex_i(x[48:96], 48)
        upper[chi, chi] = -(z_tz + z_y + z_x), z_y, z_x
        cross = jnp.where(second, cross_z, cross_t) + cross_y + cross_x
        upper[1 - chi, chi] = cross, -cross_y, -cross_x
        grams[chi][chi] = complex_of(gram, NV)
        grams[chi][1 - chi] = zero

    def whole(item, starts):
        return placed([[upper[row, col][item] for col in range(2)] for row in range(2)], *starts)

    first_rows = lax.broadcasted_iota(jnp.int32, (ROWS, 128), 0) < NV
    cols = lane_ids(ROWS)
    flip = jnp.where(first_rows == (cols < NV), 1.0, -1.0).astype(F32)
    for ri in range(2):
        first, behind = 48 * ri, 48 * ri + NV
        out_ref[a, 1, ri] = whole(1, (behind,))
        out_ref[a, 2, ri] = whole(2, (behind,))
        inner = whole(0, (first, behind))
        turned = jnp.concatenate([inner, jnp.zeros((80, 128), F32)], 0).T[:ROWS]
        turned = flip * turned if ri == 0 else -flip * turned
        out_ref[a, 0, ri] = placed(grams, NV * ri) + inner + turned


def placed(parts, *starts):
    lanes = lane_ids(NV)
    left, right = lanes < NV, (lanes >= NV) & (lanes < 2 * NV)
    rows = []
    for row in range(2):
        ahead = sum(roll(parts[row][1], NV - start) for start in starts)
        here = sum(roll(parts[row][0], -start) for start in starts)
        rows.append(jnp.where(left, here, jnp.where(right, ahead, 0.0)))
    return jnp.concatenate(rows, 0)


def inner_call(vectors, links, own):
    shape = jax.ShapeDtypeStruct
    vmem = pl.BlockSpec(memory_space=pltpu.VMEM)
    return pl.pallas_call(
        inner_kernel,
        out_shape=(
            shape((8, 3, 2, ROWS, 128), F32),
            shape((8, 2, ROWS, 384), BF16),
            shape((2, 8, 2, ROWS, 384), BF16),
            shape((8, 24, 128), F32),
            shape((8, 24, 128), F32),
        ),
        in_specs=[vmem, pl.BlockSpec(memory_space=pltpu.HBM), vmem],
        out_specs=(vmem,) * 5,
        scratch_shapes=[
            pltpu.VMEM((4, 8, 2, ROWS, 1536), BF16),
            pltpu.VMEM((8, 4, 4, 24, 128), F32),
            pltpu.VMEM((2, 3, 96, 1536), BF16),
            pltpu.VMEM((384, 128), F32),
            pltpu.VMEM((2, 16, ROWS, 128), BF16),
            pltpu.VMEM((384, 128), F32),
            pltpu.VMEM((2, 4, 3, 3, 16, 128), BF16),
            pltpu.SemaphoreType.DMA,
        ],
        compiler_params=pltpu.CompilerParams(vmem_limit_bytes=24 * 1024 * 1024),
        cost_estimate=pl.CostEstimate(
            flops=40_000_000_000, bytes_accessed=6_000_000, transcendentals=0
        ),
        name="inner",
    )(vectors, pltpu.with_memory_space_constraint(links, pltpu.HBM), own)


def face_kernel(v_hbm, phi_hbm, t_ref, z_ref, vec_ref, flat, v_ref, phi_ref, sem):
    def fetch(chi, c, k):
        part = (slice(None), slice(None), pl.ds(2 * chi, 2), c)
        return pltpu.make_async_copy(v_hbm.at[part], v_ref.at[part], sem.at[k])

    for k in range(6):
        fetch(k // 3, k % 3, k).start()
    small = pltpu.make_async_copy(phi_hbm, phi_ref, sem.at[6])
    small.start()

    @pl.loop(0, 6)
    def _(step):
        chi, c = step // 3, step % 3
        fetch(chi, c, step).wait()
        for sb in range(2):
            for ri in range(2):
                block = v_ref[ri, :, 2 * chi + sb, c].astype(F32)
                flat[sb, pl.ds(ri * 384, 384), :] = block.reshape(384, 128)
        column = pl.multiple_of(c * 128, 128)

        def load(k, plane):
            return flat[plane // 4, pl.ds(plane % 4 * (1, 4)[k], ROWS, stride=16), :].astype(BF16)

        done = exchange([[load(k, plane) for plane in range(8)] for k in range(2)])
        for out, values in zip((t_ref, z_ref), done):
            for a, value in enumerate(values):
                rows = pl.ds(pl.multiple_of((a * 2 + chi) * ROWS, ROWS), ROWS)
                out[rows, pl.ds(column, 128)] = value

    small.wait()
    vec = jnp.concatenate([phi_ref[...], jnp.zeros((8, 32), F32)], 1)
    vec_ref[...] = vec
    pieces = []
    for _ in range(3):
        piece = vec.astype(BF16)
        vec = vec - piece.astype(F32)
        pieces.append(piece.astype(F32))
    rider = jnp.concatenate(pieces, 1)
    rider = jnp.concatenate([rider, jnp.zeros((8, 384), F32)], 0).astype(BF16)
    for ref in (t_ref, z_ref):
        ref[768:784, :] = rider


def ridden(face):
    return sum(face[768:784, 128 * k : 128 * k + 128].astype(F32)[:8] for k in range(3))


def face_call(vectors, phi):
    face = jax.ShapeDtypeStruct((784, 384), BF16)
    vmem = pl.BlockSpec(memory_space=pltpu.VMEM)
    return pl.pallas_call(
        face_kernel,
        out_shape=(face, face, jax.ShapeDtypeStruct((8, 128), F32)),
        in_specs=[pl.BlockSpec(memory_space=pltpu.HBM)] * 2,
        out_specs=(vmem,) * 3,
        scratch_shapes=[
            pltpu.VMEM((2, 768, 128), F32),
            pltpu.VMEM((2, NV, 4, 3, 16, 128), BF16),
            pltpu.VMEM((8, 2 * ROWS), F32),
            pltpu.SemaphoreType.DMA((7,)),
        ],
        compiler_params=pltpu.CompilerParams(vmem_limit_bytes=12 * 1024 * 1024),
        name="faces",
    )(*(pltpu.with_memory_space_constraint(x, pltpu.HBM) for x in (vectors, phi)))


def outer_kernel(mu, face, *refs):
    lefts, (links, vec_ref, out_ref, back_ref, cm) = refs[:-5], refs[-5:]

    @pl.loop(0, 8)
    def _(a):
        for chi in range(2):
            link = [links[a, pl.ds(k, 1), :] for k in range(18)]
            vector = []
            rows = pl.ds(pl.multiple_of((a * 2 + chi) * ROWS, ROWS), ROWS)
            for d in range(3):
                value = face[rows, d * 128 : (d + 1) * 128].astype(F32)
                vector += [value[:NV], value[NV:]]
            for c, both in enumerate(colour(link, vector)):
                cm[a, chi, :, c * 128 : (c + 1) * 128] = jnp.concatenate(both, 0).astype(BF16)

    eye = eye_mask()
    row_sign, col_sign = signs()
    for a in range(8):
        parts = [[None, None], [None, None]]
        for chi in range(2):
            if mu == 0:
                near, far = lefts[0][a, chi], lefts[0][a, 1 - chi]
            else:
                near, far = lefts[0][0, a, chi], lefts[0][1, a, 1 - chi]
            product = widened(nt(jnp.concatenate([near, far], 0), cm[a, chi]))
            if mu == 0:
                cross = complex_of(product[ROWS:], NV)
            else:
                cross = (1.0 if chi == 0 else -1.0) * complex_i(product[ROWS:], NV)
            parts[chi][chi] = -complex_of(product[:ROWS], NV)
            parts[1 - chi][chi] = cross
        pr, pi = split(vec_ref[pl.ds(a, 1), :])
        column_r = row_sign * column_of(pr, eye)
        column_i = row_sign * column_of(pi, eye)
        block = placed(parts, 0), placed(parts, NV)
        out_ref[a, 0] = block[0]
        out_ref[a, 1] = block[1]
        back_ref[pl.ds(a, 1), :] = backward(block, column_r, column_i, col_sign)


def outer_call(mu, name, *args):
    vmem = pl.BlockSpec(memory_space=pltpu.VMEM)
    shape = jax.ShapeDtypeStruct
    return pl.pallas_call(
        functools.partial(outer_kernel, mu),
        out_shape=(shape((8, 2, ROWS, 128), F32), shape((8, 128), F32)),
        in_specs=[vmem] * len(args),
        out_specs=(vmem,) * 2,
        scratch_shapes=[pltpu.VMEM((8, 2, ROWS, 384), BF16)],
        compiler_params=pltpu.CompilerParams(vmem_limit_bytes=12 * 1024 * 1024),
        name=name,
    )(*args)


def signs():
    rows = lax.broadcasted_iota(jnp.int32, (ROWS, 128), 0)
    return jnp.where(rows < NV, 1.0, -1.0).astype(F32), jnp.where(lane_ids(1) < NV, 1.0, -1.0).astype(F32)


def split(row):
    keep = lane_ids(1) < ROWS
    return jnp.where(keep, row, 0.0), jnp.where(keep, roll(row, -ROWS), 0.0)


def joined(real, imag):
    lanes = lane_ids(1)
    low, high = lanes < ROWS, (lanes >= ROWS) & (lanes < 2 * ROWS)
    return jnp.where(low, real, jnp.where(high, roll(imag, ROWS), 0.0))


def forward(block, row):
    pr, pi = split(row)
    br, bi = block
    return br * pr - bi * pi, br * pi + bi * pr


def column_of(row, eye):
    return jnp.sum(jnp.where(eye, row, 0.0), axis=1, keepdims=True)


def row_of(column, eye):
    return jnp.sum(jnp.where(eye, column, 0.0), axis=0, keepdims=True)


def backward(block, column_r, column_i, col_sign):
    br, bi = block
    real = jnp.sum(br * column_r + bi * column_i, axis=0, keepdims=True)
    imag = jnp.sum(br * column_i - bi * column_r, axis=0, keepdims=True)
    return joined(col_sign * real, col_sign * imag)


def eye_mask():
    rows = lax.broadcasted_iota(jnp.int32, (ROWS, 128), 0)
    return rows == lane_ids(ROWS)


def local_apply(inner, vec, part_ref):
    eye = eye_mask()
    row_sign, col_sign = signs()
    own, kept = [], []
    for a in range(8):
        here, ahead = vec[pl.ds(a, 1), :], vec[pl.ds((a + 1) % 8, 1), :]
        diag, y, x = ((inner[a, k, 0], inner[a, k, 1]) for k in range(3))
        f0, f1, f2 = forward(diag, here), forward(y, here), forward(x, ahead)
        real = jnp.sum(f0[0] + f1[0] + f2[0], axis=1, keepdims=True)
        imag = jnp.sum(f0[1] + f1[1] + f2[1], axis=1, keepdims=True)
        pr, pi = split(here)
        column_r = row_sign * column_of(pr, eye)
        column_i = row_sign * column_of(pi, eye)
        back_y = backward(y, column_r, column_i, col_sign)
        own.append(joined(row_of(real, eye), row_of(imag, eye)) + back_y)
        kept.append(backward(x, column_r, column_i, col_sign))
    for a in range(8):
        part_ref[pl.ds(a, 1), :] = own[a] + kept[(a + 7) % 8]


def ahead_apply(outer_t, outer_z, vt, vz):
    eye = eye_mask()
    rows = []
    for a in range(8):
        ft = forward((outer_t[a, 0], outer_t[a, 1]), vt[a : a + 1])
        fz = forward((outer_z[a, 0], outer_z[a, 1]), vz[a : a + 1])
        real = jnp.sum(ft[0] + fz[0], axis=1, keepdims=True)
        imag = jnp.sum(ft[1] + fz[1], axis=1, keepdims=True)
        rows.append(joined(row_of(real, eye), row_of(imag, eye)))
    return jnp.concatenate(rows, 0)


def first_kernel(inner, outer_t, outer_z, vec, ft, fz, part_ref):
    local_apply(inner, vec, part_ref)
    part_ref[...] += ahead_apply(outer_t, outer_z, ridden(ft), ridden(fz))


def back_kernel(outer_t, outer_z, part, rt, rz, vec_ref, bt_ref, bz_ref):
    vec_ref[...] = part[...] + rt[...] + rz[...]
    eye = eye_mask()
    row_sign, col_sign = signs()
    for a in range(8):
        pr, pi = split(vec_ref[pl.ds(a, 1), :])
        column_r = row_sign * column_of(pr, eye)
        column_i = row_sign * column_of(pi, eye)
        for outer, back in ((outer_t, bt_ref), (outer_z, bz_ref)):
            block = outer[a, 0], outer[a, 1]
            back[pl.ds(a, 1), :] = backward(block, column_r, column_i, col_sign)


def last_kernel(outer_t, outer_z, part, rt, rz, vt, vz, out_ref):
    total = part[...] + rt[...] + rz[...] + ahead_apply(outer_t, outer_z, vt[...], vz[...])
    out_ref[...] = total[:, : 2 * ROWS]


def blocks_kernel(inner, outer_t, outer_z, out_ref):
    sources = (inner.at[:, 0], outer_t, outer_z, inner.at[:, 1], inner.at[:, 2])
    for slot, ref in enumerate(sources):
        for ri in range(2):
            for group in range(ROWS // 8):
                pieces = []
                for row in range(group * 8, group * 8 + 8):
                    pieces.append(jnp.concatenate([ref[a, ri, row : row + 1, :] for a in range(8)], 0))
                wide = lane_rows(pieces)
                first = ri * ROWS * ROWS + group * 8 * ROWS
                out_ref[slot, :, first : first + 8 * ROWS] = wide


def lane_rows(pieces):
    tiles = []
    for tile in range(3):
        total = None
        for k, piece in enumerate(pieces):
            shift = k * ROWS - tile * 128
            if -ROWS < shift < 128:
                moved = piece if shift == 0 else roll(piece, shift)
                if shift < 0:
                    moved = jnp.where(lane_ids(8) < ROWS + shift, moved, 0.0)
                elif shift + ROWS > 128:
                    moved = jnp.where(lane_ids(8) >= shift, moved, 0.0)
                total = moved if total is None else total + moved
        tiles.append(total)
    return jnp.concatenate(tiles, 1)


def small_call(kernel, count, name, *args, width=128):
    vmem = pl.BlockSpec(memory_space=pltpu.VMEM)
    row = jax.ShapeDtypeStruct((8, width), F32)
    return pl.pallas_call(
        kernel,
        out_shape=(row,) * count,
        in_specs=[vmem] * len(args),
        out_specs=(vmem,) * count,
        compiler_params=pltpu.CompilerParams(vmem_limit_bytes=12 * 1024 * 1024),
        name=name,
    )(*args)


def blocks_call(inner, outer_t, outer_z):
    vmem = pl.BlockSpec(memory_space=pltpu.VMEM)
    return pl.pallas_call(
        blocks_kernel,
        out_shape=jax.ShapeDtypeStruct((5, 8, 2 * ROWS * ROWS), F32),
        in_specs=[vmem] * 3,
        out_specs=vmem,
        compiler_params=pltpu.CompilerParams(vmem_limit_bytes=12 * 1024 * 1024),
        cost_estimate=pl.CostEstimate(flops=0, bytes_accessed=6_000_000, transcendentals=0),
        name="blocks",
    )(inner, outer_t, outer_z)


def shifted(value, axis, steps):
    count = lax.axis_size(axis)
    return lax.ppermute(value, axis, [(k, (k + steps) % count) for k in range(count)])


def per_device(null_vectors, gauge_links, coarse_in):
    vectors = null_vectors.reshape(2, NV, 4, 3, 16, 128)
    links = gauge_links.reshape(2, 4, 3, 3, 16, 128)
    face_t, face_z, vec = face_call(vectors, coarse_in.reshape(8, 2 * ROWS))
    own_t = face_t
    face_t, face_z = shifted(face_t, "ta", -1), shifted(face_z, "sa", -1)
    inner, left_t, left_z, link_t, link_z = inner_call(vectors, links, own_t)
    outer_t, bt = outer_call(0, "outer_t", face_t, left_t, link_t, vec)
    outer_z, bz = outer_call(1, "outer_z", face_z, left_z, link_z, vec)
    rt, rz = shifted(bt, "ta", 1), shifted(bz, "sa", 1)
    (part,) = small_call(first_kernel, 1, "first", inner, outer_t, outer_z, vec, face_t, face_z)
    once, bt, bz = small_call(back_kernel, 3, "back", outer_t, outer_z, part, rt, rz)
    vec_t, rt = shifted(once, "ta", -1), shifted(bt, "ta", 1)
    vec_z, rz = shifted(once, "sa", -1), shifted(bz, "sa", 1)
    (part,) = small_call(local_apply, 1, "local", inner, once)
    blocks = blocks_call(inner, outer_t, outer_z)
    (twice,) = small_call(last_kernel, 1, "last", outer_t, outer_z, part, rt, rz, vec_t, vec_z, width=2 * ROWS)
    blocks = jnp.swapaxes(blocks, 0, 1)
    return blocks.reshape(1, 1, 8, 5, 2 * ROWS * ROWS), twice.reshape(1, 1, 8, 2 * ROWS)


def solution(mesh):
    placed_sites = P(None, None, None, None, "ta", "sa", None)
    return jax.shard_map(
        per_device,
        mesh=mesh,
        in_specs=(placed_sites, placed_sites, P("ta", "sa", None, None)),
        out_specs=(P("ta", "sa", None, None, None), P("ta", "sa", None, None)),
        check_vma=False,
    )
```

```python
import functools

import jax
import jax.numpy as jnp
from jax import lax
from jax.experimental import pallas as pl
from jax.experimental.pallas import tpu as pltpu
from jax.sharding import PartitionSpec as P

NV = 24
ROWS = 48
F32 = jnp.float32
BF16 = jnp.bfloat16


def lane_ids(rows):
    return lax.broadcasted_iota(jnp.int32, (rows, 128), 1)


def roll(value, shift):
    return pltpu.roll(value, shift % 128, 1) if shift % 128 else value


def exchange_bit(low, high, bit):
    step = 4 << bit
    chosen = (lane_ids(low.shape[0]) & step) != 0
    return jnp.where(chosen, roll(high, step), low), jnp.where(chosen, high, roll(low, -step))


def exchange_twice(sets):
    for bit in range(2):
        for planes in sets:
            for low in range(4):
                if not low >> bit & 1:
                    high = low | 1 << bit
                    planes[low], planes[high] = exchange_bit(planes[low], planes[high], bit)
    out = []
    for planes in sets:
        pairs = [exchange_bit(plane, plane, 2) for plane in planes]
        out.append([pair[0] for pair in pairs] + [pair[1] for pair in pairs])
    return out


def exchange(sets):
    for bit in range(3):
        for planes in sets:
            for low in range(8):
                if not low >> bit & 1:
                    high = low | 1 << bit
                    planes[low], planes[high] = exchange_bit(planes[low], planes[high], bit)
    return sets


def colour(link, vector):
    out = []
    for c in range(3):
        real = imag = None
        for d in range(3):
            lr, li = link[(c * 3 + d) * 2], link[(c * 3 + d) * 2 + 1]
            vr, vi = vector[d * 2], vector[d * 2 + 1]
            re, im = lr * vr - li * vi, lr * vi + li * vr
            real = re if real is None else real + re
            imag = im if imag is None else imag + im
        out.append((real, imag))
    return out


def nt(a, b):
    return lax.dot_general(a, b, (((1,), (1,)), ((), ())), preferred_element_type=F32)


def inner_kernel(
    v_ref, u_hbm, own_ref, out_ref, lt_ref, lz_ref, ut_ref, uz_ref, vm, uf, cm, flat, sites, kept, u_ref, sem
):
    fetch = pltpu.make_async_copy(u_hbm, u_ref, sem)
    fetch.start()

    @pl.loop(0, 6)
    def _(step):
        chi, c = step // 3, step % 3
        for sb in range(2):
            parts = [v_ref[ri, :, 2 * chi + sb, c] for ri in range(2)]
            sites[sb] = jnp.swapaxes(jnp.concatenate(parts, 0), 0, 1)

        def load(t, plane):
            sb, q = plane // 4, plane % 4
            first = q * 4 + 3 if t == 4 else t * 4 + q
            return sites[sb, first]

        second = (lane_ids(ROWS) & 16) != 0
        for group in ((0,), (1, 2), (3, 4)):
            if group == (0,):
                rows = [pl.ds(pl.multiple_of((a * 2 + chi) * ROWS, ROWS), ROWS) for a in range(8)]
                column = pl.ds(pl.multiple_of(c * 128, 128), 128)
                done = [[own_ref[part, column] for part in rows]]
            else:
                done = exchange([[load(t, plane) for plane in range(8)] for t in group])
            turned = [[jnp.where(second, -value, value) for value in values] for values in done]
            swapped = [
                [jnp.where(second, roll(value, 16), roll(value, -16)) for value in values]
                for t, values in zip(group, done)
                if t < 4
            ]
            for k, t in enumerate(group):
                for a in range(8):
                    if t == 4:
                        column = pl.multiple_of(c * 128, 128)
                        lz_ref[0, a, chi, :, pl.ds(column, 128)] = done[k][a]
                        lz_ref[1, a, chi, :, pl.ds(column, 128)] = turned[k][a]
                        continue
                    column = pl.multiple_of((t * 3 + c) * 128, 128)
                    vm[0, a, chi, :, pl.ds(column, 128)] = done[k][a]
                    vm[1, a, chi, :, pl.ds(column, 128)] = turned[k][a]
                    value = swapped[k][a]
                    vm[2, a, chi, :, pl.ds(column, 128)] = value
                    vm[3, a, chi, :, pl.ds(column, 128)] = jnp.where(second, value, -value)

    for a in range(8):
        for chi in range(2):
            lt_ref[a, chi] = vm[0, a, chi, :, 9 * 128 :]

    fetch.wait()

    @pl.loop(0, 4)
    def _(mu):
        parts = [u_ref[ri, mu, c, d] for c in range(3) for d in range(3) for ri in range(2)]
        parts += [jnp.zeros((16, 128), BF16)] * 6
        flat[...] = 0.5 * jnp.swapaxes(jnp.stack(parts).astype(F32), 0, 1)
        drop = ((lane_ids(24) & 12) == 12) & (mu == 1)
        sets = [[flat[t * 4 + z] for z in range(4)] for t in range(4)]
        for group in ((0, 1), (2, 3)):
            done = exchange_twice([sets[t] for t in group])
            for t, values in zip(group, done):
                for a, value in enumerate(values):
                    uf[a, mu, t] = jnp.where(drop, 0.0, value)

        @pl.when(mu == 1)
        def _():
            last = [flat[t * 4 + 3] for t in range(4)]
            for a, value in enumerate(exchange_twice([last])[0]):
                uz_ref[a] = value

    for a in range(8):
        ut_ref[a] = uf[a, 0, 3]

    def fill(a, chi, times=range(4)):
        ahead = lax.rem(a + 1, 8)
        x_last = jnp.where((lane_ids(NV) & 3) == 3, -1.0, 0.0).astype(F32)
        x_last_pair = (lane_ids(ROWS) & 3) == 3
        y_last = jnp.where(lane_ids(NV) >= 96, -1.0, 0.0).astype(F32)

        def hop(t, mu):
            link = [uf[a, mu, t, pl.ds(k, 1), :] for k in range(18)]
            vector = []
            for d in range(3):
                first = (((t + 1) if mu == 0 else t) * 3 + d) * 128
                value = vm[0, a, chi, :, first : first + 128]
                if mu == 1:
                    value = roll(value, -4)
                elif mu == 2:
                    value = roll(value, -32)
                elif mu == 3:
                    other = vm[0, ahead, chi, :, first : first + 128]
                    value = jnp.where(x_last_pair, roll(other, 3), roll(value, -1))
                value = value.astype(F32)
                vector += [value[:NV], value[NV:]]
            return colour(link, vector)

        nothing = [(jnp.zeros((NV, 128), F32),) * 2] * 3
        for t in times:
            for slot in range(3):
                if slot == 0:
                    one, two = hop(t, 0) if t < 3 else nothing, hop(t, 1)
                else:
                    last = y_last if slot == 1 else x_last
                    one = hop(t, slot + 1)
                    two = [[part * last for part in pair] for pair in one]
                for c in range(3):
                    column = slice((t * 3 + c) * 128, (t * 3 + c + 1) * 128)
                    for ri in range(2):
                        both = jnp.concatenate([one[c][ri], two[c][ri]], 0).astype(BF16)
                        cm[chi, slot, ri * ROWS : ri * ROWS + ROWS, column] = both

    def multiply(a, chi, beside=None):
        near, far = vm[0, a, chi], vm[0, a, 1 - chi]
        lefts = (
            lambda: jnp.concatenate([near, far, vm[1, a, 1 - chi]], 0),
            lambda: jnp.concatenate([near, vm[3, a, 1 - chi]], 0),
            lambda: jnp.concatenate([near, vm[2, a, 1 - chi]], 0),
            lambda: near,
        )
        blocks = []
        for k, left in enumerate(lefts):
            blocks.append(nt(left(), cm[chi, k] if k < 3 else near))
            if beside is not None:
                beside(k)
        return blocks

    def keep(blocks):
        for value, (start, rows) in zip(blocks, ((0, 144), (144, 96), (240, 96), (336, 48))):
            kept[start : start + rows, : value.shape[1]] = value

    def finish(a, beside=None):
        second = multiply(a, 1, beside)
        first = (kept[0:144, :96], kept[144:240, :96], kept[240:336, :96], kept[336:384, :ROWS])
        combine_inner([first, second], a, out_ref)

    fill(0, 0)
    keep(multiply(0, 0))
    fill(0, 1)

    @pl.loop(1, 8)
    def _(a):
        finish(a - 1, lambda k: fill(a, 0, (k,)))
        keep(multiply(a, 0, lambda k: fill(a, 1, (k,))))

    finish(7)


def widened(value):
    return jnp.concatenate([value, jnp.zeros((value.shape[0], 128 - value.shape[1]), F32)], 1)


def other_side(value, half):
    return jnp.where(lane_ids(value.shape[0]) < half, roll(value, -half), roll(value, half))


def sides(half):
    return jnp.where(lane_ids(NV) < half, 1.0, -1.0).astype(F32)


def complex_of(product, half):
    return product[:NV] + sides(half) * other_side(product[NV:], half)


def complex_i(product, half):
    return product[NV:] - sides(half) * other_side(product[:NV], half)


def combine_inner(blocks, a, out_ref):
    lanes = lane_ids(NV)
    second = ((lanes >= 24) & (lanes < 48)) | (lanes >= 72)
    upper, grams = {}, [[None, None], [None, None]]
    zero = jnp.zeros((NV, 128), F32)
    for chi, products in enumerate(blocks):
        tz, y, x, gram = (widened(value) for value in products)
        phase = 1.0 if chi == 0 else -1.0
        z_tz, z_y, z_x = (complex_of(value[:ROWS], 48) for value in (tz, y, x))
        cross_t = complex_of(tz[48:96], 48)
        cross_z = phase * complex_i(tz[96:144], 48)
        cross_y = phase * complex_of(y[48:96], 48)
        cross_x = phase * complex_i(x[48:96], 48)
        upper[chi, chi] = -(z_tz + z_y + z_x), z_y, z_x
        cross = jnp.where(second, cross_z, cross_t) + cross_y + cross_x
        upper[1 - chi, chi] = cross, -cross_y, -cross_x
        grams[chi][chi] = complex_of(gram, NV)
        grams[chi][1 - chi] = zero

    def whole(item, starts):
        return placed([[upper[row, col][item] for col in range(2)] for row in range(2)], *starts)

    first_rows = lax.broadcasted_iota(jnp.int32, (ROWS, 128), 0) < NV
    cols = lane_ids(ROWS)
    flip = jnp.where(first_rows == (cols < NV), 1.0, -1.0).astype(F32)
    for ri in range(2):
        first, behind = 48 * ri, 48 * ri + NV
        out_ref[a, 1, ri] = whole(1, (behind,))
        out_ref[a, 2, ri] = whole(2, (behind,))
        inner = whole(0, (first, behind))
        turned = jnp.concatenate([inner, jnp.zeros((80, 128), F32)], 0).T[:ROWS]
        turned = flip * turned if ri == 0 else -flip * turned
        out_ref[a, 0, ri] = placed(grams, NV * ri) + inner + turned


def placed(parts, *starts):
    lanes = lane_ids(NV)
    left, right = lanes < NV, (lanes >= NV) & (lanes < 2 * NV)
    rows = []
    for row in range(2):
        ahead = sum(roll(parts[row][1], NV - start) for start in starts)
        here = sum(roll(parts[row][0], -start) for start in starts)
        rows.append(jnp.where(left, here, jnp.where(right, ahead, 0.0)))
    return jnp.concatenate(rows, 0)


def inner_call(vectors, links, own):
    shape = jax.ShapeDtypeStruct
    vmem = pl.BlockSpec(memory_space=pltpu.VMEM)
    return pl.pallas_call(
        inner_kernel,
        out_shape=(
            shape((8, 3, 2, ROWS, 128), F32),
            shape((8, 2, ROWS, 384), BF16),
            shape((2, 8, 2, ROWS, 384), BF16),
            shape((8, 24, 128), F32),
            shape((8, 24, 128), F32),
        ),
        in_specs=[vmem, pl.BlockSpec(memory_space=pltpu.HBM), vmem],
        out_specs=(vmem,) * 5,
        scratch_shapes=[
            pltpu.VMEM((4, 8, 2, ROWS, 1536), BF16),
            pltpu.VMEM((8, 4, 4, 24, 128), F32),
            pltpu.VMEM((2, 3, 96, 1536), BF16),
            pltpu.VMEM((16, 24, 128), F32),
            pltpu.VMEM((2, 16, ROWS, 128), BF16),
            pltpu.VMEM((384, 128), F32),
            pltpu.VMEM((2, 4, 3, 3, 16, 128), BF16),
            pltpu.SemaphoreType.DMA,
        ],
        compiler_params=pltpu.CompilerParams(vmem_limit_bytes=24 * 1024 * 1024),
        cost_estimate=pl.CostEstimate(
            flops=40_000_000_000, bytes_accessed=6_000_000, transcendentals=0
        ),
        name="inner",
    )(vectors, pltpu.with_memory_space_constraint(links, pltpu.HBM), own)


def face_kernel(v_hbm, phi_hbm, t_ref, z_ref, vec_ref, flat, v_ref, phi_ref, sem):
    def fetch(chi, c, k):
        part = (slice(None), slice(None), pl.ds(2 * chi, 2), c)
        return pltpu.make_async_copy(v_hbm.at[part], v_ref.at[part], sem.at[k])

    for k in range(6):
        fetch(k // 3, k % 3, k).start()
    small = pltpu.make_async_copy(phi_hbm, phi_ref, sem.at[6])
    small.start()

    @pl.loop(0, 6)
    def _(step):
        chi, c = step // 3, step % 3
        fetch(chi, c, step).wait()
        for sb in range(2):
            for ri in range(2):
                block = v_ref[ri, :, 2 * chi + sb, c].astype(F32)
                flat[sb, pl.ds(ri * 384, 384), :] = block.reshape(384, 128)
        column = pl.multiple_of(c * 128, 128)

        def load(k, plane):
            return flat[plane // 4, pl.ds(plane % 4 * (1, 4)[k], ROWS, stride=16), :].astype(BF16)

        done = exchange([[load(k, plane) for plane in range(8)] for k in range(2)])
        for out, values in zip((t_ref, z_ref), done):
            for a, value in enumerate(values):
                rows = pl.ds(pl.multiple_of((a * 2 + chi) * ROWS, ROWS), ROWS)
                out[rows, pl.ds(column, 128)] = value

    small.wait()
    vec = jnp.concatenate([phi_ref[...], jnp.zeros((8, 32), F32)], 1)
    vec_ref[...] = vec
    pieces = []
    for _ in range(3):
        piece = vec.astype(BF16)
        vec = vec - piece.astype(F32)
        pieces.append(piece.astype(F32))
    rider = jnp.concatenate(pieces, 1)
    rider = jnp.concatenate([rider, jnp.zeros((8, 384), F32)], 0).astype(BF16)
    for ref in (t_ref, z_ref):
        ref[768:784, :] = rider


def ridden(face):
    return sum(face[768:784, 128 * k : 128 * k + 128].astype(F32)[:8] for k in range(3))


def face_call(vectors, phi):
    face = jax.ShapeDtypeStruct((784, 384), BF16)
    vmem = pl.BlockSpec(memory_space=pltpu.VMEM)
    return pl.pallas_call(
        face_kernel,
        out_shape=(face, face, jax.ShapeDtypeStruct((8, 128), F32)),
        in_specs=[pl.BlockSpec(memory_space=pltpu.HBM)] * 2,
        out_specs=(vmem,) * 3,
        scratch_shapes=[
            pltpu.VMEM((2, 768, 128), F32),
            pltpu.VMEM((2, NV, 4, 3, 16, 128), BF16),
            pltpu.VMEM((8, 2 * ROWS), F32),
            pltpu.SemaphoreType.DMA((7,)),
        ],
        compiler_params=pltpu.CompilerParams(vmem_limit_bytes=12 * 1024 * 1024),
        name="faces",
    )(*(pltpu.with_memory_space_constraint(x, pltpu.HBM) for x in (vectors, phi)))


def outer_kernel(mu, face, *refs):
    lefts, (links, vec_ref, out_ref, back_ref, cm) = refs[:-5], refs[-5:]

    for a in range(8):
        for chi in range(2):
            link = [links[a, pl.ds(k, 1), :] for k in range(18)]
            vector = []
            rows = pl.ds((a * 2 + chi) * ROWS, ROWS)
            for d in range(3):
                value = face[rows, d * 128 : (d + 1) * 128].astype(F32)
                vector += [value[:NV], value[NV:]]
            for c, both in enumerate(colour(link, vector)):
                cm[a, chi, :, c * 128 : (c + 1) * 128] = jnp.concatenate(both, 0).astype(BF16)

    eye = eye_mask()
    row_sign, col_sign = signs()
    for a in range(8):
        parts = [[None, None], [None, None]]
        for chi in range(2):
            if mu == 0:
                near, far = lefts[0][a, chi], lefts[0][a, 1 - chi]
            else:
                near, far = lefts[0][0, a, chi], lefts[0][1, a, 1 - chi]
            product = widened(nt(jnp.concatenate([near, far], 0), cm[a, chi]))
            if mu == 0:
                cross = complex_of(product[ROWS:], NV)
            else:
                cross = (1.0 if chi == 0 else -1.0) * complex_i(product[ROWS:], NV)
            parts[chi][chi] = -complex_of(product[:ROWS], NV)
            parts[1 - chi][chi] = cross
        pr, pi = split(vec_ref[pl.ds(a, 1), :])
        column_r = row_sign * column_of(pr, eye)
        column_i = row_sign * column_of(pi, eye)
        block = placed(parts, 0), placed(parts, NV)
        out_ref[a, 0] = block[0]
        out_ref[a, 1] = block[1]
        back_ref[pl.ds(a, 1), :] = backward(block, column_r, column_i, col_sign)


def outer_call(mu, name, *args):
    vmem = pl.BlockSpec(memory_space=pltpu.VMEM)
    shape = jax.ShapeDtypeStruct
    return pl.pallas_call(
        functools.partial(outer_kernel, mu),
        out_shape=(shape((8, 2, ROWS, 128), F32), shape((8, 128), F32)),
        in_specs=[vmem] * len(args),
        out_specs=(vmem,) * 2,
        scratch_shapes=[pltpu.VMEM((8, 2, ROWS, 384), BF16)],
        compiler_params=pltpu.CompilerParams(vmem_limit_bytes=12 * 1024 * 1024),
        name=name,
    )(*args)


def signs():
    rows = lax.broadcasted_iota(jnp.int32, (ROWS, 128), 0)
    return jnp.where(rows < NV, 1.0, -1.0).astype(F32), jnp.where(lane_ids(1) < NV, 1.0, -1.0).astype(F32)


def split(row):
    keep = lane_ids(1) < ROWS
    return jnp.where(keep, row, 0.0), jnp.where(keep, roll(row, -ROWS), 0.0)


def joined(real, imag):
    lanes = lane_ids(1)
    low, high = lanes < ROWS, (lanes >= ROWS) & (lanes < 2 * ROWS)
    return jnp.where(low, real, jnp.where(high, roll(imag, ROWS), 0.0))


def forward(block, row):
    pr, pi = split(row)
    br, bi = block
    return br * pr - bi * pi, br * pi + bi * pr


def column_of(row, eye):
    return jnp.sum(jnp.where(eye, row, 0.0), axis=1, keepdims=True)


def row_of(column, eye):
    return jnp.sum(jnp.where(eye, column, 0.0), axis=0, keepdims=True)


def backward(block, column_r, column_i, col_sign):
    br, bi = block
    real = jnp.sum(br * column_r + bi * column_i, axis=0, keepdims=True)
    imag = jnp.sum(br * column_i - bi * column_r, axis=0, keepdims=True)
    return joined(col_sign * real, col_sign * imag)


def eye_mask():
    rows = lax.broadcasted_iota(jnp.int32, (ROWS, 128), 0)
    return rows == lane_ids(ROWS)


def local_apply(inner, vec, part_ref):
    eye = eye_mask()
    row_sign, col_sign = signs()
    own, kept = [], []
    for a in range(8):
        here, ahead = vec[pl.ds(a, 1), :], vec[pl.ds((a + 1) % 8, 1), :]
        diag, y, x = ((inner[a, k, 0], inner[a, k, 1]) for k in range(3))
        f0, f1, f2 = forward(diag, here), forward(y, here), forward(x, ahead)
        real = jnp.sum(f0[0] + f1[0] + f2[0], axis=1, keepdims=True)
        imag = jnp.sum(f0[1] + f1[1] + f2[1], axis=1, keepdims=True)
        pr, pi = split(here)
        column_r = row_sign * column_of(pr, eye)
        column_i = row_sign * column_of(pi, eye)
        back_y = backward(y, column_r, column_i, col_sign)
        own.append(joined(row_of(real, eye), row_of(imag, eye)) + back_y)
        kept.append(backward(x, column_r, column_i, col_sign))
    for a in range(8):
        part_ref[pl.ds(a, 1), :] = own[a] + kept[(a + 7) % 8]


def ahead_apply(outer_t, outer_z, vt, vz):
    eye = eye_mask()
    rows = []
    for a in range(8):
        ft = forward((outer_t[a, 0], outer_t[a, 1]), vt[a : a + 1])
        fz = forward((outer_z[a, 0], outer_z[a, 1]), vz[a : a + 1])
        real = jnp.sum(ft[0] + fz[0], axis=1, keepdims=True)
        imag = jnp.sum(ft[1] + fz[1], axis=1, keepdims=True)
        rows.append(joined(row_of(real, eye), row_of(imag, eye)))
    return jnp.concatenate(rows, 0)


def first_kernel(inner, outer_t, outer_z, vec, ft, fz, part_ref):
    local_apply(inner, vec, part_ref)
    part_ref[...] += ahead_apply(outer_t, outer_z, ridden(ft), ridden(fz))


def back_kernel(outer_t, outer_z, part, rt, rz, vec_ref, bt_ref, bz_ref):
    vec_ref[...] = part[...] + rt[...] + rz[...]
    eye = eye_mask()
    row_sign, col_sign = signs()
    for a in range(8):
        pr, pi = split(vec_ref[pl.ds(a, 1), :])
        column_r = row_sign * column_of(pr, eye)
        column_i = row_sign * column_of(pi, eye)
        for outer, back in ((outer_t, bt_ref), (outer_z, bz_ref)):
            block = outer[a, 0], outer[a, 1]
            back[pl.ds(a, 1), :] = backward(block, column_r, column_i, col_sign)


def last_kernel(outer_t, outer_z, part, rt, rz, vt, vz, out_ref):
    total = part[...] + rt[...] + rz[...] + ahead_apply(outer_t, outer_z, vt[...], vz[...])
    out_ref[...] = total[:, : 2 * ROWS]


def blocks_kernel(inner, outer_t, outer_z, out_ref):
    sources = (inner.at[:, 0], outer_t, outer_z, inner.at[:, 1], inner.at[:, 2])
    for slot, ref in enumerate(sources):
        for ri in range(2):
            for group in range(ROWS // 8):
                pieces = []
                for row in range(group * 8, group * 8 + 8):
                    pieces.append(jnp.concatenate([ref[a, ri, row : row + 1, :] for a in range(8)], 0))
                wide = lane_rows(pieces)
                first = ri * ROWS * ROWS + group * 8 * ROWS
                out_ref[slot, :, first : first + 8 * ROWS] = wide


def lane_rows(pieces):
    tiles = []
    for tile in range(3):
        total = None
        for k, piece in enumerate(pieces):
            shift = k * ROWS - tile * 128
            if -ROWS < shift < 128:
                moved = piece if shift == 0 else roll(piece, shift)
                if shift < 0:
                    moved = jnp.where(lane_ids(8) < ROWS + shift, moved, 0.0)
                elif shift + ROWS > 128:
                    moved = jnp.where(lane_ids(8) >= shift, moved, 0.0)
                total = moved if total is None else total + moved
        tiles.append(total)
    return jnp.concatenate(tiles, 1)


def small_call(kernel, count, name, *args, width=128):
    vmem = pl.BlockSpec(memory_space=pltpu.VMEM)
    row = jax.ShapeDtypeStruct((8, width), F32)
    return pl.pallas_call(
        kernel,
        out_shape=(row,) * count,
        in_specs=[vmem] * len(args),
        out_specs=(vmem,) * count,
        compiler_params=pltpu.CompilerParams(vmem_limit_bytes=12 * 1024 * 1024),
        name=name,
    )(*args)


def blocks_call(inner, outer_t, outer_z):
    vmem = pl.BlockSpec(memory_space=pltpu.VMEM)
    return pl.pallas_call(
        blocks_kernel,
        out_shape=jax.ShapeDtypeStruct((5, 8, 2 * ROWS * ROWS), F32),
        in_specs=[vmem] * 3,
        out_specs=vmem,
        compiler_params=pltpu.CompilerParams(vmem_limit_bytes=12 * 1024 * 1024),
        cost_estimate=pl.CostEstimate(flops=0, bytes_accessed=6_000_000, transcendentals=0),
        name="blocks",
    )(inner, outer_t, outer_z)


def shifted(value, axis, steps):
    count = lax.axis_size(axis)
    return lax.ppermute(value, axis, [(k, (k + steps) % count) for k in range(count)])


def per_device(null_vectors, gauge_links, coarse_in):
    vectors = null_vectors.reshape(2, NV, 4, 3, 16, 128)
    links = gauge_links.reshape(2, 4, 3, 3, 16, 128)
    face_t, face_z, vec = face_call(vectors, coarse_in.reshape(8, 2 * ROWS))
    own_t = face_t
    face_t, face_z = shifted(face_t, "ta", -1), shifted(face_z, "sa", -1)
    inner, left_t, left_z, link_t, link_z = inner_call(vectors, links, own_t)
    outer_t, bt = outer_call(0, "outer_t", face_t, left_t, link_t, vec)
    outer_z, bz = outer_call(1, "outer_z", face_z, left_z, link_z, vec)
    rt, rz = shifted(bt, "ta", 1), shifted(bz, "sa", 1)
    (part,) = small_call(first_kernel, 1, "first", inner, outer_t, outer_z, vec, face_t, face_z)
    once, bt, bz = small_call(back_kernel, 3, "back", outer_t, outer_z, part, rt, rz)
    vec_t, rt = shifted(once, "ta", -1), shifted(bt, "ta", 1)
    vec_z, rz = shifted(once, "sa", -1), shifted(bz, "sa", 1)
    (part,) = small_call(local_apply, 1, "local", inner, once)
    blocks = blocks_call(inner, outer_t, outer_z)
    (twice,) = small_call(last_kernel, 1, "last", outer_t, outer_z, part, rt, rz, vec_t, vec_z, width=2 * ROWS)
    blocks = jnp.swapaxes(blocks, 0, 1)
    return blocks.reshape(1, 1, 8, 5, 2 * ROWS * ROWS), twice.reshape(1, 1, 8, 2 * ROWS)


def solution(mesh):
    placed_sites = P(None, None, None, None, "ta", "sa", None)
    return jax.shard_map(
        per_device,
        mesh=mesh,
        in_specs=(placed_sites, placed_sites, P("ta", "sa", None, None)),
        out_specs=(P("ta", "sa", None, None, None), P("ta", "sa", None, None)),
        check_vma=False,
    )
```

```python
import functools

import jax
import jax.numpy as jnp
from jax import lax
from jax.experimental import pallas as pl
from jax.experimental.pallas import tpu as pltpu
from jax.sharding import PartitionSpec as P

NV = 24
ROWS = 48
F32 = jnp.float32
BF16 = jnp.bfloat16


def lane_ids(rows):
    return lax.broadcasted_iota(jnp.int32, (rows, 128), 1)


def roll(value, shift):
    return pltpu.roll(value, shift % 128, 1) if shift % 128 else value


def exchange_bit(low, high, bit):
    step = 4 << bit
    chosen = (lane_ids(low.shape[0]) & step) != 0
    return jnp.where(chosen, roll(high, step), low), jnp.where(chosen, high, roll(low, -step))


def exchange_twice(sets):
    for bit in range(2):
        for planes in sets:
            for low in range(4):
                if not low >> bit & 1:
                    high = low | 1 << bit
                    planes[low], planes[high] = exchange_bit(planes[low], planes[high], bit)
    out = []
    for planes in sets:
        pairs = [exchange_bit(plane, plane, 2) for plane in planes]
        out.append([pair[0] for pair in pairs] + [pair[1] for pair in pairs])
    return out


def exchange(sets):
    for bit in range(3):
        for planes in sets:
            for low in range(8):
                if not low >> bit & 1:
                    high = low | 1 << bit
                    planes[low], planes[high] = exchange_bit(planes[low], planes[high], bit)
    return sets


def colour(link, vector):
    out = []
    for c in range(3):
        real = imag = None
        for d in range(3):
            lr, li = link[(c * 3 + d) * 2], link[(c * 3 + d) * 2 + 1]
            vr, vi = vector[d * 2], vector[d * 2 + 1]
            re, im = lr * vr - li * vi, lr * vi + li * vr
            real = re if real is None else real + re
            imag = im if imag is None else imag + im
        out.append((real, imag))
    return out


def nt(a, b):
    return lax.dot_general(a, b, (((1,), (1,)), ((), ())), preferred_element_type=F32)


def inner_kernel(
    v_ref, u_hbm, own_ref, out_ref, lt_ref, lz_ref, ut_ref, uz_ref, vm, uf, cm, flat, sites, kept, u_ref, sem
):
    fetch = pltpu.make_async_copy(u_hbm, u_ref, sem)
    fetch.start()

    @pl.loop(0, 6)
    def _(step):
        chi, c = step // 3, step % 3
        for sb in range(2):
            parts = [v_ref[ri, :, 2 * chi + sb, c] for ri in range(2)]
            sites[sb] = jnp.swapaxes(jnp.concatenate(parts, 0), 0, 1)

        def load(t, plane):
            sb, q = plane // 4, plane % 4
            first = q * 4 + 3 if t == 4 else t * 4 + q
            return sites[sb, first]

        second = (lane_ids(ROWS) & 16) != 0
        for group in ((0,), (1, 2), (3, 4)):
            if group == (0,):
                rows = [pl.ds(pl.multiple_of((a * 2 + chi) * ROWS, ROWS), ROWS) for a in range(8)]
                column = pl.ds(pl.multiple_of(c * 128, 128), 128)
                done = [[own_ref[part, column] for part in rows]]
            else:
                done = exchange([[load(t, plane) for plane in range(8)] for t in group])
            turned = [[jnp.where(second, -value, value) for value in values] for values in done]
            swapped = [
                [jnp.where(second, roll(value, 16), roll(value, -16)) for value in values]
                for t, values in zip(group, done)
                if t < 4
            ]
            for k, t in enumerate(group):
                for a in range(8):
                    if t == 4:
                        column = pl.multiple_of(c * 128, 128)
                        lz_ref[0, a, chi, :, pl.ds(column, 128)] = done[k][a]
                        lz_ref[1, a, chi, :, pl.ds(column, 128)] = turned[k][a]
                        continue
                    column = pl.multiple_of((t * 3 + c) * 128, 128)
                    vm[0, a, chi, :, pl.ds(column, 128)] = done[k][a]
                    vm[1, a, chi, :, pl.ds(column, 128)] = turned[k][a]
                    value = swapped[k][a]
                    vm[2, a, chi, :, pl.ds(column, 128)] = value
                    vm[3, a, chi, :, pl.ds(column, 128)] = jnp.where(second, value, -value)

    for a in range(8):
        for chi in range(2):
            lt_ref[a, chi] = vm[0, a, chi, :, 9 * 128 :]

    fetch.wait()

    @pl.loop(0, 4)
    def _(mu):
        parts = [u_ref[ri, mu, c, d] for c in range(3) for d in range(3) for ri in range(2)]
        parts += [jnp.zeros((16, 128), BF16)] * 6
        flat[...] = 0.5 * jnp.swapaxes(jnp.stack(parts).astype(F32), 0, 1)
        drop = ((lane_ids(24) & 12) == 12) & (mu == 1)
        sets = [[flat[t * 4 + z] for z in range(4)] for t in range(4)]
        for group in ((0, 1), (2, 3)):
            done = exchange_twice([sets[t] for t in group])
            for t, values in zip(group, done):
                for a, value in enumerate(values):
                    uf[a, mu, t] = jnp.where(drop, 0.0, value)

        @pl.when(mu == 1)
        def _():
            last = [flat[t * 4 + 3] for t in range(4)]
            for a, value in enumerate(exchange_twice([last])[0]):
                uz_ref[a] = value

    for a in range(8):
        ut_ref[a] = uf[a, 0, 3]

    def fill(a, chi, times=range(4)):
        ahead = lax.rem(a + 1, 8)
        x_last = jnp.where((lane_ids(NV) & 3) == 3, -1.0, 0.0).astype(F32)
        x_last_pair = (lane_ids(ROWS) & 3) == 3
        y_last = jnp.where(lane_ids(NV) >= 96, -1.0, 0.0).astype(F32)

        def hop(t, mu):
            link = [uf[a, mu, t, pl.ds(k, 1), :] for k in range(18)]
            vector = []
            for d in range(3):
                first = (((t + 1) if mu == 0 else t) * 3 + d) * 128
                value = vm[0, a, chi, :, first : first + 128]
                if mu == 1:
                    value = roll(value, -4)
                elif mu == 2:
                    value = roll(value, -32)
                elif mu == 3:
                    other = vm[0, ahead, chi, :, first : first + 128]
                    value = jnp.where(x_last_pair, roll(other, 3), roll(value, -1))
                value = value.astype(F32)
                vector += [value[:NV], value[NV:]]
            return colour(link, vector)

        nothing = [(jnp.zeros((NV, 128), F32),) * 2] * 3
        for t in times:
            for slot in range(3):
                if slot == 0:
                    one, two = hop(t, 0) if t < 3 else nothing, hop(t, 1)
                else:
                    last = y_last if slot == 1 else x_last
                    one = hop(t, slot + 1)
                    two = [[part * last for part in pair] for pair in one]
                for c in range(3):
                    column = slice((t * 3 + c) * 128, (t * 3 + c + 1) * 128)
                    for ri in range(2):
                        both = jnp.concatenate([one[c][ri], two[c][ri]], 0).astype(BF16)
                        cm[chi, slot, ri * ROWS : ri * ROWS + ROWS, column] = both

    def multiply(a, chi, beside=None):
        near, far = vm[0, a, chi], vm[0, a, 1 - chi]
        lefts = (
            lambda: jnp.concatenate([near, far, vm[1, a, 1 - chi]], 0),
            lambda: jnp.concatenate([near, vm[3, a, 1 - chi]], 0),
            lambda: jnp.concatenate([near, vm[2, a, 1 - chi]], 0),
            lambda: near,
        )
        blocks = []
        for k, left in enumerate(lefts):
            blocks.append(nt(left(), cm[chi, k] if k < 3 else near))
            if beside is not None:
                beside(k)
        return blocks

    def keep(blocks):
        for value, (start, rows) in zip(blocks, ((0, 144), (144, 96), (240, 96), (336, 48))):
            kept[start : start + rows, : value.shape[1]] = value

    def finish(a, beside=None):
        second = multiply(a, 1, beside)
        first = (kept[0:144, :96], kept[144:240, :96], kept[240:336, :96], kept[336:384, :ROWS])
        combine_inner([first, second], a, out_ref)

    fill(0, 0)
    keep(multiply(0, 0))
    fill(0, 1)

    @pl.loop(1, 8)
    def _(a):
        finish(a - 1, lambda k: fill(a, 0, (k,)))
        keep(multiply(a, 0, lambda k: fill(a, 1, (k,))))

    finish(7)


def widened(value):
    return jnp.concatenate([value, jnp.zeros((value.shape[0], 128 - value.shape[1]), F32)], 1)


def other_side(value, half):
    return jnp.where(lane_ids(value.shape[0]) < half, roll(value, -half), roll(value, half))


def sides(half):
    return jnp.where(lane_ids(NV) < half, 1.0, -1.0).astype(F32)


def complex_of(product, half):
    return product[:NV] + sides(half) * other_side(product[NV:], half)


def complex_i(product, half):
    return product[NV:] - sides(half) * other_side(product[:NV], half)


def combine_inner(blocks, a, out_ref):
    lanes = lane_ids(NV)
    second = ((lanes >= 24) & (lanes < 48)) | (lanes >= 72)
    upper, grams = {}, [[None, None], [None, None]]
    zero = jnp.zeros((NV, 128), F32)
    for chi, products in enumerate(blocks):
        tz, y, x, gram = (widened(value) for value in products)
        phase = 1.0 if chi == 0 else -1.0
        z_tz, z_y, z_x = (complex_of(value[:ROWS], 48) for value in (tz, y, x))
        cross_t = complex_of(tz[48:96], 48)
        cross_z = phase * complex_i(tz[96:144], 48)
        cross_y = phase * complex_of(y[48:96], 48)
        cross_x = phase * complex_i(x[48:96], 48)
        upper[chi, chi] = -(z_tz + z_y + z_x), z_y, z_x
        cross = jnp.where(second, cross_z, cross_t) + cross_y + cross_x
        upper[1 - chi, chi] = cross, -cross_y, -cross_x
        grams[chi][chi] = complex_of(gram, NV)
        grams[chi][1 - chi] = zero

    def whole(item, starts):
        return placed([[upper[row, col][item] for col in range(2)] for row in range(2)], *starts)

    first_rows = lax.broadcasted_iota(jnp.int32, (ROWS, 128), 0) < NV
    cols = lane_ids(ROWS)
    flip = jnp.where(first_rows == (cols < NV), 1.0, -1.0).astype(F32)
    for ri in range(2):
        first, behind = 48 * ri, 48 * ri + NV
        out_ref[a, 1, ri] = whole(1, (behind,))
        out_ref[a, 2, ri] = whole(2, (behind,))
        inner = whole(0, (first, behind))
        turned = jnp.concatenate([inner, jnp.zeros((80, 128), F32)], 0).T[:ROWS]
        turned = flip * turned if ri == 0 else -flip * turned
        out_ref[a, 0, ri] = placed(grams, NV * ri) + inner + turned


def placed(parts, *starts):
    lanes = lane_ids(NV)
    left, right = lanes < NV, (lanes >= NV) & (lanes < 2 * NV)
    rows = []
    for row in range(2):
        ahead = sum(roll(parts[row][1], NV - start) for start in starts)
        here = sum(roll(parts[row][0], -start) for start in starts)
        rows.append(jnp.where(left, here, jnp.where(right, ahead, 0.0)))
    return jnp.concatenate(rows, 0)


def inner_call(vectors, links, own):
    shape = jax.ShapeDtypeStruct
    vmem = pl.BlockSpec(memory_space=pltpu.VMEM)
    return pl.pallas_call(
        inner_kernel,
        out_shape=(
            shape((8, 3, 2, ROWS, 128), F32),
            shape((8, 2, ROWS, 384), BF16),
            shape((2, 8, 2, ROWS, 384), BF16),
            shape((8, 24, 128), F32),
            shape((8, 24, 128), F32),
        ),
        in_specs=[vmem, pl.BlockSpec(memory_space=pltpu.HBM), vmem],
        out_specs=(vmem,) * 5,
        scratch_shapes=[
            pltpu.VMEM((4, 8, 2, ROWS, 1536), BF16),
            pltpu.VMEM((8, 4, 4, 24, 128), F32),
            pltpu.VMEM((2, 3, 96, 1536), BF16),
            pltpu.VMEM((16, 24, 128), F32),
            pltpu.VMEM((2, 16, ROWS, 128), BF16),
            pltpu.VMEM((384, 128), F32),
            pltpu.VMEM((2, 4, 3, 3, 16, 128), BF16),
            pltpu.SemaphoreType.DMA,
        ],
        compiler_params=pltpu.CompilerParams(vmem_limit_bytes=24 * 1024 * 1024),
        cost_estimate=pl.CostEstimate(
            flops=40_000_000_000, bytes_accessed=6_000_000, transcendentals=0
        ),
        name="inner",
    )(vectors, pltpu.with_memory_space_constraint(links, pltpu.HBM), own)


def face_kernel(stride, v_hbm, phi_hbm, out, vec_ref, flat, v_ref, phi_ref, sem):
    def fetch(chi, c, k):
        part = (slice(None), slice(None), pl.ds(2 * chi, 2), c)
        return pltpu.make_async_copy(v_hbm.at[part], v_ref.at[part], sem.at[k])

    for k in range(6):
        fetch(k // 3, k % 3, k).start()
    small = pltpu.make_async_copy(phi_hbm, phi_ref, sem.at[6])
    small.start()

    for pair in range(3):
        steps = [(pair * 2 + k) for k in range(2)]
        for k, step in enumerate(steps):
            chi, c = step // 3, step % 3
            fetch(chi, c, step).wait()
            for sb in range(2):
                for ri in range(2):
                    block = v_ref[ri, :, 2 * chi + sb, c].astype(F32)
                    flat[k, sb, ri * 384 : ri * 384 + 384, :] = block.reshape(384, 128)

        def load(k, plane):
            first = plane % 4 * stride
            return flat[k, plane // 4, pl.ds(first, ROWS, stride=16), :].astype(BF16)

        done = exchange([[load(k, plane) for plane in range(8)] for k in range(2)])
        for step, values in zip(steps, done):
            chi, c = step // 3, step % 3
            for a, value in enumerate(values):
                row = (a * 2 + chi) * ROWS
                out[row : row + ROWS, c * 128 : c * 128 + 128] = value

    small.wait()
    vec = jnp.concatenate([phi_ref[...], jnp.zeros((8, 32), F32)], 1)
    vec_ref[...] = vec
    pieces = []
    for _ in range(3):
        piece = vec.astype(BF16)
        vec = vec - piece.astype(F32)
        pieces.append(piece.astype(F32))
    rider = jnp.concatenate(pieces, 1)
    rider = jnp.concatenate([rider, jnp.zeros((8, 384), F32)], 0).astype(BF16)
    out[768:784, :] = rider


def ridden(face):
    return sum(face[768:784, 128 * k : 128 * k + 128].astype(F32)[:8] for k in range(3))


def face_call(stride, name, vectors, phi):
    face = jax.ShapeDtypeStruct((784, 384), BF16)
    vmem = pl.BlockSpec(memory_space=pltpu.VMEM)
    return pl.pallas_call(
        functools.partial(face_kernel, stride),
        out_shape=(face, jax.ShapeDtypeStruct((8, 128), F32)),
        in_specs=[pl.BlockSpec(memory_space=pltpu.HBM)] * 2,
        out_specs=(vmem,) * 2,
        scratch_shapes=[
            pltpu.VMEM((2, 2, 768, 128), F32),
            pltpu.VMEM((2, NV, 4, 3, 16, 128), BF16),
            pltpu.VMEM((8, 2 * ROWS), F32),
            pltpu.SemaphoreType.DMA((7,)),
        ],
        compiler_params=pltpu.CompilerParams(vmem_limit_bytes=12 * 1024 * 1024),
        name=name,
    )(*(pltpu.with_memory_space_constraint(x, pltpu.HBM) for x in (vectors, phi)))


def outer_kernel(mu, face, *refs):
    lefts, (links, vec_ref, out_ref, back_ref, cm) = refs[:-5], refs[-5:]

    for a in range(8):
        for chi in range(2):
            link = [links[a, pl.ds(k, 1), :] for k in range(18)]
            vector = []
            rows = pl.ds((a * 2 + chi) * ROWS, ROWS)
            for d in range(3):
                value = face[rows, d * 128 : (d + 1) * 128].astype(F32)
                vector += [value[:NV], value[NV:]]
            for c, both in enumerate(colour(link, vector)):
                cm[a, chi, :, c * 128 : (c + 1) * 128] = jnp.concatenate(both, 0).astype(BF16)

    eye = eye_mask()
    row_sign, col_sign = signs()
    for a in range(8):
        parts = [[None, None], [None, None]]
        for chi in range(2):
            if mu == 0:
                near, far = lefts[0][a, chi], lefts[0][a, 1 - chi]
            else:
                near, far = lefts[0][0, a, chi], lefts[0][1, a, 1 - chi]
            product = widened(nt(jnp.concatenate([near, far], 0), cm[a, chi]))
            if mu == 0:
                cross = complex_of(product[ROWS:], NV)
            else:
                cross = (1.0 if chi == 0 else -1.0) * complex_i(product[ROWS:], NV)
            parts[chi][chi] = -complex_of(product[:ROWS], NV)
            parts[1 - chi][chi] = cross
        pr, pi = split(vec_ref[pl.ds(a, 1), :])
        column_r = row_sign * column_of(pr, eye)
        column_i = row_sign * column_of(pi, eye)
        block = placed(parts, 0), placed(parts, NV)
        out_ref[a, 0] = block[0]
        out_ref[a, 1] = block[1]
        back_ref[pl.ds(a, 1), :] = backward(block, column_r, column_i, col_sign)


def outer_call(mu, name, *args):
    vmem = pl.BlockSpec(memory_space=pltpu.VMEM)
    shape = jax.ShapeDtypeStruct
    return pl.pallas_call(
        functools.partial(outer_kernel, mu),
        out_shape=(shape((8, 2, ROWS, 128), F32), shape((8, 128), F32)),
        in_specs=[vmem] * len(args),
        out_specs=(vmem,) * 2,
        scratch_shapes=[pltpu.VMEM((8, 2, ROWS, 384), BF16)],
        compiler_params=pltpu.CompilerParams(vmem_limit_bytes=12 * 1024 * 1024),
        name=name,
    )(*args)


def signs():
    rows = lax.broadcasted_iota(jnp.int32, (ROWS, 128), 0)
    return jnp.where(rows < NV, 1.0, -1.0).astype(F32), jnp.where(lane_ids(1) < NV, 1.0, -1.0).astype(F32)


def split(row):
    keep = lane_ids(1) < ROWS
    return jnp.where(keep, row, 0.0), jnp.where(keep, roll(row, -ROWS), 0.0)


def joined(real, imag):
    lanes = lane_ids(1)
    low, high = lanes < ROWS, (lanes >= ROWS) & (lanes < 2 * ROWS)
    return jnp.where(low, real, jnp.where(high, roll(imag, ROWS), 0.0))


def forward(block, row):
    pr, pi = split(row)
    br, bi = block
    return br * pr - bi * pi, br * pi + bi * pr


def column_of(row, eye):
    return jnp.sum(jnp.where(eye, row, 0.0), axis=1, keepdims=True)


def row_of(column, eye):
    return jnp.sum(jnp.where(eye, column, 0.0), axis=0, keepdims=True)


def backward(block, column_r, column_i, col_sign):
    br, bi = block
    real = jnp.sum(br * column_r + bi * column_i, axis=0, keepdims=True)
    imag = jnp.sum(br * column_i - bi * column_r, axis=0, keepdims=True)
    return joined(col_sign * real, col_sign * imag)


def eye_mask():
    rows = lax.broadcasted_iota(jnp.int32, (ROWS, 128), 0)
    return rows == lane_ids(ROWS)


def local_apply(inner, vec, part_ref):
    eye = eye_mask()
    row_sign, col_sign = signs()
    own, kept = [], []
    for a in range(8):
        here, ahead = vec[pl.ds(a, 1), :], vec[pl.ds((a + 1) % 8, 1), :]
        diag, y, x = ((inner[a, k, 0], inner[a, k, 1]) for k in range(3))
        f0, f1, f2 = forward(diag, here), forward(y, here), forward(x, ahead)
        real = jnp.sum(f0[0] + f1[0] + f2[0], axis=1, keepdims=True)
        imag = jnp.sum(f0[1] + f1[1] + f2[1], axis=1, keepdims=True)
        pr, pi = split(here)
        column_r = row_sign * column_of(pr, eye)
        column_i = row_sign * column_of(pi, eye)
        back_y = backward(y, column_r, column_i, col_sign)
        own.append(joined(row_of(real, eye), row_of(imag, eye)) + back_y)
        kept.append(backward(x, column_r, column_i, col_sign))
    for a in range(8):
        part_ref[pl.ds(a, 1), :] = own[a] + kept[(a + 7) % 8]


def ahead_apply(outer_t, outer_z, vt, vz):
    eye = eye_mask()
    rows = []
    for a in range(8):
        ft = forward((outer_t[a, 0], outer_t[a, 1]), vt[a : a + 1])
        fz = forward((outer_z[a, 0], outer_z[a, 1]), vz[a : a + 1])
        real = jnp.sum(ft[0] + fz[0], axis=1, keepdims=True)
        imag = jnp.sum(ft[1] + fz[1], axis=1, keepdims=True)
        rows.append(joined(row_of(real, eye), row_of(imag, eye)))
    return jnp.concatenate(rows, 0)


def first_kernel(inner, outer_t, outer_z, vec, ft, fz, part_ref):
    local_apply(inner, vec, part_ref)
    part_ref[...] += ahead_apply(outer_t, outer_z, ridden(ft), ridden(fz))


def back_kernel(outer_t, outer_z, part, rt, rz, vec_ref, bt_ref, bz_ref):
    vec_ref[...] = part[...] + rt[...] + rz[...]
    eye = eye_mask()
    row_sign, col_sign = signs()
    for a in range(8):
        pr, pi = split(vec_ref[pl.ds(a, 1), :])
        column_r = row_sign * column_of(pr, eye)
        column_i = row_sign * column_of(pi, eye)
        for outer, back in ((outer_t, bt_ref), (outer_z, bz_ref)):
            block = outer[a, 0], outer[a, 1]
            back[pl.ds(a, 1), :] = backward(block, column_r, column_i, col_sign)


def last_kernel(outer_t, outer_z, part, rt, rz, vt, vz, out_ref):
    total = part[...] + rt[...] + rz[...] + ahead_apply(outer_t, outer_z, vt[...], vz[...])
    out_ref[...] = total[:, : 2 * ROWS]


def blocks_kernel(inner, outer_t, outer_z, out_ref):
    sources = (inner.at[:, 0], outer_t, outer_z, inner.at[:, 1], inner.at[:, 2])
    for slot, ref in enumerate(sources):
        for ri in range(2):
            for group in range(ROWS // 8):
                pieces = []
                for row in range(group * 8, group * 8 + 8):
                    pieces.append(jnp.concatenate([ref[a, ri, row : row + 1, :] for a in range(8)], 0))
                wide = lane_rows(pieces)
                first = ri * ROWS * ROWS + group * 8 * ROWS
                out_ref[slot, :, first : first + 8 * ROWS] = wide


def lane_rows(pieces):
    tiles = []
    for tile in range(3):
        total = None
        for k, piece in enumerate(pieces):
            shift = k * ROWS - tile * 128
            if -ROWS < shift < 128:
                moved = piece if shift == 0 else roll(piece, shift)
                if shift < 0:
                    moved = jnp.where(lane_ids(8) < ROWS + shift, moved, 0.0)
                elif shift + ROWS > 128:
                    moved = jnp.where(lane_ids(8) >= shift, moved, 0.0)
                total = moved if total is None else total + moved
        tiles.append(total)
    return jnp.concatenate(tiles, 1)


def small_call(kernel, count, name, *args, width=128):
    vmem = pl.BlockSpec(memory_space=pltpu.VMEM)
    row = jax.ShapeDtypeStruct((8, width), F32)
    return pl.pallas_call(
        kernel,
        out_shape=(row,) * count,
        in_specs=[vmem] * len(args),
        out_specs=(vmem,) * count,
        compiler_params=pltpu.CompilerParams(vmem_limit_bytes=12 * 1024 * 1024),
        name=name,
    )(*args)


def blocks_call(inner, outer_t, outer_z):
    vmem = pl.BlockSpec(memory_space=pltpu.VMEM)
    return pl.pallas_call(
        blocks_kernel,
        out_shape=jax.ShapeDtypeStruct((5, 8, 2 * ROWS * ROWS), F32),
        in_specs=[vmem] * 3,
        out_specs=vmem,
        compiler_params=pltpu.CompilerParams(vmem_limit_bytes=12 * 1024 * 1024),
        cost_estimate=pl.CostEstimate(flops=0, bytes_accessed=6_000_000, transcendentals=0),
        name="blocks",
    )(inner, outer_t, outer_z)


def shifted(value, axis, steps):
    count = lax.axis_size(axis)
    return lax.ppermute(value, axis, [(k, (k + steps) % count) for k in range(count)])


def per_device(null_vectors, gauge_links, coarse_in):
    vectors = null_vectors.reshape(2, NV, 4, 3, 16, 128)
    links = gauge_links.reshape(2, 4, 3, 3, 16, 128)
    phi = coarse_in.reshape(8, 2 * ROWS)
    face_z, vec = face_call(4, "face_z", vectors, phi)
    own_t, _ = face_call(1, "face_t", vectors, phi)
    face_z = shifted(face_z, "sa", -1)
    face_t = shifted(own_t, "ta", -1)
    inner, left_t, left_z, link_t, link_z = inner_call(vectors, links, own_t)
    outer_t, bt = outer_call(0, "outer_t", face_t, left_t, link_t, vec)
    outer_z, bz = outer_call(1, "outer_z", face_z, left_z, link_z, vec)
    rt, rz = shifted(bt, "ta", 1), shifted(bz, "sa", 1)
    (part,) = small_call(first_kernel, 1, "first", inner, outer_t, outer_z, vec, face_t, face_z)
    once, bt, bz = small_call(back_kernel, 3, "back", outer_t, outer_z, part, rt, rz)
    vec_t, rt = shifted(once, "ta", -1), shifted(bt, "ta", 1)
    vec_z, rz = shifted(once, "sa", -1), shifted(bz, "sa", 1)
    (part,) = small_call(local_apply, 1, "local", inner, once)
    blocks = blocks_call(inner, outer_t, outer_z)
    (twice,) = small_call(last_kernel, 1, "last", outer_t, outer_z, part, rt, rz, vec_t, vec_z, width=2 * ROWS)
    blocks = jnp.swapaxes(blocks, 0, 1)
    return blocks.reshape(1, 1, 8, 5, 2 * ROWS * ROWS), twice.reshape(1, 1, 8, 2 * ROWS)


def solution(mesh):
    placed_sites = P(None, None, None, None, "ta", "sa", None)
    return jax.shard_map(
        per_device,
        mesh=mesh,
        in_specs=(placed_sites, placed_sites, P("ta", "sa", None, None)),
        out_specs=(P("ta", "sa", None, None, None), P("ta", "sa", None, None)),
        check_vma=False,
    )
```
